32 devices in a mesh: wide: 8 (over y, x, core), narrow: 4 (over z).
Axes of the slice: x: 2, y: 2, z: 4, core: 2. Of those that a mesh axis runs over, the one named last changes fastest.
Arguments:
- tokens: bfloat16 [10240, 2048], P(('wide', 'narrow')), may hold values from -6 to 6
- lengths: int32 [32], P(('wide', 'narrow')), may hold values from 80 to 320, as said below
- cotangent: bfloat16 [10240, 2048], P(('wide', 'narrow')), may hold values from -6 to 6
- norm_gain1: bfloat16 [2048], P(('wide', 'narrow')), may hold values from 0.5 to 1.5
- gate_in: bfloat16 [2048, 2560], P(('wide', 'narrow')), may hold values from -0.125 to 0.125
- x_in: bfloat16 [2048, 2560], P(('wide', 'narrow')), may hold values from -0.125 to 0.125
- conv_kernel: bfloat16 [4, 2560], P(None, ('wide', 'narrow')), may hold values from -3 to 3
- conv_bias: bfloat16 [2560], P(('wide', 'narrow')), may hold values from -3 to 3
- rate_weight: bfloat16 [160, 2560], P(None, ('wide', 'narrow')), may hold values from -0.5 to 0.5
- rate_bias: bfloat16 [2560], P(('wide', 'narrow')), may hold values from -3 to 3
- input_weight: bfloat16 [160, 2560], P(None, ('wide', 'narrow')), may hold values from -0.5 to 0.5
- input_bias: bfloat16 [2560], P(('wide', 'narrow')), may hold values from -3 to 3
- decay_param: bfloat16 [2560], P(('wide', 'narrow')), may hold values from 4.5 to 9.5
- out_proj: bfloat16 [2560, 2048], P(('wide', 'narrow')), may hold values from -0.3125 to 0.3125
- norm_gain2: bfloat16 [2048], P(('wide', 'narrow')), may hold values from 0.5 to 1.5
- mlp_gate: bfloat16 [2048, 6144], P(('wide', 'narrow')), may hold values from -0.125 to 0.125
- mlp_up: bfloat16 [2048, 6144], P(('wide', 'narrow')), may hold values from -0.125 to 0.125
- mlp_down: bfloat16 [6144, 2048], P(('wide', 'narrow')), may hold values from -0.109375 to 0.109375
Outputs:
- block_out: bfloat16 [10240, 2048], P(('wide', 'narrow'))
- input_grad: float32 [10240, 2048], P(('wide', 'narrow'))
- grad_norm_gain1: float32 [2048], P(('wide', 'narrow'))
- grad_gate_in: float32 [2048, 2560], P(('wide', 'narrow'))
- grad_x_in: float32 [2048, 2560], P(('wide', 'narrow'))
- grad_conv_kernel: float32 [4, 2560], P(None, ('wide', 'narrow'))
- grad_conv_bias: float32 [2560], P(('wide', 'narrow'))
- grad_rate_weight: float32 [160, 2560], P(None, ('wide', 'narrow'))
- grad_rate_bias: float32 [2560], P(('wide', 'narrow'))
- grad_input_weight: float32 [160, 2560], P(None, ('wide', 'narrow'))
- grad_input_bias: float32 [2560], P(('wide', 'narrow'))
- grad_decay_param: float32 [2560], P(('wide', 'narrow'))
- grad_out_proj: float32 [2560, 2048], P(('wide', 'narrow'))
- grad_norm_gain2: float32 [2048], P(('wide', 'narrow'))
- grad_mlp_gate: float32 [2048, 6144], P(('wide', 'narrow'))
- grad_mlp_up: float32 [2048, 6144], P(('wide', 'narrow'))
- grad_mlp_down: float32 [6144, 2048], P(('wide', 'narrow'))
The draws below stay inside these ranges and needn't reach their ends.
Inputs may be any that keep to these rules, and one draw needn't show every extreme that they name: Sequence s has lengths[s] real tokens at the start of its 320 slots, the rest is padding; some sequence fills all its slots.
All inputs are finite; a program needn't handle non-finite values.
Results may differ from the reference program's by a relative error of at most 0.014.
Values may be sent and summed in bfloat16 or wider, within the bound.
A program may use at most 448 MiB of HBM per device.

```python
import jax
import jax.numpy as jnp
from jax import lax

D = 2048
R = 2560
FF = 6144
HD = 160
CONV = 4
SEQ_LEN = 320
MIN_LEN = 80
SEQS = 32
TOKENS = 10240


def draw_lengths(key, part):
    key = jax.random.fold_in(key, 7)
    first_key, second_key = jax.random.split(key)
    picks = jax.random.randint(first_key, (SEQS,), 0, 64)
    spans = MIN_LEN + (SEQ_LEN - MIN_LEN) * picks * picks // 3969
    longest = jax.random.randint(second_key, (), 0, SEQS)
    places = jnp.arange(SEQS, dtype=jnp.int32)
    return jnp.where(places == longest, SEQ_LEN, spans).astype(jnp.int32)


def shard_levels(rng, extent, cuts, least, top_value):
    def one(axis_at, blocks):
        steps = jax.random.uniform(jax.random.fold_in(jax.random.fold_in(rng, 6), axis_at), (blocks,), jnp.float32, least / len(cuts), top_value / len(cuts))
        return jnp.repeat(jnp.exp(steps), extent[axis_at] // blocks).reshape((-1,) + (1,) * (len(extent) - axis_at - 1))

    level = one(*cuts[0])
    for cut in cuts[1:]:
        level = level * one(*cut)
    return level


def normal_values(stream_key, shape, spread, reach, cuts=(), kind=jnp.bfloat16):
    values = jax.random.normal(stream_key, shape, jnp.float32) * spread
    if len(cuts) > 0:
        values = shard_levels(stream_key, shape, cuts, -0.22, 0.18) * values
    return jnp.clip(values, min=-reach, max=reach).astype(kind)


def setup_inputs(seed: int = 0) -> dict:
    arg_keys = jax.random.split(jax.random.key(seed), 19)
    return {
        "tokens": normal_values(arg_keys[0], (TOKENS, D), 1.0, 6.0, ((0, 32),)),
        "lengths": draw_lengths(jax.random.fold_in(arg_keys[18], 71), 0),
        "cotangent": normal_values(arg_keys[2], (TOKENS, D), 1.0, 6.0, ((0, 32),)),
        "norm_gain1": jnp.clip(1.0 + 0.1 * jax.random.normal(arg_keys[3], (D,), jnp.float32), 0.5, 1.5).astype(jnp.bfloat16),
        "gate_in": normal_values(arg_keys[4], (D, R), D ** -0.5, 0.125, ((0, 32),)),
        "x_in": normal_values(arg_keys[5], (D, R), D ** -0.5, 0.125, ((0, 32),)),
        "conv_kernel": normal_values(arg_keys[6], (CONV, R), CONV ** -0.5, 3.0, ((1, 32),)),
        "conv_bias": normal_values(arg_keys[7], (R,), 0.5, 3.0, ((0, 32),)),
        "rate_weight": normal_values(arg_keys[8], (HD, R), HD ** -0.5, 0.5, ((1, 32),)),
        "rate_bias": normal_values(arg_keys[9], (R,), 0.5, 3.0, ((0, 32),)),
        "input_weight": normal_values(arg_keys[10], (HD, R), HD ** -0.5, 0.5, ((1, 32),)),
        "input_bias": normal_values(arg_keys[11], (R,), 0.5, 3.0, ((0, 32),)),
        "decay_param": jnp.clip(4.5 + 5.0 * jax.random.uniform(arg_keys[12], (R,), jnp.float32) ** shard_levels(arg_keys[12], (R,), ((0, 32),), -0.2, 0.2), 4.5, 9.5).astype(jnp.bfloat16),
        "out_proj": normal_values(arg_keys[13], (R, D), (R // 8) ** -0.5, 0.3125, ((0, 32),)),
        "norm_gain2": jnp.clip(1.0 + 0.1 * jax.random.normal(arg_keys[14], (D,), jnp.float32), 0.5, 1.5).astype(jnp.bfloat16),
        "mlp_gate": normal_values(arg_keys[15], (D, FF), D ** -0.5, 0.125, ((0, 32),)),
        "mlp_up": normal_values(arg_keys[16], (D, FF), D ** -0.5, 0.125, ((0, 32),)),
        "mlp_down": normal_values(arg_keys[17], (FF, D), (FF // 2) ** -0.5, 0.109375, ((0, 32),)),
    }


EPSILON = 1e-06
RATE_SCALE = 8.0

@jax.custom_vjp
def low(v):
    return lax.optimization_barrier(v.astype(jnp.bfloat16)).astype(jnp.float32)

@jax.custom_vjp
def low_back(v):
    return v

def low_keep(v):
    return (low(v), None)

def low_pass(kept, grad):
    return (grad,)

def back_keep(v):
    return (v, None)

def back_low(kept, grad):
    return (low(grad),)
low.defvjp(low_keep, low_pass)
low_back.defvjp(back_keep, back_low)

def matmul_high(left, right):
    return jnp.dot(left, right, precision=lax.Precision.HIGHEST)

def rms_scale(values, gain):
    inverse = lax.rsqrt(lax.optimization_barrier(jnp.mean(values * values, axis=-1, keepdims=True)) + EPSILON)
    return values * inverse * gain

def gelu_tanh(values):
    return jax.nn.gelu(values, approximate=True)

def conv_causal(inputs, kernel, conv_shift):
    width = kernel.shape[0]
    padded = jnp.pad(inputs, ((width - 1, 0), (0, 0)))
    totals = conv_shift + jnp.zeros_like(inputs)
    for offset in range(width):
        totals = totals + kernel[offset] * padded[offset:offset + inputs.shape[0]]
    return totals

def combine_steps(earlier, later):
    return (earlier[0] * later[0], later[0] * earlier[1] + later[1])

def lru_mix(conv_vals, rate_pre, input_pre, gate_pre, decay_vals):
    rate_gate = jax.nn.sigmoid(rate_pre)
    input_gate = jax.nn.sigmoid(input_pre)
    log_decay = -RATE_SCALE * rate_gate * jax.nn.softplus(-decay_vals)
    decay_now = jnp.exp(log_decay)
    scale_in = jnp.sqrt(-jnp.expm1(2.0 * log_decay))
    driven = scale_in * input_gate * conv_vals
    states = lax.associative_scan(combine_steps, (decay_now, driven), axis=0)[1]
    return states * gelu_tanh(gate_pre)

def block_mix(values, weight):
    head_size = weight.shape[0]
    row_count = values.shape[0]
    by_heads = values.reshape(row_count, -1, head_size)
    head_table = weight.reshape(head_size, -1, head_size)
    mixed_heads = jnp.einsum('thi,ihj->thj', by_heads, head_table, precision=lax.Precision.HIGHEST)
    return mixed_heads.reshape(row_count, -1)

def forward(inputs, live_mask, params):
    gain_one, w_gate, w_branch, kernel, conv_shift, w_rate, b_rate, w_input, b_input, decay_vals, w_out, gain_two, w_mgate, w_mup, w_down = params
    normed1 = low(rms_scale(inputs, gain_one))
    gate_pre = low_back(matmul_high(normed1, w_gate))
    branch_pre = low_back(matmul_high(normed1, w_branch))
    conv_vals = low(conv_causal(branch_pre, kernel, conv_shift))
    rate_pre = low_back(block_mix(conv_vals, w_rate)) + b_rate
    input_pre = low_back(block_mix(conv_vals, w_input)) + b_input
    mixed = low(lru_mix(conv_vals, rate_pre, input_pre, gate_pre, decay_vals))
    merged = inputs + low_back(matmul_high(mixed, w_out))
    normed2 = low(rms_scale(merged, gain_two))
    gate_two = low_back(matmul_high(normed2, w_mgate))
    up_two = low_back(matmul_high(normed2, w_mup))
    product = low(gelu_tanh(gate_two) * up_two)
    result = merged + low_back(matmul_high(product, w_down))
    return result * live_mask

def reference(tokens, lengths, cotangent, norm_gain1, gate_in, x_in, conv_kernel, conv_bias, rate_weight, rate_bias, input_weight, input_bias, decay_param, out_proj, norm_gain2, mlp_gate, mlp_up, mlp_down):
    params = tuple((member.astype(jnp.float32) for member in (norm_gain1, gate_in, x_in, conv_kernel, conv_bias, rate_weight, rate_bias, input_weight, input_bias, decay_param, out_proj, norm_gain2, mlp_gate, mlp_up, mlp_down)))
    seq_count = lengths.shape[0]
    row_count = tokens.shape[0] // seq_count
    seq_tokens = tokens.reshape(seq_count, row_count, -1)
    seq_cots = cotangent.reshape(seq_count, row_count, -1)

    def per_sequence(totals, item):
        seq_in, seq_cot, seq_len = item
        live_mask = (jnp.arange(row_count, dtype=jnp.int32) < seq_len).astype(jnp.float32)[:, None]

        def apply_block(inputs, weights):
            return forward(inputs, live_mask, weights)
        result, pullback = jax.vjp(apply_block, seq_in.astype(jnp.float32), params)
        grad_in, grad_params = pullback(seq_cot.astype(jnp.float32))
        totals = jax.tree.map(jnp.add, totals, grad_params)
        return (totals, (result.astype(jnp.bfloat16), grad_in))
    zeros = jax.tree.map(jnp.zeros_like, params)
    totals, (outputs, grads_in) = lax.scan(per_sequence, zeros, (seq_tokens, seq_cots, lengths))
    block_out = outputs.reshape(tokens.shape)
    input_grad = grads_in.reshape(tokens.shape)
    return (block_out, input_grad, totals[0], totals[1], totals[2], totals[3], totals[4], totals[5], totals[6], totals[7], totals[8], totals[9], totals[10], totals[11], totals[12], totals[13], totals[14])
```

```python
import functools
import math

import jax
import jax.numpy as jnp
from jax import lax
from jax.experimental import pallas as pl
from jax.experimental.pallas import tpu as pltpu
from jax.sharding import Mesh
from jax.sharding import PartitionSpec as P

EPSILON = 1e-06
RATE_SCALE = 8.0
GELU_ROOT = 0.7978845608028654
GELU_CUBE = 0.044715
LANES = 128
HEADS = 16


def matmul_low(left, right):
    return jnp.dot(left, right, preferred_element_type=jnp.float32)


def matmul_nt(left, right):
    return lax.dot_general(left, right, (((1,), (1,)), ((), ())), preferred_element_type=jnp.float32)


def matmul_tn(left, right):
    return lax.dot_general(left, right, (((0,), (0,)), ((), ())), preferred_element_type=jnp.float32)


def rms_inverse(values):
    return lax.rsqrt(jnp.mean(values * values, axis=-1, keepdims=True) + EPSILON)


def rms_back(values, inverse, gain, grads):
    scaled = grads * gain
    dots = jnp.mean(scaled * values, axis=-1, keepdims=True)
    return inverse * scaled - values * (inverse * inverse * inverse * dots)


def gelu_pair(values):
    square = values * values
    slope = jnp.tanh(GELU_ROOT * values * (1.0 + GELU_CUBE * square))
    half = 0.5 * (1.0 + slope)
    grad = half + 0.5 * values * (1.0 - slope * slope) * (GELU_ROOT * (1.0 + 3.0 * GELU_CUBE * square))
    return values * half, grad


def minus_expm1(values):
    series = 1.0 + values * (1.0 / 6.0) * (1.0 + values * (1.0 / 7.0))
    for order in (5.0, 4.0, 3.0, 2.0):
        series = 1.0 + values * (1.0 / order) * series
    return jnp.where(values > -0.25, -values * series, 1.0 - jnp.exp(values))


def softplus_minus(values):
    return jnp.maximum(-values, 0.0) + jnp.log(1.0 + jnp.exp(-jnp.abs(values)))


def lru_terms(conv, rate_pre, input_pre, soft):
    rate_gate = 1.0 / (1.0 + jnp.exp(-rate_pre))
    input_gate = 1.0 / (1.0 + jnp.exp(-input_pre))
    log_decay = -RATE_SCALE * rate_gate * soft
    decay_now = jnp.exp(log_decay)
    scale_in = jnp.sqrt(minus_expm1(2.0 * log_decay))
    return rate_gate, input_gate, decay_now, scale_in


CHUNK = 64
UNROLL = 8


def lru_forward_kernel(seqs, conv_ref, rate_ref, input_ref, gate_ref, soft_ref, states_ref, mixed_ref, decay_s, drive_s):
    rows = conv_ref.shape[0]
    length = rows // seqs
    soft = soft_ref[0:1, :]

    def prepare(i, carry):
        at = pl.ds(pl.multiple_of(i * CHUNK, CHUNK), CHUNK)
        conv = conv_ref[at, :].astype(jnp.float32)
        _, input_gate, decay_now, scale_in = lru_terms(conv, rate_ref[at, :], input_ref[at, :], soft)
        decay_s[at, :] = decay_now
        drive_s[at, :] = scale_in * input_gate * conv
        return carry

    lax.fori_loop(0, rows // CHUNK, prepare, 0)

    def advance(i, state):
        for j in range(UNROLL):
            at = pl.ds(i * UNROLL + j, seqs, stride=length)
            state = decay_s[at, :] * state + drive_s[at, :]
            states_ref[at, :] = state
        return state

    lax.fori_loop(0, length // UNROLL, advance, jnp.zeros((seqs, LANES), jnp.float32))

    def finish(i, carry):
        at = pl.ds(pl.multiple_of(i * CHUNK, CHUNK), CHUNK)
        value, _ = gelu_pair(gate_ref[at, :])
        mixed_ref[at, :] = (states_ref[at, :] * value).astype(jnp.bfloat16)
        return carry

    lax.fori_loop(0, rows // CHUNK, finish, 0)


def lru_backward_kernel(
    seqs,
    conv_ref,
    rate_ref,
    input_ref,
    gate_ref,
    soft_ref,
    states_ref,
    grad_ref,
    d_conv_ref,
    d_rate_ref,
    d_input_ref,
    d_gate_ref,
    sums_ref,
    decay_s,
    flow_s,
    before_s,
):
    rows = conv_ref.shape[0]
    length = rows // seqs
    soft = soft_ref[0:1, :]

    def prepare(i, carry):
        at = pl.ds(pl.multiple_of(i * CHUNK, CHUNK), CHUNK)
        value, slope = gelu_pair(gate_ref[at, :])
        grad = grad_ref[at, :]
        d_gate_ref[at, :] = (grad * states_ref[at, :] * slope).astype(jnp.bfloat16)
        flow_s[at, :] = grad * value
        rate_gate = 1.0 / (1.0 + jnp.exp(-rate_ref[at, :]))
        decay_s[at, :] = jnp.exp(-RATE_SCALE * rate_gate * soft)
        return carry

    lax.fori_loop(0, rows // CHUNK, prepare, 0)

    def retreat(i, carry):
        flow, decay = carry
        for j in range(UNROLL):
            step = length - 1 - (i * UNROLL + j)
            at = pl.ds(step, seqs, stride=length)
            flow = flow_s[at, :] + decay * flow
            flow_s[at, :] = flow
            decay = decay_s[at, :]
        return flow, decay

    nothing = jnp.zeros((seqs, LANES), jnp.float32)
    lax.fori_loop(0, length // UNROLL, retreat, (nothing, nothing))

    def shift(i, last):
        for j in range(UNROLL):
            at = pl.ds(i * UNROLL + j, seqs, stride=length)
            before_s[at, :] = last
            last = states_ref[at, :]
        return last

    lax.fori_loop(0, length // UNROLL, shift, nothing)

    def finish(i, carry):
        rate_sum, input_sum, soft_sum = carry
        at = pl.ds(pl.multiple_of(i * CHUNK, CHUNK), CHUNK)
        conv = conv_ref[at, :].astype(jnp.float32)
        rate_gate, input_gate, decay_now, scale_in = lru_terms(conv, rate_ref[at, :], input_ref[at, :], soft)
        flow = flow_s[at, :]
        d_scale = flow * input_gate * conv
        d_log = decay_now * (flow * before_s[at, :] - d_scale * decay_now / scale_in)
        d_input = flow * scale_in * conv * input_gate * (1.0 - input_gate)
        d_rate = d_log * (-RATE_SCALE) * soft * rate_gate * (1.0 - rate_gate)
        d_conv_ref[at, :] = flow * scale_in * input_gate
        d_rate_ref[at, :] = d_rate.astype(jnp.bfloat16)
        d_input_ref[at, :] = d_input.astype(jnp.bfloat16)

        def fold(total, part):
            for k in range(CHUNK // 8):
                total = total + part[k * 8 : (k + 1) * 8, :]
            return total

        return (fold(rate_sum, d_rate), fold(input_sum, d_input), fold(soft_sum, d_log * (-RATE_SCALE) * rate_gate))

    blank = jnp.zeros((8, LANES), jnp.float32)
    rate_sum, input_sum, soft_sum = lax.fori_loop(0, rows // CHUNK, finish, (blank, blank, blank))
    sums_ref[0:8, :] = rate_sum
    sums_ref[8:16, :] = input_sum
    sums_ref[16:24, :] = soft_sum


def lru_forward(seqs, conv, rate_pre, input_pre, gate_pre, soft):
    rows, channels = conv.shape
    block = pl.BlockSpec((rows, LANES), lambda i: (0, i))
    return pl.pallas_call(
        functools.partial(lru_forward_kernel, seqs),
        grid=(pl.cdiv(channels, LANES),),
        out_shape=(
            jax.ShapeDtypeStruct((rows, channels), jnp.float32),
            jax.ShapeDtypeStruct((rows, channels), jnp.bfloat16),
        ),
        in_specs=[block, block, block, block, pl.BlockSpec((8, LANES), lambda i: (0, i))],
        out_specs=(block, block),
        scratch_shapes=[pltpu.VMEM((rows, LANES), jnp.float32)] * 2,
        compiler_params=pltpu.CompilerParams(vmem_limit_bytes=48 * 2**20),
        name="lru_forward",
    )(conv, rate_pre, input_pre, gate_pre, soft)


def lru_backward(seqs, conv, rate_pre, input_pre, gate_pre, soft, states, grads):
    rows, channels = conv.shape
    block = pl.BlockSpec((rows, LANES), lambda i: (0, i))
    return pl.pallas_call(
        functools.partial(lru_backward_kernel, seqs),
        grid=(pl.cdiv(channels, LANES),),
        out_shape=(
            jax.ShapeDtypeStruct((rows, channels), jnp.float32),
            jax.ShapeDtypeStruct((rows, channels), jnp.bfloat16),
            jax.ShapeDtypeStruct((rows, channels), jnp.bfloat16),
            jax.ShapeDtypeStruct((rows, channels), jnp.bfloat16),
            jax.ShapeDtypeStruct((24, channels), jnp.float32),
        ),
        in_specs=[block, block, block, block, pl.BlockSpec((8, LANES), lambda i: (0, i)), block, block],
        out_specs=(block, block, block, block, pl.BlockSpec((24, LANES), lambda i: (0, i))),
        scratch_shapes=[pltpu.VMEM((rows, LANES), jnp.float32)] * 3,
        compiler_params=pltpu.CompilerParams(vmem_limit_bytes=48 * 2**20),
        name="lru_backward",
    )(conv, rate_pre, input_pre, gate_pre, soft, states, grads)


def block_diagonal(table):
    size, channels = table.shape
    tall = jnp.concatenate([table] * (channels // size), axis=0)
    row_head = lax.broadcasted_iota(jnp.int32, tall.shape, 0) // size
    column_head = lax.broadcasted_iota(jnp.int32, tall.shape, 1) // size
    return jnp.where(row_head == column_head, tall, jnp.zeros_like(tall))


def diagonal_blocks(square, size):
    channels = square.shape[0]
    cube = square.reshape(channels // size, size, channels)
    row_head = lax.broadcasted_iota(jnp.int32, cube.shape, 0)
    column_head = lax.broadcasted_iota(jnp.int32, cube.shape, 2) // size
    return jnp.sum(jnp.where(row_head == column_head, cube, jnp.zeros_like(cube)), axis=0)


def shift_rows(values, seqs, by):
    rows, channels = values.shape
    length = rows // seqs
    cube = values.reshape(seqs, length, channels)
    if by > 0:
        cube = jnp.pad(cube, ((0, 0), (by, 0), (0, 0)))[:, :length]
    elif by < 0:
        cube = jnp.pad(cube, ((0, 0), (0, -by), (0, 0)))[:, -by:]
    return cube.reshape(rows, channels)


def make_block(tp, dp, tp_size, dp_size):
    every = (tp,) + dp

    def gather_rows(values):
        return lax.all_gather(values, tp, axis=0, tiled=True)

    def scatter_rows(values):
        return lax.psum_scatter(values, tp, scatter_dimension=0, tiled=True)

    def columns_out(shard):
        rows, columns = shard.shape
        cut = shard.reshape(rows, tp_size, columns // tp_size)
        return lax.all_to_all(cut, tp, 1, 0, tiled=False)

    def gather_weight(part):
        whole = lax.all_gather(part.reshape(-1, part.shape[-1]), dp, axis=0, tiled=True)
        whole = whole.reshape((dp_size,) + part.shape)
        return whole.swapaxes(0, 1).reshape(-1, part.shape[-1])

    def scatter_weight(grad, rows):
        columns = grad.shape[-1]
        cut = grad.reshape(tp_size, dp_size, rows, columns).swapaxes(0, 1).reshape(-1, columns)
        mine = lax.psum_scatter(cut, dp, scatter_dimension=0, tiled=True)
        return lax.all_to_all(mine.reshape(tp_size, rows, columns), tp, 0, 1, tiled=False)

    def on_device(
        tokens,
        lengths,
        cotangent,
        norm_gain1,
        gate_in,
        x_in,
        conv_kernel,
        conv_bias,
        rate_weight,
        rate_bias,
        input_weight,
        input_bias,
        decay_param,
        out_proj,
        norm_gain2,
        mlp_gate,
        mlp_up,
        mlp_down,
    ):
        bf16, f32 = jnp.bfloat16, jnp.float32
        row_count, width = tokens.shape
        head = rate_weight.shape[0]
        shard_rows = gate_in.shape[0]
        taps = conv_kernel.shape[0]
        seqs = tp_size
        live = (jnp.arange(row_count, dtype=jnp.int32) < lengths[0]).astype(f32)[:, None]

        low_res = (cotangent.astype(f32) * live).astype(bf16)
        tokens_all = gather_rows(tokens)
        low_res_all = gather_rows(low_res)

        gains = lax.all_gather(jnp.stack([norm_gain1, norm_gain2]), every, axis=1, tiled=True).astype(f32)
        gain_one, gain_two = gains[0:1], gains[1:2]

        w_gate = gather_weight(columns_out(gate_in))
        w_branch = gather_weight(columns_out(x_in))
        table = jnp.concatenate(
            [
                conv_kernel,
                conv_bias[None],
                rate_weight,
                rate_bias[None],
                input_weight,
                input_bias[None],
                decay_param[None],
            ],
            axis=0,
        )
        table = lax.all_gather(table.T, dp, axis=0, tiled=True).T
        w_out = lax.all_gather(out_proj, dp, axis=0, tiled=True)
        w_mgate = gather_weight(columns_out(mlp_gate))
        w_mup = gather_weight(columns_out(mlp_up))
        w_down = lax.all_gather(mlp_down, dp, axis=0, tiled=True)

        cuts = [taps, 1, head, 1, head, 1, 1]
        places = [sum(cuts[:i]) for i in range(len(cuts) + 1)]
        kernel, shift, rate_table, b_rate, input_table, b_input, decay = (
            table[places[i] : places[i + 1]] for i in range(len(cuts))
        )
        kernel_f, shift_f, b_rate, b_input, decay_f = (v.astype(f32) for v in (kernel, shift, b_rate, b_input, decay))
        w_rate = block_diagonal(rate_table)
        w_input = block_diagonal(input_table)
        soft = softplus_minus(decay_f)
        soft_rows = jnp.broadcast_to(soft, (8, soft.shape[1]))

        tokens_f = tokens_all.astype(f32)
        normed1 = (tokens_f * rms_inverse(tokens_f) * gain_one).astype(bf16)
        gate_pre = matmul_low(normed1, w_gate)
        branch_pre = matmul_low(normed1, w_branch)
        conv = shift_f
        for tap in range(taps):
            conv = conv + kernel_f[tap] * shift_rows(branch_pre, seqs, taps - 1 - tap)
        conv = conv.astype(bf16)
        rate_pre = matmul_low(conv, w_rate) + b_rate
        input_pre = matmul_low(conv, w_input) + b_input
        states, mixed = lru_forward(seqs, conv, rate_pre, input_pre, gate_pre, soft_rows)
        merged = tokens.astype(f32) + scatter_rows(matmul_low(mixed, w_out).astype(bf16)).astype(f32)

        inverse2 = rms_inverse(merged)
        normed2 = (merged * inverse2 * gain_two).astype(bf16)
        normed2_all = gather_rows(normed2)
        gate_two = matmul_low(normed2_all, w_mgate)
        up_two = matmul_low(normed2_all, w_mup)
        value, slope = gelu_pair(gate_two)
        product = (value * up_two).astype(bf16)
        result = merged + scatter_rows(matmul_low(product, w_down).astype(bf16)).astype(f32)
        block_out = (result * live).astype(bf16)

        grad_down = matmul_tn(product, low_res_all).astype(bf16)
        down_out = lax.psum_scatter(grad_down, dp, scatter_dimension=0, tiled=True).astype(f32)
        d_product = matmul_nt(low_res_all, w_down)
        d_gate_two = (d_product * up_two * slope).astype(bf16)
        d_up_two = (d_product * value).astype(bf16)
        mgate_out = scatter_weight(matmul_tn(normed2_all, d_gate_two).astype(bf16), shard_rows)
        mup_out = scatter_weight(matmul_tn(normed2_all, d_up_two).astype(bf16), shard_rows)
        d_normed2 = scatter_rows((matmul_nt(d_gate_two, w_mgate) + matmul_nt(d_up_two, w_mup)).astype(bf16)).astype(f32)
        grad_gain2 = jnp.sum(d_normed2 * merged * inverse2, axis=0)
        d_merged = low_res.astype(f32) + rms_back(merged, inverse2, gain_two, d_normed2)

        low_merged_all = gather_rows(d_merged.astype(bf16))
        grad_out = matmul_tn(mixed, low_merged_all).astype(bf16)
        out_out = lax.psum_scatter(grad_out, dp, scatter_dimension=0, tiled=True).astype(f32)
        d_mixed = matmul_nt(low_merged_all, w_out)
        d_conv_lru, d_rate, d_input, d_gate, sums = lru_backward(
            seqs, conv, rate_pre, input_pre, gate_pre, soft_rows, states, d_mixed
        )
        sums = sums.reshape(3, 8, -1).sum(axis=1)
        grad_decay = sums[2] * (-1.0 / (1.0 + jnp.exp(decay_f[0])))
        d_conv = d_conv_lru + matmul_nt(d_rate, w_rate) + matmul_nt(d_input, w_input)
        grad_rate_weight = diagonal_blocks(matmul_tn(conv, d_rate), head)
        grad_input_weight = diagonal_blocks(matmul_tn(conv, d_input), head)
        d_branch = jnp.zeros_like(d_conv)
        grad_taps = []
        for tap in range(taps):
            moved = shift_rows(d_conv, seqs, tap - (taps - 1))
            d_branch = d_branch + kernel_f[tap] * moved
            grad_taps.append(jnp.sum(branch_pre * moved, axis=0))
        d_branch = d_branch.astype(bf16)
        gate_out = scatter_weight(matmul_tn(normed1, d_gate).astype(bf16), shard_rows)
        branch_out = scatter_weight(matmul_tn(normed1, d_branch).astype(bf16), shard_rows)
        d_normed1 = scatter_rows((matmul_nt(d_gate, w_gate) + matmul_nt(d_branch, w_branch)).astype(bf16)).astype(f32)
        own = tokens.astype(f32)
        inverse1 = rms_inverse(own)
        grad_gain1 = jnp.sum(d_normed1 * own * inverse1, axis=0)
        input_grad = d_merged + rms_back(own, inverse1, gain_one, d_normed1)

        table_grad = jnp.concatenate(
            [
                jnp.stack(grad_taps),
                jnp.sum(d_conv, axis=0)[None],
                grad_rate_weight,
                sums[0:1],
                grad_input_weight,
                sums[1:2],
                grad_decay[None],
            ],
            axis=0,
        )
        table_out = lax.psum_scatter(table_grad.T, dp, scatter_dimension=0, tiled=True).T
        kernel_out, shift_out, rate_out, rate_bias_out, input_out, input_bias_out, decay_out = (
            table_out[places[i] : places[i + 1]] for i in range(len(cuts))
        )
        gain_out = lax.psum_scatter(jnp.stack([grad_gain1, grad_gain2]), every, scatter_dimension=1, tiled=True)

        def flat(values):
            return values.reshape(shard_rows, -1).astype(f32)

        return (
            block_out,
            input_grad,
            gain_out[0],
            flat(gate_out),
            flat(branch_out),
            kernel_out,
            shift_out[0],
            rate_out,
            rate_bias_out[0],
            input_out,
            input_bias_out[0],
            decay_out[0],
            out_out,
            gain_out[1],
            flat(mgate_out),
            flat(mup_out),
            down_out,
        )

    return on_device


def split_mesh(mesh):
    wide, narrow = mesh.shape["wide"], mesh.shape["narrow"]
    group = math.gcd(wide, HEADS)
    if group == wide:
        return mesh, ("narrow",), group, narrow
    places = mesh.devices.reshape(group, wide // group, narrow)
    return Mesh(places, ("wide", "rest", "narrow")), ("rest", "narrow"), group, wide // group * narrow


def solution(mesh):
    mesh, dp, tp_size, dp_size = split_mesh(mesh)
    every = ("wide",) + dp
    rows, columns, vector = P(every, None), P(None, every), P(every)
    return jax.shard_map(
        make_block("wide", dp, tp_size, dp_size),
        mesh=mesh,
        in_specs=(
            rows,
            vector,
            rows,
            vector,
            rows,
            rows,
            columns,
            vector,
            columns,
            vector,
            columns,
            vector,
            vector,
            rows,
            vector,
            rows,
            rows,
            rows,
        ),
        out_specs=(
            rows,
            rows,
            vector,
            rows,
            rows,
            columns,
            vector,
            columns,
            vector,
            columns,
            vector,
            vector,
            rows,
            vector,
            rows,
            rows,
            rows,
        ),
        check_vma=False,
    )
```

```python
import functools

import jax
import jax.numpy as jnp
from jax import lax
from jax.experimental import pallas as pl
from jax.experimental.pallas import tpu as pltpu
from jax.sharding import Mesh
from jax.sharding import PartitionSpec as P

EPSILON = 1e-06
RATE_SCALE = 8.0
GELU_ROOT = 0.7978845608028654
GELU_CUBE = 0.044715
LANES = 128
PLANE = 4


def matmul_low(left, right):
    return jnp.dot(left, right, preferred_element_type=jnp.float32)


def matmul_nt(left, right):
    return lax.dot_general(left, right, (((1,), (1,)), ((), ())), preferred_element_type=jnp.float32)


def matmul_tn(left, right):
    return lax.dot_general(left, right, (((0,), (0,)), ((), ())), preferred_element_type=jnp.float32)


def rms_inverse(values):
    return lax.rsqrt(jnp.mean(values * values, axis=-1, keepdims=True) + EPSILON)


def rms_back(values, inverse, gain, grads):
    scaled = grads * gain
    dots = jnp.mean(scaled * values, axis=-1, keepdims=True)
    return inverse * scaled - values * (inverse * inverse * inverse * dots)


def gelu_pair(values):
    square = values * values
    slope = jnp.tanh(GELU_ROOT * values * (1.0 + GELU_CUBE * square))
    half = 0.5 * (1.0 + slope)
    grad = half + 0.5 * values * (1.0 - slope * slope) * (GELU_ROOT * (1.0 + 3.0 * GELU_CUBE * square))
    return values * half, grad


def minus_expm1(values):
    series = 1.0 + values * (1.0 / 6.0) * (1.0 + values * (1.0 / 7.0))
    for order in (5.0, 4.0, 3.0, 2.0):
        series = 1.0 + values * (1.0 / order) * series
    return jnp.where(values > -0.25, -values * series, 1.0 - jnp.exp(values))


def softplus_minus(values):
    return jnp.maximum(-values, 0.0) + jnp.log(1.0 + jnp.exp(-jnp.abs(values)))


def lru_terms(conv, rate_pre, input_pre, soft):
    rate_gate = 1.0 / (1.0 + jnp.exp(-rate_pre))
    input_gate = 1.0 / (1.0 + jnp.exp(-input_pre))
    log_decay = -RATE_SCALE * rate_gate * soft
    decay_now = jnp.exp(log_decay)
    scale_in = jnp.sqrt(minus_expm1(2.0 * log_decay))
    return rate_gate, input_gate, decay_now, scale_in


CHUNK = 64
UNROLL = 8


def lru_forward_kernel(seqs, conv_ref, rate_ref, input_ref, gate_ref, soft_ref, states_ref, mixed_ref, decay_s, drive_s):
    rows = conv_ref.shape[0]
    length = rows // seqs
    soft = soft_ref[0:1, :]

    def prepare(i, carry):
        at = pl.ds(pl.multiple_of(i * CHUNK, CHUNK), CHUNK)
        conv = conv_ref[at, :].astype(jnp.float32)
        _, input_gate, decay_now, scale_in = lru_terms(conv, rate_ref[at, :], input_ref[at, :], soft)
        decay_s[at, :] = decay_now
        drive_s[at, :] = scale_in * input_gate * conv
        return carry

    lax.fori_loop(0, rows // CHUNK, prepare, 0)

    def advance(i, state):
        for j in range(UNROLL):
            at = pl.ds(i * UNROLL + j, seqs, stride=length)
            state = decay_s[at, :] * state + drive_s[at, :]
            states_ref[at, :] = state
        return state

    lax.fori_loop(0, length // UNROLL, advance, jnp.zeros((seqs, LANES), jnp.float32))

    def finish(i, carry):
        at = pl.ds(pl.multiple_of(i * CHUNK, CHUNK), CHUNK)
        value, _ = gelu_pair(gate_ref[at, :])
        mixed_ref[at, :] = (states_ref[at, :] * value).astype(jnp.bfloat16)
        return carry

    lax.fori_loop(0, rows // CHUNK, finish, 0)


def lru_backward_kernel(
    seqs,
    conv_ref,
    rate_ref,
    input_ref,
    gate_ref,
    soft_ref,
    states_ref,
    grad_ref,
    d_conv_ref,
    d_rate_ref,
    d_input_ref,
    d_gate_ref,
    sums_ref,
    decay_s,
    flow_s,
    before_s,
):
    rows = conv_ref.shape[0]
    length = rows // seqs
    soft = soft_ref[0:1, :]

    def prepare(i, carry):
        at = pl.ds(pl.multiple_of(i * CHUNK, CHUNK), CHUNK)
        value, slope = gelu_pair(gate_ref[at, :])
        grad = grad_ref[at, :]
        d_gate_ref[at, :] = (grad * states_ref[at, :] * slope).astype(jnp.bfloat16)
        flow_s[at, :] = grad * value
        rate_gate = 1.0 / (1.0 + jnp.exp(-rate_ref[at, :]))
        decay_s[at, :] = jnp.exp(-RATE_SCALE * rate_gate * soft)
        return carry

    lax.fori_loop(0, rows // CHUNK, prepare, 0)

    def retreat(i, carry):
        flow, decay = carry
        for j in range(UNROLL):
            step = length - 1 - (i * UNROLL + j)
            at = pl.ds(step, seqs, stride=length)
            flow = flow_s[at, :] + decay * flow
            flow_s[at, :] = flow
            decay = decay_s[at, :]
        return flow, decay

    nothing = jnp.zeros((seqs, LANES), jnp.float32)
    lax.fori_loop(0, length // UNROLL, retreat, (nothing, nothing))

    def shift(i, last):
        for j in range(UNROLL):
            at = pl.ds(i * UNROLL + j, seqs, stride=length)
            before_s[at, :] = last
            last = states_ref[at, :]
        return last

    lax.fori_loop(0, length // UNROLL, shift, nothing)

    def finish(i, carry):
        rate_sum, input_sum, soft_sum = carry
        at = pl.ds(pl.multiple_of(i * CHUNK, CHUNK), CHUNK)
        conv = conv_ref[at, :].astype(jnp.float32)
        rate_gate, input_gate, decay_now, scale_in = lru_terms(conv, rate_ref[at, :], input_ref[at, :], soft)
        flow = flow_s[at, :]
        d_scale = flow * input_gate * conv
        d_log = decay_now * (flow * before_s[at, :] - d_scale * decay_now / scale_in)
        d_input = flow * scale_in * conv * input_gate * (1.0 - input_gate)
        d_rate = d_log * (-RATE_SCALE) * soft * rate_gate * (1.0 - rate_gate)
        d_conv_ref[at, :] = flow * scale_in * input_gate
        d_rate_ref[at, :] = d_rate.astype(jnp.bfloat16)
        d_input_ref[at, :] = d_input.astype(jnp.bfloat16)

        def fold(total, part):
            for k in range(CHUNK // 8):
                total = total + part[k * 8 : (k + 1) * 8, :]
            return total

        return (fold(rate_sum, d_rate), fold(input_sum, d_input), fold(soft_sum, d_log * (-RATE_SCALE) * rate_gate))

    blank = jnp.zeros((8, LANES), jnp.float32)
    rate_sum, input_sum, soft_sum = lax.fori_loop(0, rows // CHUNK, finish, (blank, blank, blank))
    sums_ref[0:8, :] = rate_sum
    sums_ref[8:16, :] = input_sum
    sums_ref[16:24, :] = soft_sum


def lru_forward(seqs, conv, rate_pre, input_pre, gate_pre, soft):
    rows, channels = conv.shape
    block = pl.BlockSpec((rows, LANES), lambda i: (0, i))
    return pl.pallas_call(
        functools.partial(lru_forward_kernel, seqs),
        grid=(pl.cdiv(channels, LANES),),
        out_shape=(
            jax.ShapeDtypeStruct((rows, channels), jnp.float32),
            jax.ShapeDtypeStruct((rows, channels), jnp.bfloat16),
        ),
        in_specs=[block, block, block, block, pl.BlockSpec((8, LANES), lambda i: (0, i))],
        out_specs=(block, block),
        scratch_shapes=[pltpu.VMEM((rows, LANES), jnp.float32)] * 2,
        compiler_params=pltpu.CompilerParams(vmem_limit_bytes=48 * 2**20),
        name="lru_forward",
    )(conv, rate_pre, input_pre, gate_pre, soft)


def lru_backward(seqs, conv, rate_pre, input_pre, gate_pre, soft, states, grads):
    rows, channels = conv.shape
    block = pl.BlockSpec((rows, LANES), lambda i: (0, i))
    return pl.pallas_call(
        functools.partial(lru_backward_kernel, seqs),
        grid=(pl.cdiv(channels, LANES),),
        out_shape=(
            jax.ShapeDtypeStruct((rows, channels), jnp.float32),
            jax.ShapeDtypeStruct((rows, channels), jnp.bfloat16),
            jax.ShapeDtypeStruct((rows, channels), jnp.bfloat16),
            jax.ShapeDtypeStruct((rows, channels), jnp.bfloat16),
            jax.ShapeDtypeStruct((24, channels), jnp.float32),
        ),
        in_specs=[block, block, block, block, pl.BlockSpec((8, LANES), lambda i: (0, i)), block, block],
        out_specs=(block, block, block, block, pl.BlockSpec((24, LANES), lambda i: (0, i))),
        scratch_shapes=[pltpu.VMEM((rows, LANES), jnp.float32)] * 3,
        compiler_params=pltpu.CompilerParams(vmem_limit_bytes=48 * 2**20),
        name="lru_backward",
    )(conv, rate_pre, input_pre, gate_pre, soft, states, grads)


def block_diagonal(table):
    size, channels = table.shape
    tall = jnp.concatenate([table] * (channels // size), axis=0)
    row_head = lax.broadcasted_iota(jnp.int32, tall.shape, 0) // size
    column_head = lax.broadcasted_iota(jnp.int32, tall.shape, 1) // size
    return jnp.where(row_head == column_head, tall, jnp.zeros_like(tall))


def diagonal_blocks(square, size):
    channels = square.shape[0]
    cube = square.reshape(channels // size, size, channels)
    row_head = lax.broadcasted_iota(jnp.int32, cube.shape, 0)
    column_head = lax.broadcasted_iota(jnp.int32, cube.shape, 2) // size
    return jnp.sum(jnp.where(row_head == column_head, cube, jnp.zeros_like(cube)), axis=0)


def shift_rows(values, seqs, by):
    rows, channels = values.shape
    length = rows // seqs
    cube = values.reshape(seqs, length, channels)
    if by > 0:
        cube = jnp.pad(cube, ((0, 0), (by, 0), (0, 0)))[:, :length]
    elif by < 0:
        cube = jnp.pad(cube, ((0, 0), (0, -by), (0, 0)))[:, -by:]
    return cube.reshape(rows, channels)


def make_block(rest_size, narrow_size):
    bf16, f32 = jnp.bfloat16, jnp.float32
    spread = ("rest", "narrow")

    def swap(values, mask):
        return lax.ppermute(values, "wide", [(i, i ^ mask) for i in range(PLANE)])

    def gather_rows(shard):
        half = shard.shape[0] // 2
        one, two = swap(shard, 1), swap(shard, 2)
        far = [swap(one[:half], 2), swap(two[half:], 1)]
        return jnp.concatenate(far + [one, two, shard], axis=0)

    def scatter_rows(parts):
        far, one, two, own = parts
        half = own.shape[0] // 2
        via_one, via_two = swap(far[:half], 1), swap(far[half:], 2)
        one_low, two_high = swap(one[:half], 1), swap(two[half:], 2)
        one_high = swap((one[half:].astype(f32) + via_two.astype(f32)).astype(bf16), 1)
        two_low = swap((two[:half].astype(f32) + via_one.astype(f32)).astype(bf16), 2)
        low = own[:half].astype(f32) + one_low.astype(f32) + two_low.astype(f32)
        high = own[half:].astype(f32) + one_high.astype(f32) + two_high.astype(f32)
        return jnp.concatenate([low, high], axis=0)

    def rows_to_parts(values):
        return jnp.split(values, PLANE, axis=0)

    def gather_columns(blocks):
        part = lax.all_to_all(blocks, "wide", 0, 0, tiled=False)
        plane, rows, columns = part.shape
        whole = lax.all_gather(part.reshape(plane * rows, columns), spread, axis=0, tiled=True)
        whole = whole.reshape(rest_size * narrow_size, plane, rows, columns)
        return whole.swapaxes(0, 1).reshape(-1, columns)

    def reduce_spread(values):
        if rest_size == 2:
            me = lax.axis_index("rest")
            theirs = lax.dynamic_index_in_dim(values, 1 - me, 0, keepdims=False)
            mine = lax.dynamic_index_in_dim(values, me, 0, keepdims=False)
            other = lax.ppermute(theirs, "rest", [(0, 1), (1, 0)])
            total = (mine.astype(f32) + other.astype(f32)).astype(values.dtype)
        else:
            total = lax.psum_scatter(values, "rest", scatter_dimension=0, tiled=False)
        flat = total.reshape(-1, total.shape[-1])
        return lax.psum_scatter(flat, "narrow", scatter_dimension=0, tiled=True)

    def reduce_columns(grad, rows):
        columns = grad.shape[-1]
        cut = grad.reshape(PLANE, rest_size, narrow_size, rows, columns)
        mine = reduce_spread(cut.transpose(1, 2, 0, 3, 4))
        return lax.all_to_all(mine.reshape(PLANE, rows, columns), "wide", 0, 1, tiled=False)

    def reduce_rows(grad):
        return reduce_spread(grad.reshape(rest_size, narrow_size, -1, grad.shape[-1]))

    def sum_all(values):
        values = values + swap(values, 1)
        values = values + swap(values, 2)
        if rest_size == 2:
            values = values + lax.ppermute(values, "rest", [(0, 1), (1, 0)])
        else:
            values = lax.psum(values, "rest")
        total = values
        for step in range(1, narrow_size):
            total = total + lax.ppermute(values, "narrow", [(i, (i + step) % narrow_size) for i in range(narrow_size)])
        return total

    def on_device(
        tokens,
        lengths,
        cotangent,
        norm_gain1,
        gate_in,
        x_in,
        conv_kernel,
        conv_bias,
        rate_weight,
        rate_bias,
        input_weight,
        input_bias,
        decay_param,
        out_proj,
        norm_gain2,
        mlp_gate,
        mlp_up,
        mlp_down,
    ):
        row_count, width = tokens.shape
        head = rate_weight.shape[0]
        rows = gate_in.shape[0]
        taps = conv_kernel.shape[0]
        seqs = PLANE
        channels = gate_in.shape[1] // PLANE
        hidden = mlp_gate.shape[1] // PLANE
        live = (jnp.arange(row_count, dtype=jnp.int32) < lengths[0]).astype(f32)[:, None]

        def by_plane(*weights):
            cut = [w.reshape(rows, PLANE, -1).swapaxes(0, 1) for w in weights]
            return jnp.concatenate(cut, axis=2)

        gains = jnp.pad(jnp.stack([norm_gain1, norm_gain2], axis=1), ((0, 0), (0, LANES - 2)))
        gains = jnp.broadcast_to(gains[None], (PLANE, rows, LANES))
        w_rec = gather_columns(jnp.concatenate([by_plane(gate_in, x_in), gains], axis=2))
        table = jnp.concatenate(
            [
                conv_kernel,
                conv_bias[None],
                rate_weight,
                rate_bias[None],
                input_weight,
                input_bias[None],
                decay_param[None],
            ],
            axis=0,
        )
        cuts = [taps, 1, head, 1, head, 1, 1]
        places = [sum(cuts[:i]) for i in range(len(cuts) + 1)]
        table = jnp.pad(table, ((0, -places[-1] % LANES), (0, 0)))
        out_and_table = lax.all_gather(jnp.concatenate([out_proj, table.T], axis=1), spread, axis=0, tiled=True)
        w_mlp = gather_columns(by_plane(mlp_gate, mlp_up))
        w_down = lax.all_gather(mlp_down, spread, axis=0, tiled=True)

        low_res = (cotangent.astype(f32) * live).astype(bf16)
        tokens_all = gather_rows(tokens)
        low_res_all = gather_rows(low_res)

        gain_one = w_rec[:, 2 * channels].astype(f32)[None]
        gain_two = w_rec[:, 2 * channels + 1].astype(f32)[None]
        w_rec = w_rec[:, : 2 * channels]
        w_out = out_and_table[:, :width]
        table = out_and_table[:, width:].T
        kernel, shift, rate_table, b_rate, input_table, b_input, decay = (
            table[places[i] : places[i + 1]] for i in range(len(cuts))
        )
        kernel_f, shift_f, b_rate, b_input, decay_f = (v.astype(f32) for v in (kernel, shift, b_rate, b_input, decay))
        w_rate = block_diagonal(rate_table)
        w_input = block_diagonal(input_table)
        soft = softplus_minus(decay_f)
        soft_rows = jnp.broadcast_to(soft, (8, soft.shape[1]))

        tokens_f = tokens_all.astype(f32)
        normed1 = (tokens_f * rms_inverse(tokens_f) * gain_one).astype(bf16)
        gate_pre = matmul_low(normed1, w_rec[:, :channels])
        branch_pre = matmul_low(normed1, w_rec[:, channels:])
        conv = shift_f
        for tap in range(taps):
            conv = conv + kernel_f[tap] * shift_rows(branch_pre, seqs, taps - 1 - tap)
        conv = conv.astype(bf16)
        rate_pre = matmul_low(conv, w_rate) + b_rate
        input_pre = matmul_low(conv, w_input) + b_input
        states, mixed = lru_forward(seqs, conv, rate_pre, input_pre, gate_pre, soft_rows)
        merged = tokens.astype(f32) + scatter_rows(rows_to_parts(matmul_low(mixed, w_out).astype(bf16)))

        inverse2 = rms_inverse(merged)
        normed2 = (merged * inverse2 * gain_two).astype(bf16)
        normed2_all = gather_rows(normed2)
        gate_two = matmul_low(normed2_all, w_mlp[:, :hidden])
        up_two = matmul_low(normed2_all, w_mlp[:, hidden:])
        value, slope = gelu_pair(gate_two)
        product = (value * up_two).astype(bf16)
        result = merged + scatter_rows(rows_to_parts(matmul_low(product, w_down).astype(bf16)))
        block_out = (result * live).astype(bf16)

        down_out = reduce_rows(matmul_tn(product, low_res_all).astype(bf16)).astype(f32)
        d_product = matmul_nt(low_res_all, w_down)
        d_gate_two = (d_product * up_two * slope).astype(bf16)
        d_up_two = (d_product * value).astype(bf16)
        d_mlp = jnp.concatenate([d_gate_two, d_up_two], axis=1)
        d_normed2 = scatter_rows(rows_to_parts(matmul_nt(d_mlp, w_mlp).astype(bf16)))
        mlp_out = reduce_columns(matmul_tn(normed2_all, d_mlp).astype(bf16), rows)
        grad_gain2 = jnp.sum(d_normed2 * merged * inverse2, axis=0)
        d_merged = low_res.astype(f32) + rms_back(merged, inverse2, gain_two, d_normed2)

        low_merged_all = gather_rows(d_merged.astype(bf16))
        d_mixed = matmul_nt(low_merged_all, w_out)
        out_out = reduce_rows(matmul_tn(mixed, low_merged_all).astype(bf16)).astype(f32)
        d_conv_lru, d_rate, d_input, d_gate, sums = lru_backward(
            seqs, conv, rate_pre, input_pre, gate_pre, soft_rows, states, d_mixed
        )
        sums = sums.reshape(3, 8, -1).sum(axis=1)
        grad_decay = sums[2] * (-1.0 / (1.0 + jnp.exp(decay_f[0])))
        d_conv = d_conv_lru + matmul_nt(d_rate, w_rate) + matmul_nt(d_input, w_input)
        grad_rate_weight = diagonal_blocks(matmul_tn(conv, d_rate), head)
        grad_input_weight = diagonal_blocks(matmul_tn(conv, d_input), head)
        d_branch = jnp.zeros_like(d_conv)
        grad_taps = []
        for tap in range(taps):
            moved = shift_rows(d_conv, seqs, tap - (taps - 1))
            d_branch = d_branch + kernel_f[tap] * moved
            grad_taps.append(jnp.sum(branch_pre * moved, axis=0))
        d_rec = jnp.concatenate([d_gate, d_branch.astype(bf16)], axis=1)
        rec_out = reduce_columns(matmul_tn(normed1, d_rec).astype(bf16), rows)
        d_normed1 = scatter_rows(rows_to_parts(matmul_nt(d_rec, w_rec).astype(bf16)))
        own = tokens.astype(f32)
        inverse1 = rms_inverse(own)
        grad_gain1 = jnp.sum(d_normed1 * own * inverse1, axis=0)
        input_grad = d_merged + rms_back(own, inverse1, gain_one, d_normed1)

        table_grad = jnp.concatenate(
            [
                jnp.stack(grad_taps),
                jnp.sum(d_conv, axis=0)[None],
                grad_rate_weight,
                sums[0:1],
                grad_input_weight,
                sums[1:2],
                grad_decay[None],
            ],
            axis=0,
        )
        table_out = reduce_rows(jnp.pad(table_grad, ((0, -places[-1] % LANES), (0, 0))).T).T
        kernel_out, shift_out, rate_out, rate_bias_out, input_out, input_bias_out, decay_out = (
            table_out[places[i] : places[i + 1]] for i in range(len(cuts))
        )
        index = lax.axis_index(("wide",) + spread)
        gain_sums = sum_all(jnp.stack([grad_gain1, grad_gain2]))
        gain_out = lax.dynamic_slice_in_dim(gain_sums, index * rows, rows, axis=1)

        def whole_rows(cut):
            return cut.reshape(rows, -1).astype(f32)

        return (
            block_out,
            input_grad,
            gain_out[0],
            whole_rows(rec_out[:, :, :channels]),
            whole_rows(rec_out[:, :, channels:]),
            kernel_out,
            shift_out[0],
            rate_out,
            rate_bias_out[0],
            input_out,
            input_bias_out[0],
            decay_out[0],
            out_out,
            gain_out[1],
            whole_rows(mlp_out[:, :, :hidden]),
            whole_rows(mlp_out[:, :, hidden:]),
            down_out,
        )

    return on_device


def solution(mesh):
    wide, narrow = mesh.shape["wide"], mesh.shape["narrow"]
    mesh = Mesh(mesh.devices.reshape(PLANE, wide // PLANE, narrow), ("wide", "rest", "narrow"))
    every = mesh.axis_names
    rows, columns, vector = P(every, None), P(None, every), P(every)
    return jax.shard_map(
        make_block(wide // PLANE, narrow),
        mesh=mesh,
        in_specs=(
            rows,
            vector,
            rows,
            vector,
            rows,
            rows,
            columns,
            vector,
            columns,
            vector,
            columns,
            vector,
            vector,
            rows,
            vector,
            rows,
            rows,
            rows,
        ),
        out_specs=(
            rows,
            rows,
            vector,
            rows,
            rows,
            columns,
            vector,
            columns,
            vector,
            columns,
            vector,
            vector,
            rows,
            vector,
            rows,
            rows,
            rows,
        ),
        check_vma=False,
    )
```

```python
import functools

import jax
import jax.numpy as jnp
from jax import lax
from jax.experimental import pallas as pl
from jax.experimental.pallas import tpu as pltpu
from jax.sharding import Mesh
from jax.sharding import PartitionSpec as P

EPSILON = 1e-06
RATE_SCALE = 8.0
GELU_ROOT = 0.7978845608028654
GELU_CUBE = 0.044715
LANES = 128
PLANE = 4


def matmul_low(left, right):
    return jnp.dot(left, right, preferred_element_type=jnp.float32)


def matmul_nt(left, right):
    return lax.dot_general(left, right, (((1,), (1,)), ((), ())), preferred_element_type=jnp.float32)


def matmul_tn(left, right):
    return lax.dot_general(left, right, (((0,), (0,)), ((), ())), preferred_element_type=jnp.float32)


def rms_inverse(values):
    return lax.rsqrt(jnp.mean(values * values, axis=-1, keepdims=True) + EPSILON)


def rms_back(values, inverse, gain, grads):
    scaled = grads * gain
    dots = jnp.mean(scaled * values, axis=-1, keepdims=True)
    return inverse * scaled - values * (inverse * inverse * inverse * dots)


def gelu_pair(values):
    square = values * values
    slope = jnp.tanh(GELU_ROOT * values * (1.0 + GELU_CUBE * square))
    half = 0.5 * (1.0 + slope)
    grad = half + 0.5 * values * (1.0 - slope * slope) * (GELU_ROOT * (1.0 + 3.0 * GELU_CUBE * square))
    return values * half, grad


def minus_expm1(values):
    series = 1.0 + values * (1.0 / 6.0) * (1.0 + values * (1.0 / 7.0))
    for order in (5.0, 4.0, 3.0, 2.0):
        series = 1.0 + values * (1.0 / order) * series
    return jnp.where(values > -0.25, -values * series, 1.0 - jnp.exp(values))


def softplus_minus(values):
    return jnp.maximum(-values, 0.0) + jnp.log(1.0 + jnp.exp(-jnp.abs(values)))


def lru_terms(conv, rate_pre, input_pre, soft):
    rate_gate = 1.0 / (1.0 + jnp.exp(-rate_pre))
    input_gate = 1.0 / (1.0 + jnp.exp(-input_pre))
    log_decay = -RATE_SCALE * rate_gate * soft
    decay_now = jnp.exp(log_decay)
    scale_in = jnp.sqrt(minus_expm1(2.0 * log_decay))
    return rate_gate, input_gate, decay_now, scale_in


CHUNK = 64
UNROLL = 8


def lru_forward_kernel(seqs, conv_ref, rate_ref, input_ref, gate_ref, soft_ref, states_ref, mixed_ref, decay_s, drive_s):
    rows = conv_ref.shape[0]
    length = rows // seqs
    soft = soft_ref[0:1, :]

    def prepare(i, carry):
        at = pl.ds(pl.multiple_of(i * CHUNK, CHUNK), CHUNK)
        conv = conv_ref[at, :].astype(jnp.float32)
        _, input_gate, decay_now, scale_in = lru_terms(conv, rate_ref[at, :], input_ref[at, :], soft)
        decay_s[at, :] = decay_now
        drive_s[at, :] = scale_in * input_gate * conv
        return carry

    lax.fori_loop(0, rows // CHUNK, prepare, 0)

    def advance(i, state):
        for j in range(UNROLL):
            at = pl.ds(i * UNROLL + j, seqs, stride=length)
            state = decay_s[at, :] * state + drive_s[at, :]
            states_ref[at, :] = state
        return state

    lax.fori_loop(0, length // UNROLL, advance, jnp.zeros((seqs, LANES), jnp.float32))

    def finish(i, carry):
        at = pl.ds(pl.multiple_of(i * CHUNK, CHUNK), CHUNK)
        value, _ = gelu_pair(gate_ref[at, :])
        mixed_ref[at, :] = (states_ref[at, :] * value).astype(jnp.bfloat16)
        return carry

    lax.fori_loop(0, rows // CHUNK, finish, 0)


def lru_backward_kernel(
    seqs,
    conv_ref,
    rate_ref,
    input_ref,
    gate_ref,
    soft_ref,
    states_ref,
    grad_ref,
    d_conv_ref,
    d_rate_ref,
    d_input_ref,
    d_gate_ref,
    sums_ref,
    decay_s,
    flow_s,
    before_s,
):
    rows = conv_ref.shape[0]
    length = rows // seqs
    soft = soft_ref[0:1, :]

    def prepare(i, carry):
        at = pl.ds(pl.multiple_of(i * CHUNK, CHUNK), CHUNK)
        value, slope = gelu_pair(gate_ref[at, :])
        grad = grad_ref[at, :]
        d_gate_ref[at, :] = (grad * states_ref[at, :] * slope).astype(jnp.bfloat16)
        flow_s[at, :] = grad * value
        rate_gate = 1.0 / (1.0 + jnp.exp(-rate_ref[at, :]))
        decay_s[at, :] = jnp.exp(-RATE_SCALE * rate_gate * soft)
        return carry

    lax.fori_loop(0, rows // CHUNK, prepare, 0)

    def retreat(i, carry):
        flow, decay = carry
        for j in range(UNROLL):
            step = length - 1 - (i * UNROLL + j)
            at = pl.ds(step, seqs, stride=length)
            flow = flow_s[at, :] + decay * flow
            flow_s[at, :] = flow
            decay = decay_s[at, :]
        return flow, decay

    nothing = jnp.zeros((seqs, LANES), jnp.float32)
    lax.fori_loop(0, length // UNROLL, retreat, (nothing, nothing))

    def shift(i, last):
        for j in range(UNROLL):
            at = pl.ds(i * UNROLL + j, seqs, stride=length)
            before_s[at, :] = last
            last = states_ref[at, :]
        return last

    lax.fori_loop(0, length // UNROLL, shift, nothing)

    def finish(i, carry):
        rate_sum, input_sum, soft_sum = carry
        at = pl.ds(pl.multiple_of(i * CHUNK, CHUNK), CHUNK)
        conv = conv_ref[at, :].astype(jnp.float32)
        rate_gate, input_gate, decay_now, scale_in = lru_terms(conv, rate_ref[at, :], input_ref[at, :], soft)
        flow = flow_s[at, :]
        d_scale = flow * input_gate * conv
        d_log = decay_now * (flow * before_s[at, :] - d_scale * decay_now / scale_in)
        d_input = flow * scale_in * conv * input_gate * (1.0 - input_gate)
        d_rate = d_log * (-RATE_SCALE) * soft * rate_gate * (1.0 - rate_gate)
        d_conv_ref[at, :] = flow * scale_in * input_gate
        d_rate_ref[at, :] = d_rate.astype(jnp.bfloat16)
        d_input_ref[at, :] = d_input.astype(jnp.bfloat16)

        def fold(total, part):
            for k in range(CHUNK // 8):
                total = total + part[k * 8 : (k + 1) * 8, :]
            return total

        return (fold(rate_sum, d_rate), fold(input_sum, d_input), fold(soft_sum, d_log * (-RATE_SCALE) * rate_gate))

    blank = jnp.zeros((8, LANES), jnp.float32)
    rate_sum, input_sum, soft_sum = lax.fori_loop(0, rows // CHUNK, finish, (blank, blank, blank))
    sums_ref[0:8, :] = rate_sum
    sums_ref[8:16, :] = input_sum
    sums_ref[16:24, :] = soft_sum


def lru_forward(seqs, conv, rate_pre, input_pre, gate_pre, soft):
    rows, channels = conv.shape
    block = pl.BlockSpec((rows, LANES), lambda i: (0, i))
    return pl.pallas_call(
        functools.partial(lru_forward_kernel, seqs),
        grid=(pl.cdiv(channels, LANES),),
        out_shape=(
            jax.ShapeDtypeStruct((rows, channels), jnp.float32),
            jax.ShapeDtypeStruct((rows, channels), jnp.bfloat16),
        ),
        in_specs=[block, block, block, block, pl.BlockSpec((8, LANES), lambda i: (0, i))],
        out_specs=(block, block),
        scratch_shapes=[pltpu.VMEM((rows, LANES), jnp.float32)] * 2,
        compiler_params=pltpu.CompilerParams(vmem_limit_bytes=48 * 2**20),
        cost_estimate=pl.CostEstimate(flops=200000 * rows * channels // 10, bytes_accessed=20 * rows * channels, transcendentals=8 * rows * channels),
        name="lru_forward",
    )(conv, rate_pre, input_pre, gate_pre, soft)


def lru_backward(seqs, conv, rate_pre, input_pre, gate_pre, soft, states, grads):
    rows, channels = conv.shape
    block = pl.BlockSpec((rows, LANES), lambda i: (0, i))
    return pl.pallas_call(
        functools.partial(lru_backward_kernel, seqs),
        grid=(pl.cdiv(channels, LANES),),
        out_shape=(
            jax.ShapeDtypeStruct((rows, channels), jnp.float32),
            jax.ShapeDtypeStruct((rows, channels), jnp.bfloat16),
            jax.ShapeDtypeStruct((rows, channels), jnp.bfloat16),
            jax.ShapeDtypeStruct((rows, channels), jnp.bfloat16),
            jax.ShapeDtypeStruct((24, channels), jnp.float32),
        ),
        in_specs=[block, block, block, block, pl.BlockSpec((8, LANES), lambda i: (0, i)), block, block],
        out_specs=(block, block, block, block, pl.BlockSpec((24, LANES), lambda i: (0, i))),
        scratch_shapes=[pltpu.VMEM((rows, LANES), jnp.float32)] * 3,
        compiler_params=pltpu.CompilerParams(vmem_limit_bytes=48 * 2**20),
        cost_estimate=pl.CostEstimate(flops=200000 * rows * channels // 10, bytes_accessed=20 * rows * channels, transcendentals=16 * rows * channels),
        name="lru_backward",
    )(conv, rate_pre, input_pre, gate_pre, soft, states, grads)


CONSTANT = pl.Buffered(1)
VMEM_BYTES = 56 * 2**20


def column_block(columns, most):
    return max(w for w in range(LANES, most + 1, LANES) if columns % w == 0)


def mlp_kernel(slots, n2_ref, low_ref, gate_ref, up_ref, down_ref, product_ref, d_gate_ref, d_up_ref, w_s):
    groups, rows = gate_ref.shape[1], gate_ref.shape[2]
    stride = gate_ref.shape[0] * rows
    for c in range(groups):
        for k in range(gate_ref.shape[0]):
            at = pl.ds(c * stride + k * rows, rows)
            w_s[0, at, :] = gate_ref[k, c]
            w_s[1, at, :] = up_ref[k, c]
    length = n2_ref.shape[0] // slots

    for i in range(slots):
        at = pl.ds(i * length, length)
        here = n2_ref[at, :]
        gate = jnp.dot(here, w_s[0], preferred_element_type=jnp.float32)
        up = jnp.dot(here, w_s[1], preferred_element_type=jnp.float32)
        grad = matmul_nt(low_ref[at, :], down_ref[...])
        value, slope = gelu_pair(gate)
        product_ref[at, :] = (value * up).astype(jnp.bfloat16)
        d_gate_ref[at, :] = (grad * up * slope).astype(jnp.bfloat16)
        d_up_ref[at, :] = (grad * value).astype(jnp.bfloat16)


def mlp_both(slots, normed, low_res, weights, w_down):
    tokens, width = normed.shape
    hidden = w_down.shape[0]
    block = column_block(hidden, 256)
    steps = hidden // block
    lead = weights.shape[:3]
    return pl.pallas_call(
        functools.partial(mlp_kernel, slots),
        grid=(steps,),
        out_shape=(jax.ShapeDtypeStruct((tokens, hidden), jnp.bfloat16),) * 3,
        in_specs=[
            pl.BlockSpec((tokens, width), lambda j: (0, 0), pipeline_mode=CONSTANT),
            pl.BlockSpec((tokens, width), lambda j: (0, 0), pipeline_mode=CONSTANT),
            pl.BlockSpec(lead + (block,), lambda j: (0, 0, 0, j)),
            pl.BlockSpec(lead + (block,), lambda j: (0, 0, 0, j + steps)),
            pl.BlockSpec((block, width), lambda j: (j, 0)),
        ],
        out_specs=(pl.BlockSpec((tokens, block), lambda j: (0, j)),) * 3,
        scratch_shapes=[pltpu.VMEM((2, width, block), jnp.bfloat16)],
        compiler_params=pltpu.CompilerParams(vmem_limit_bytes=VMEM_BYTES),
        cost_estimate=pl.CostEstimate(
            flops=6 * tokens * width * hidden, bytes_accessed=2 * (2 * tokens * width + 3 * width * hidden), transcendentals=tokens * hidden
        ),
        name="mlp_both",
    )(normed, low_res, weights, weights, w_down)


def store_parts(refs, length, part, value):
    value = value.astype(jnp.bfloat16)
    if part == 0:
        refs[0][...] = value[: length // 2]
        refs[1][...] = value[length // 2 :]
    else:
        refs[part + 1][...] = value


def store_all(refs, total):
    length = refs[-1].shape[0]
    for part in range(PLANE):
        store_parts(refs, length, part, total[part * length : (part + 1) * length])


def back_kernel(pieces, *refs):
    grads, w_ref, outs = refs[:pieces], refs[pieces], refs[pieces + 1 :]
    shares, _, rows, _ = w_ref.shape
    total = None
    start = 0
    for grads_ref in grads:
        cut = grads_ref.shape[1]
        weight = w_ref[:, 0, :, start : start + cut].reshape(shares * rows, cut)
        term = matmul_nt(grads_ref[...], weight)
        total = term if total is None else total + term
        start += cut
    store_all(outs, total)


def parts_out(length, width, block):
    heights = (length // 2, length // 2, length, length, length)
    return (
        tuple(jax.ShapeDtypeStruct((h, width), jnp.bfloat16) for h in heights),
        tuple(pl.BlockSpec((h, block), lambda j: (0, j)) for h in heights),
    )


def back_parts(grads, weights):
    tokens = grads[0].shape[0]
    inner = sum(g.shape[1] for g in grads)
    shares, groups, rows, columns = weights.shape
    block = shares * rows
    shapes, specs = parts_out(tokens // PLANE, groups * block, block)
    return pl.pallas_call(
        functools.partial(back_kernel, len(grads)),
        grid=(groups,),
        out_shape=shapes,
        in_specs=[pl.BlockSpec(g.shape, lambda j: (0, 0), pipeline_mode=CONSTANT) for g in grads]
        + [pl.BlockSpec((shares, 1, rows, columns), lambda j: (0, j, 0, 0))],
        out_specs=specs,
        compiler_params=pltpu.CompilerParams(vmem_limit_bytes=VMEM_BYTES),
        cost_estimate=pl.CostEstimate(
            flops=2 * tokens * inner * groups * block,
            bytes_accessed=2 * (tokens * inner + groups * block * (columns + tokens)),
            transcendentals=0,
        ),
        name="back_parts",
    )(*grads, weights)


def out_kernel(values_ref, w_ref, *refs):
    store_all(refs, jnp.dot(values_ref[...], w_ref[...], preferred_element_type=jnp.float32))


def out_parts(values, weight):
    tokens, inner = values.shape
    width = weight.shape[1]
    block = column_block(width, 512)
    shapes, specs = parts_out(tokens // PLANE, width, block)
    return pl.pallas_call(
        out_kernel,
        grid=(width // block,),
        out_shape=shapes,
        in_specs=[
            pl.BlockSpec((tokens, inner), lambda j: (0, 0), pipeline_mode=CONSTANT),
            pl.BlockSpec((inner, block), lambda j: (0, j)),
        ],
        out_specs=specs,
        compiler_params=pltpu.CompilerParams(vmem_limit_bytes=VMEM_BYTES),
        cost_estimate=pl.CostEstimate(
            flops=2 * tokens * inner * width, bytes_accessed=2 * (tokens * inner + inner * width + tokens * width), transcendentals=0
        ),
        name="out_parts",
    )(values, weight)


def weight_grad_kernel(rows, me_ref, left_ref, right_ref, mine_ref, theirs_ref, left_s):
    @pl.when(pl.program_id(1) == 0)
    def _():
        left_s[...] = left_ref[...].T

    narrow, groups, _, block = mine_ref.shape
    height = narrow * rows
    total = jnp.dot(left_s[...], right_ref[0], preferred_element_type=jnp.float32).astype(jnp.bfloat16)

    def store(first_ref, second_ref):
        for g in range(groups):
            for share, ref in enumerate((first_ref, second_ref)):
                start = (g * 2 + share) * height
                ref[:, g] = total[start : start + height].reshape(narrow, rows, block)

    @pl.when(me_ref[0] == 0)
    def _():
        store(mine_ref, theirs_ref)

    @pl.when(me_ref[0] != 0)
    def _():
        store(theirs_ref, mine_ref)


def weight_grad(me, left, right, narrow, groups, rows):
    tokens = left.shape[0]
    pieces, _, piece = right.shape
    block = column_block(piece, 768)
    steps = piece // block
    together = 2 if groups % 2 == 0 else 1
    height = together * 2 * narrow * rows
    place = pl.BlockSpec((narrow, together, rows, block), lambda g, j, me_ref: (0, g, 0, j))
    shape = jax.ShapeDtypeStruct((narrow, groups, rows, pieces * piece), jnp.bfloat16)
    return pl.pallas_call(
        functools.partial(weight_grad_kernel, rows),
        grid_spec=pltpu.PrefetchScalarGridSpec(
            num_scalar_prefetch=1,
            grid=(groups // together, pieces * steps),
            in_specs=[
                pl.BlockSpec((tokens, height), lambda g, j, me_ref: (0, g)),
                pl.BlockSpec((1, tokens, block), lambda g, j, me_ref: (j // steps, 0, j % steps)),
            ],
            out_specs=(place, place),
            scratch_shapes=[pltpu.VMEM((height, tokens), jnp.bfloat16)],
        ),
        out_shape=(shape, shape),
        compiler_params=pltpu.CompilerParams(vmem_limit_bytes=VMEM_BYTES),
        cost_estimate=pl.CostEstimate(
            flops=2 * tokens * left.shape[1] * pieces * piece,
            bytes_accessed=2 * (left.size + groups // together * right.size + left.shape[1] * pieces * piece),
            transcendentals=0,
        ),
        name="weight_grad",
    )(me, left, right)


def block_diagonal(table):
    size, channels = table.shape
    tall = jnp.concatenate([table] * (channels // size), axis=0)
    row_head = lax.broadcasted_iota(jnp.int32, tall.shape, 0) // size
    column_head = lax.broadcasted_iota(jnp.int32, tall.shape, 1) // size
    return jnp.where(row_head == column_head, tall, jnp.zeros_like(tall))


def diagonal_blocks(square, size):
    channels = square.shape[0]
    cube = square.reshape(channels // size, size, channels)
    row_head = lax.broadcasted_iota(jnp.int32, cube.shape, 0)
    column_head = lax.broadcasted_iota(jnp.int32, cube.shape, 2) // size
    return jnp.sum(jnp.where(row_head == column_head, cube, jnp.zeros_like(cube)), axis=0)


def shift_rows(values, seqs, by):
    rows, channels = values.shape
    length = rows // seqs
    cube = values.reshape(seqs, length, channels)
    if by > 0:
        cube = jnp.pad(cube, ((0, 0), (by, 0), (0, 0)))[:, :length]
    elif by < 0:
        cube = jnp.pad(cube, ((0, 0), (0, -by), (0, 0)))[:, -by:]
    return cube.reshape(rows, channels)


def make_block(rest_size, narrow_size):
    bf16, f32 = jnp.bfloat16, jnp.float32
    spread = ("rest", "narrow")

    def swap(values, mask):
        return lax.ppermute(values, "wide", [(i, i ^ mask) for i in range(PLANE)])

    def gather_rows(shard):
        half = shard.shape[0] // 2
        one, two = swap(shard, 1), swap(shard, 2)
        far = [swap(one[:half], 2), swap(two[half:], 1)]
        return jnp.concatenate(far + [one, two, shard], axis=0)

    def scatter_rows(parts, *hold):
        far_low, far_high, one, two, own = parts
        half = own.shape[0] // 2
        via_one, via_two = swap(far_low, 1), swap(far_high, 2)
        one, two = after(one, *hold), after(two, *hold)
        one = jnp.concatenate([one[:half], (one[half:].astype(f32) + via_two.astype(f32)).astype(bf16)], axis=0)
        two = jnp.concatenate([(two[:half].astype(f32) + via_one.astype(f32)).astype(bf16), two[half:]], axis=0)
        return own.astype(f32) + swap(one, 1).astype(f32) + swap(two, 2).astype(f32)

    def cut_columns(blocks):
        return lax.all_to_all(blocks, "wide", 0, 0, tiled=False)

    def gather_spread(part):
        whole = lax.all_gather(part.reshape(-1, part.shape[-1]), spread, axis=0, tiled=True)
        return whole.reshape((rest_size * narrow_size,) + part.shape)

    def grad_shares(left, right, rows, groups):
        if rest_size != 2:
            grad = matmul_tn(left, right.swapaxes(0, 1).reshape(right.shape[1], -1)).astype(bf16)
            cut = grad.reshape(groups, rest_size, narrow_size, rows, -1).transpose(1, 2, 0, 3, 4)
            return grad, lambda *waits: lax.psum_scatter(after(cut, *waits), "rest", scatter_dimension=0, tiled=False)
        me = lax.axis_index("rest").astype(jnp.int32)[None]
        mine, theirs = weight_grad(me, left, right, narrow_size, groups, rows)
        other = lax.ppermute(theirs, "rest", [(0, 1), (1, 0)])
        return theirs, lambda *waits: (after(mine, *waits).astype(f32) + other.astype(f32)).astype(bf16)

    def sum_rest(values):
        if rest_size != 2:
            return lax.psum_scatter(values, "rest", scatter_dimension=0, tiled=False)
        me = lax.axis_index("rest")
        theirs = lax.dynamic_index_in_dim(values, 1 - me, 0, keepdims=False)
        mine = lax.dynamic_index_in_dim(values, me, 0, keepdims=False)
        other = lax.ppermute(theirs, "rest", [(0, 1), (1, 0)])
        return (mine.astype(f32) + other.astype(f32)).astype(values.dtype)

    def sum_narrow(values):
        return lax.psum_scatter(values.reshape(-1, values.shape[-1]), "narrow", scatter_dimension=0, tiled=True)

    def columns_home(mine, rows):
        return lax.all_to_all(mine.reshape(PLANE, rows, -1), "wide", 0, 1, tiled=False)

    def sum_narrow_direct(values):
        me = lax.axis_index("narrow")
        total = lax.dynamic_index_in_dim(values, me, 0, keepdims=False).astype(f32)
        for step in range(1, narrow_size):
            part = lax.dynamic_index_in_dim(values, lax.rem(me + step, narrow_size), 0, keepdims=False)
            pairs = [(i, (i + step) % narrow_size) for i in range(narrow_size)]
            total = total + lax.ppermute(part, "narrow", pairs).astype(f32)
        return total

    def to_all(values, axes, count):
        return lax.all_to_all(jnp.broadcast_to(values[None], (count,) + values.shape), axes, 0, 0, tiled=False)

    def rows_cut(grad):
        return grad.reshape(rest_size, narrow_size, -1, grad.shape[-1])

    def fence(*values):
        return lax.optimization_barrier(values)

    def after(values, *others):
        return lax.optimization_barrier((values,) + others)[0]

    def sum_all(values):
        values = values + swap(values, 1)
        values = values + swap(values, 2)
        if rest_size == 2:
            values = values + lax.ppermute(values, "rest", [(0, 1), (1, 0)])
        else:
            values = lax.psum(values, "rest")
        total = values
        for step in range(1, narrow_size):
            total = total + lax.ppermute(values, "narrow", [(i, (i + step) % narrow_size) for i in range(narrow_size)])
        return total

    def on_device(
        tokens,
        lengths,
        cotangent,
        norm_gain1,
        gate_in,
        x_in,
        conv_kernel,
        conv_bias,
        rate_weight,
        rate_bias,
        input_weight,
        input_bias,
        decay_param,
        out_proj,
        norm_gain2,
        mlp_gate,
        mlp_up,
        mlp_down,
    ):
        row_count, width = tokens.shape
        head = rate_weight.shape[0]
        rows = gate_in.shape[0]
        taps = conv_kernel.shape[0]
        seqs = PLANE
        channels = gate_in.shape[1] // PLANE
        hidden = mlp_gate.shape[1] // PLANE
        live = (jnp.arange(row_count, dtype=jnp.int32) < lengths[0]).astype(f32)[:, None]

        def by_plane(*weights):
            cut = [w.reshape(rows, PLANE, -1).swapaxes(0, 1) for w in weights]
            return jnp.concatenate(cut, axis=2)

        table = jnp.concatenate(
            [
                conv_kernel,
                conv_bias[None],
                rate_weight,
                rate_bias[None],
                input_weight,
                input_bias[None],
                decay_param[None],
            ],
            axis=0,
        )
        cuts = [taps, 1, head, 1, head, 1, 1]
        places = [sum(cuts[:i]) for i in range(len(cuts) + 1)]
        columns = 2 * channels
        shares = rest_size * narrow_size
        part_rec = cut_columns(by_plane(gate_in, x_in)).reshape(PLANE, rows, columns)
        w_rec = gather_spread(part_rec)
        tokens_all = gather_rows(after(tokens, part_rec))
        table = jnp.pad(table, ((0, -places[-1] % LANES), (0, 0))).T
        table = to_all(after(table, part_rec), spread, shares)
        gains = to_all(after(jnp.stack([norm_gain1, norm_gain2]), table), ("wide",) + spread, PLANE * shares)
        cut_mlp = by_plane(mlp_gate, mlp_up)
        w_rec, tokens_all, table, gains, cut_mlp = fence(w_rec, tokens_all, table, gains, cut_mlp)

        out_and_down = lax.all_gather(
            after(jnp.concatenate([out_proj, mlp_down], axis=0), w_rec), spread, axis=0, tiled=True
        ).reshape(rest_size * narrow_size, -1, width)
        low_res = (cotangent.astype(f32) * live).astype(bf16)
        low_res_all = gather_rows(after(low_res, w_rec))
        gains = gains.swapaxes(0, 1).reshape(2, width).astype(f32)
        gain_one, gain_two = gains[0:1], gains[1:2]
        table = table.reshape(channels, -1).T
        w_flat = w_rec.swapaxes(0, 1).reshape(width, columns)
        tokens_f = tokens_all.astype(f32)
        normed1 = (tokens_f * rms_inverse(tokens_f) * gain_one).astype(bf16)
        gate_pre = matmul_low(normed1, w_flat[:, :channels])
        branch_pre = matmul_low(normed1, w_flat[:, channels:])
        kernel, shift, rate_table, b_rate, input_table, b_input, decay = (
            table[places[i] : places[i + 1]] for i in range(len(cuts))
        )
        kernel_f, shift_f, b_rate, b_input, decay_f = (v.astype(f32) for v in (kernel, shift, b_rate, b_input, decay))
        w_rate = block_diagonal(rate_table)
        w_input = block_diagonal(input_table)
        soft = softplus_minus(decay_f)
        soft_rows = jnp.broadcast_to(soft, (8, soft.shape[1]))
        part_mlp = cut_columns(after(cut_mlp, low_res_all))

        conv = shift_f
        for tap in range(taps):
            conv = conv + kernel_f[tap] * shift_rows(branch_pre, seqs, taps - 1 - tap)
        conv = conv.astype(bf16)
        rate_pre = matmul_low(conv, w_rate) + b_rate
        input_pre = matmul_low(conv, w_input) + b_input
        states, mixed = lru_forward(seqs, conv, rate_pre, input_pre, gate_pre, soft_rows)
        mixed, part_mlp, out_and_down = fence(mixed, part_mlp, out_and_down)
        w_out = out_and_down[:, : out_proj.shape[0]].reshape(-1, width)
        w_down = out_and_down[:, out_proj.shape[0] :].reshape(-1, width)

        w_mlp = gather_spread(part_mlp)
        merged = tokens.astype(f32) + scatter_rows(out_parts(mixed, w_out))
        inverse2 = rms_inverse(merged)
        normed2 = (merged * inverse2 * gain_two).astype(bf16)
        normed2_all = gather_rows(normed2)
        normed2_all, w_mlp = fence(normed2_all, w_mlp)

        product, d_gate_two, d_up_two = mlp_both(PLANE, normed2_all, low_res_all, w_mlp, w_down)
        first, finish_down = grad_shares(product, low_res_all[None], mlp_down.shape[0], 1)
        parts2 = back_parts((after(d_gate_two, first), d_up_two), w_mlp)
        grad_down = finish_down(parts2[0])
        down_out = sum_narrow(grad_down)
        d_normed2 = scatter_rows(parts2)
        _, finish = grad_shares(normed2_all, after(d_gate_two, parts2)[None], rows, PLANE)
        grad_mgate = finish()
        d_normed2, grad_mgate, down_out = fence(d_normed2, grad_mgate, down_out)

        mgate_sum = sum_narrow(grad_mgate)
        grad_gain2 = jnp.sum(d_normed2 * merged * inverse2, axis=0)
        d_merged = low_res.astype(f32) + rms_back(merged, inverse2, gain_two, d_normed2)
        low_merged_all = gather_rows(d_merged.astype(bf16))
        _, finish = grad_shares(normed2_all, after(d_up_two, d_normed2)[None], rows, PLANE)
        grad_mup = finish()
        parts_result = out_parts(after(product, d_normed2), w_down)
        low_merged_all, parts_result, grad_mup, mgate_sum = fence(low_merged_all, parts_result, grad_mup, mgate_sum)
        mup_sum = sum_narrow(grad_mup)
        d_mixed = matmul_nt(low_merged_all, w_out)
        d_conv_lru, d_rate, d_input, d_gate, sums = lru_backward(
            seqs, conv, rate_pre, input_pre, gate_pre, soft_rows, states, d_mixed
        )
        result = merged + scatter_rows(parts_result, d_conv_lru)
        mgate_out = columns_home(after(mgate_sum, d_conv_lru), rows)
        sums = sums.reshape(3, 8, -1).sum(axis=1)
        grad_decay = sums[2] * (-1.0 / (1.0 + jnp.exp(decay_f[0])))
        d_conv = d_conv_lru + matmul_nt(d_rate, w_rate) + matmul_nt(d_input, w_input)
        d_branch = jnp.zeros_like(d_conv)
        grad_taps = []
        for tap in range(taps):
            moved = shift_rows(d_conv, seqs, tap - (taps - 1))
            d_branch = d_branch + kernel_f[tap] * moved
            grad_taps.append(jnp.sum(branch_pre * moved, axis=0))
        d_rec = jnp.stack([d_gate, d_branch.astype(bf16)])
        grad_out = sum_rest(rows_cut(matmul_tn(mixed, after(low_merged_all, d_conv_lru)).astype(bf16)))

        d_rec, mup_sum, grad_out = fence(d_rec, mup_sum, grad_out)
        out_out = sum_narrow(grad_out)
        first, finish = grad_shares(normed1, d_rec, rows, PLANE)
        parts1 = back_parts((after(d_rec[0], first), d_rec[1]), w_rec)
        grad_rec = finish(parts1[0])
        mup_out = columns_home(after(mup_sum, d_rec), rows)
        grad_rec, parts1, out_out, mup_out, mgate_out = fence(grad_rec, parts1, out_out, mup_out, mgate_out)
        rec_sum = sum_narrow(grad_rec)
        d_normed1 = scatter_rows(parts1)
        block_out = (after(result, d_normed1) * live).astype(bf16)
        grad_rate_weight = diagonal_blocks(matmul_tn(conv, after(d_rate, grad_rec)), head)
        grad_input_weight = diagonal_blocks(matmul_tn(conv, after(d_input, grad_rec)), head)
        own = tokens.astype(f32)
        inverse1 = rms_inverse(own)
        grad_gain1 = jnp.sum(d_normed1 * own * inverse1, axis=0)
        input_grad = d_merged + rms_back(own, inverse1, gain_one, d_normed1)

        table_grad = jnp.concatenate(
            [
                jnp.stack(grad_taps),
                jnp.sum(d_conv, axis=0)[None],
                grad_rate_weight,
                sums[0:1],
                grad_input_weight,
                sums[1:2],
                grad_decay[None],
            ],
            axis=0,
        )
        table_grad = sum_rest(rows_cut(jnp.pad(table_grad, ((0, -places[-1] % LANES), (0, 0))).T))
        table_out = sum_narrow(after(table_grad, rec_sum)).T
        rec_out = columns_home(rec_sum, rows)
        kernel_out, shift_out, rate_out, rate_bias_out, input_out, input_bias_out, decay_out = (
            table_out[places[i] : places[i + 1]] for i in range(len(cuts))
        )
        index = lax.axis_index(("wide",) + spread)
        gain_sums = sum_all(jnp.stack([grad_gain1, grad_gain2]))
        gain_out = lax.dynamic_slice_in_dim(gain_sums, index * rows, rows, axis=1)

        def whole_rows(cut):
            return cut.reshape(rows, -1).astype(f32)

        return (
            block_out,
            input_grad,
            gain_out[0],
            whole_rows(rec_out[:, :, :channels]),
            whole_rows(rec_out[:, :, channels:]),
            kernel_out,
            shift_out[0],
            rate_out,
            rate_bias_out[0],
            input_out,
            input_bias_out[0],
            decay_out[0],
            out_out.astype(f32),
            gain_out[1],
            whole_rows(mgate_out),
            whole_rows(mup_out),
            down_out.astype(f32),
        )

    return on_device


def solution(mesh):
    wide, narrow = mesh.shape["wide"], mesh.shape["narrow"]
    mesh = Mesh(mesh.devices.reshape(PLANE, wide // PLANE, narrow), ("wide", "rest", "narrow"))
    every = mesh.axis_names
    rows, columns, vector = P(every, None), P(None, every), P(every)
    return jax.shard_map(
        make_block(wide // PLANE, narrow),
        mesh=mesh,
        in_specs=(
            rows,
            vector,
            rows,
            vector,
            rows,
            rows,
            columns,
            vector,
            columns,
            vector,
            columns,
            vector,
            vector,
            rows,
            vector,
            rows,
            rows,
            rows,
        ),
        out_specs=(
            rows,
            rows,
            vector,
            rows,
            rows,
            columns,
            vector,
            columns,
            vector,
            columns,
            vector,
            vector,
            rows,
            vector,
            rows,
            rows,
            rows,
        ),
        check_vma=False,
    )
```

```python
import functools

import jax
import jax.numpy as jnp
from jax import lax
from jax.experimental import pallas as pl
from jax.experimental.pallas import tpu as pltpu
from jax.sharding import Mesh
from jax.sharding import PartitionSpec as P

EPSILON = 1e-06
RATE_SCALE = 8.0
GELU_ROOT = 0.7978845608028654
GELU_CUBE = 0.044715
LANES = 128
PLANE = 4


def matmul_low(left, right):
    return jnp.dot(left, right, preferred_element_type=jnp.float32)


def matmul_nt(left, right):
    return lax.dot_general(left, right, (((1,), (1,)), ((), ())), preferred_element_type=jnp.float32)


def matmul_tn(left, right):
    return lax.dot_general(left, right, (((0,), (0,)), ((), ())), preferred_element_type=jnp.float32)


def rms_inverse(values):
    return lax.rsqrt(jnp.mean(values * values, axis=-1, keepdims=True) + EPSILON)


def rms_back(values, inverse, gain, grads):
    scaled = grads * gain
    dots = jnp.mean(scaled * values, axis=-1, keepdims=True)
    return inverse * scaled - values * (inverse * inverse * inverse * dots)


def gelu_pair(values):
    square = values * values
    slope = jnp.tanh(GELU_ROOT * values * (1.0 + GELU_CUBE * square))
    half = 0.5 * (1.0 + slope)
    grad = half + 0.5 * values * (1.0 - slope * slope) * (GELU_ROOT * (1.0 + 3.0 * GELU_CUBE * square))
    return values * half, grad


def softplus_minus(values):
    return jnp.maximum(-values, 0.0) + jnp.log(1.0 + jnp.exp(-jnp.abs(values)))


def sigmoid(values):
    return 1.0 / (1.0 + jnp.exp(jnp.minimum(-values, 80.0)))


def lru_terms(rate_pre, input_pre, soft):
    rate_gate = sigmoid(rate_pre)
    input_gate = sigmoid(input_pre)
    log_decay = -RATE_SCALE * rate_gate * soft
    decay_now = jnp.exp(log_decay)
    twice = 2.0 * log_decay
    series = -twice * (1.0 + twice * 0.5 * (1.0 + twice * (1.0 / 3.0) * (1.0 + twice * 0.25)))
    square = jnp.maximum(jnp.where(twice > -0.0625, series, 1.0 - decay_now * decay_now), 1e-30)
    return rate_gate, input_gate, decay_now, square, lax.rsqrt(square)


CHUNK = 160
UNROLL = 16


def lru_forward_kernel(seqs, conv_ref, rate_ref, input_ref, gate_ref, soft_ref, states_ref, mixed_ref, decay_s, drive_s):
    rows = conv_ref.shape[0]
    length = rows // seqs
    soft = soft_ref[0:1, :]

    def prepare(i, carry):
        at = pl.ds(pl.multiple_of(i * CHUNK, CHUNK), CHUNK)
        conv = conv_ref[at, :].astype(jnp.float32)
        _, input_gate, decay_now, square, inverse = lru_terms(rate_ref[at, :], input_ref[at, :], soft)
        decay_s[at, :] = decay_now
        drive_s[at, :] = square * inverse * input_gate * conv
        return carry

    lax.fori_loop(0, rows // CHUNK, prepare, 0)

    def advance(i, state):
        places = [pl.ds(i * UNROLL + j, seqs, stride=length) for j in range(UNROLL)]
        decays = [decay_s[at, :] for at in places]
        drives = [drive_s[at, :] for at in places]
        for at, decay, drive in zip(places, decays, drives):
            state = decay * state + drive
            states_ref[at, :] = state
        return state

    lax.fori_loop(0, length // UNROLL, advance, jnp.zeros((seqs, LANES), jnp.float32))

    def finish(i, carry):
        at = pl.ds(pl.multiple_of(i * CHUNK, CHUNK), CHUNK)
        value, _ = gelu_pair(gate_ref[at, :])
        mixed_ref[at, :] = (states_ref[at, :] * value).astype(jnp.bfloat16)
        return carry

    lax.fori_loop(0, rows // CHUNK, finish, 0)


def lru_backward_kernel(
    seqs,
    conv_ref,
    rate_ref,
    input_ref,
    gate_ref,
    soft_ref,
    states_ref,
    grad_ref,
    d_conv_ref,
    d_rate_ref,
    d_input_ref,
    d_gate_ref,
    sums_ref,
    decay_s,
    flow_s,
    total_s,
    gate_s,
    drive_s,
    input_s,
    scale_s,
):
    rows = conv_ref.shape[0]
    length = rows // seqs
    soft = soft_ref[0:1, :]

    def prepare(i, carry):
        at = pl.ds(pl.multiple_of(i * CHUNK, CHUNK), CHUNK)
        value, slope = gelu_pair(gate_ref[at, :])
        grad = grad_ref[at, :]
        d_gate_ref[at, :] = (grad * states_ref[at, :] * slope).astype(jnp.bfloat16)
        flow_s[at, :] = grad * value
        conv = conv_ref[at, :].astype(jnp.float32)
        rate_gate, input_gate, decay_now, square, inverse = lru_terms(rate_ref[at, :], input_ref[at, :], soft)
        drive = square * inverse * input_gate
        decay_s[at, :] = decay_now
        gate_s[at, :] = rate_gate
        drive_s[at, :] = drive
        input_s[at, :] = drive * conv * (1.0 - input_gate)
        scale_s[at, :] = input_gate * conv * decay_now * inverse
        return carry

    lax.fori_loop(0, rows // CHUNK, prepare, 0)

    def retreat(i, carry):
        flow, decay = carry
        places = [pl.ds(length - 1 - (i * UNROLL + j), seqs, stride=length) for j in range(UNROLL)]
        flows = [flow_s[at, :] for at in places]
        decays = [decay_s[at, :] for at in places]
        for at, here, later in zip(places, flows, [decay] + decays[:-1]):
            flow = here + later * flow
            total_s[at, :] = flow
        return flow, decays[-1]

    nothing = jnp.zeros((seqs, LANES), jnp.float32)
    lax.fori_loop(0, length // UNROLL, retreat, (nothing, nothing))

    first_row = lax.broadcasted_iota(jnp.int32, (CHUNK, LANES), 0) == 0

    def finish(i, carry):
        rate_sum, input_sum, soft_sum, last = carry
        at = pl.ds(pl.multiple_of(i * CHUNK, CHUNK), CHUNK)
        states = states_ref[at, :]
        last = jnp.where(lax.rem(i, length // CHUNK) == 0, jnp.zeros_like(last), last)
        before = jnp.where(first_row, last, pltpu.roll(states, 1, 0))
        flow = total_s[at, :]
        rate_gate = gate_s[at, :]
        d_log = flow * decay_s[at, :] * (before - scale_s[at, :])
        d_soft = d_log * rate_gate * (-RATE_SCALE)
        d_rate = d_soft * soft * (1.0 - rate_gate)
        d_input = flow * input_s[at, :]
        d_conv_ref[at, :] = flow * drive_s[at, :]
        d_rate_ref[at, :] = d_rate.astype(jnp.bfloat16)
        d_input_ref[at, :] = d_input.astype(jnp.bfloat16)

        def fold(total, part):
            for k in range(CHUNK // 8):
                total = total + part[k * 8 : (k + 1) * 8, :]
            return total

        return fold(rate_sum, d_rate), fold(input_sum, d_input), fold(soft_sum, d_soft), states[CHUNK - 1 :, :]

    blank = jnp.zeros((8, LANES), jnp.float32)
    sums = lax.fori_loop(0, rows // CHUNK, finish, (blank, blank, blank, jnp.zeros((1, LANES), jnp.float32)))
    for k in range(3):
        sums_ref[k * 8 : (k + 1) * 8, :] = sums[k]


def lru_forward(seqs, conv, rate_pre, input_pre, gate_pre, soft):
    rows, channels = conv.shape
    block = pl.BlockSpec((rows, LANES), lambda i: (0, i))
    return pl.pallas_call(
        functools.partial(lru_forward_kernel, seqs),
        grid=(pl.cdiv(channels, LANES),),
        out_shape=(
            jax.ShapeDtypeStruct((rows, channels), jnp.float32),
            jax.ShapeDtypeStruct((rows, channels), jnp.bfloat16),
        ),
        in_specs=[block, block, block, block, pl.BlockSpec((8, LANES), lambda i: (0, i))],
        out_specs=(block, block),
        scratch_shapes=[pltpu.VMEM((rows, LANES), jnp.float32)] * 2,
        compiler_params=pltpu.CompilerParams(vmem_limit_bytes=48 * 2**20),
        cost_estimate=pl.CostEstimate(flops=200000 * rows * channels // 10, bytes_accessed=20 * rows * channels, transcendentals=8 * rows * channels),
        name="lru_forward",
    )(conv, rate_pre, input_pre, gate_pre, soft)


def lru_backward(seqs, conv, rate_pre, input_pre, gate_pre, soft, states, grads):
    rows, channels = conv.shape
    block = pl.BlockSpec((rows, LANES), lambda i: (0, i))
    return pl.pallas_call(
        functools.partial(lru_backward_kernel, seqs),
        grid=(pl.cdiv(channels, LANES),),
        out_shape=(
            jax.ShapeDtypeStruct((rows, channels), jnp.float32),
            jax.ShapeDtypeStruct((rows, channels), jnp.bfloat16),
            jax.ShapeDtypeStruct((rows, channels), jnp.bfloat16),
            jax.ShapeDtypeStruct((rows, channels), jnp.bfloat16),
            jax.ShapeDtypeStruct((24, channels), jnp.float32),
        ),
        in_specs=[block, block, block, block, pl.BlockSpec((8, LANES), lambda i: (0, i)), block, block],
        out_specs=(block, block, block, block, pl.BlockSpec((24, LANES), lambda i: (0, i))),
        scratch_shapes=[pltpu.VMEM((rows, LANES), jnp.float32)] * 7,
        compiler_params=pltpu.CompilerParams(vmem_limit_bytes=48 * 2**20),
        cost_estimate=pl.CostEstimate(flops=200000 * rows * channels // 10, bytes_accessed=20 * rows * channels, transcendentals=16 * rows * channels),
        name="lru_backward",
    )(conv, rate_pre, input_pre, gate_pre, soft, states, grads)


CONSTANT = pl.Buffered(1)
VMEM_BYTES = 56 * 2**20


def column_block(columns, most):
    return max(w for w in range(LANES, most + 1, LANES) if columns % w == 0)


def mlp_kernel(slots, *refs):
    parts, refs = refs[: slots + 1], refs[slots + 1 :]
    low_ref, gate_ref, up_ref, down_ref, product_ref, d_gate_ref, d_up_ref, normed_ref, w_s = refs
    groups, rows = gate_ref.shape[1], gate_ref.shape[2]
    stride = gate_ref.shape[0] * rows

    @pl.when(pl.program_id(0) == 0)
    def _():
        start = 0
        for part in parts:
            normed_ref[start : start + part.shape[0], :] = part[...]
            start += part.shape[0]

    for c in range(groups):
        for k in range(gate_ref.shape[0]):
            at = pl.ds(c * stride + k * rows, rows)
            w_s[0, at, :] = gate_ref[k, c]
            w_s[1, at, :] = up_ref[k, c]
    length = low_ref.shape[0] // slots

    for i in range(slots):
        at = pl.ds(i * length, length)
        here = normed_ref[at, :]
        gate = jnp.dot(here, w_s[0], preferred_element_type=jnp.float32)
        up = jnp.dot(here, w_s[1], preferred_element_type=jnp.float32)
        grad = matmul_nt(low_ref[at, :], down_ref[...])
        value, slope = gelu_pair(gate)
        product_ref[at, :] = (value * up).astype(jnp.bfloat16)
        d_gate_ref[at, :] = (grad * up * slope).astype(jnp.bfloat16)
        d_up_ref[at, :] = (grad * value).astype(jnp.bfloat16)


def mlp_both(parts, low_res, weights, w_down):
    tokens, width = low_res.shape
    hidden = w_down.shape[0]
    block = column_block(hidden, 256)
    steps = hidden // block
    lead = weights.shape[:3]
    return pl.pallas_call(
        functools.partial(mlp_kernel, PLANE),
        grid=(steps,),
        out_shape=(jax.ShapeDtypeStruct((tokens, hidden), jnp.bfloat16),) * 3
        + (jax.ShapeDtypeStruct((tokens, width), jnp.bfloat16),),
        in_specs=[pl.BlockSpec(p.shape, lambda j: (0, 0), pipeline_mode=CONSTANT) for p in parts]
        + [
            pl.BlockSpec((tokens, width), lambda j: (0, 0), pipeline_mode=CONSTANT),
            pl.BlockSpec(lead + (block,), lambda j: (0, 0, 0, j)),
            pl.BlockSpec(lead + (block,), lambda j: (0, 0, 0, j + steps)),
            pl.BlockSpec((block, width), lambda j: (j, 0)),
        ],
        out_specs=(pl.BlockSpec((tokens, block), lambda j: (0, j)),) * 3
        + (pl.BlockSpec((tokens, width), lambda j: (0, 0)),),
        scratch_shapes=[pltpu.VMEM((2, width, block), jnp.bfloat16)],
        compiler_params=pltpu.CompilerParams(vmem_limit_bytes=VMEM_BYTES),
        cost_estimate=pl.CostEstimate(
            flops=6 * tokens * width * hidden, bytes_accessed=2 * (3 * tokens * width + 3 * width * hidden), transcendentals=tokens * hidden
        ),
        name="mlp_both",
    )(*parts, low_res, weights, weights, w_down)


def mixed_grad_kernel(*refs):
    parts, w_ref, grad_ref, whole_ref = refs[:-3], refs[-3], refs[-2], refs[-1]
    start = 0
    weight = w_ref[...].reshape(-1, w_ref.shape[-1])
    for part in parts:
        at = pl.ds(start, part.shape[0])
        here = part[...]
        whole_ref[at, :] = here
        grad_ref[at, :] = matmul_nt(here, weight)
        start += part.shape[0]


def mixed_grad(parts, weight):
    weight, rows = weight
    width = parts[0].shape[1]
    tokens = sum(p.shape[0] for p in parts)
    inner = weight.shape[0] * rows
    return pl.pallas_call(
        mixed_grad_kernel,
        grid=(1,),
        out_shape=(jax.ShapeDtypeStruct((tokens, inner), jnp.float32), jax.ShapeDtypeStruct((tokens, width), jnp.bfloat16)),
        in_specs=[pl.BlockSpec(p.shape, lambda j: (0, 0)) for p in parts]
        + [pl.BlockSpec((weight.shape[0], rows, width), lambda j: (0, 0, 0))],
        out_specs=(pl.BlockSpec((tokens, inner), lambda j: (0, 0)), pl.BlockSpec((tokens, width), lambda j: (0, 0))),
        compiler_params=pltpu.CompilerParams(vmem_limit_bytes=VMEM_BYTES),
        cost_estimate=pl.CostEstimate(
            flops=2 * tokens * inner * width, bytes_accessed=4 * tokens * (width + inner) + 2 * inner * width, transcendentals=0
        ),
        name="mixed_grad",
    )(*parts, weight)


def store_parts(refs, length, part, value):
    value = value.astype(jnp.bfloat16)
    if part == 0:
        refs[0][...] = value[: length // 2]
        refs[1][...] = value[length // 2 :]
    else:
        refs[part + 1][...] = value


def store_all(refs, total):
    length = refs[-1].shape[0]
    for part in range(PLANE):
        store_parts(refs, length, part, total[part * length : (part + 1) * length])


def back_kernel(pieces, *refs):
    grads, w_ref, outs = refs[:pieces], refs[pieces], refs[pieces + 1 :]
    shares, _, rows, _ = w_ref.shape
    total = None
    start = 0
    for grads_ref in grads:
        cut = grads_ref.shape[1]
        weight = w_ref[:, 0, :, start : start + cut].reshape(shares * rows, cut)
        term = matmul_nt(grads_ref[...], weight)
        total = term if total is None else total + term
        start += cut
    store_all(outs, total)


def parts_out(length, width, block):
    heights = (length // 2, length // 2, length, length, length)
    return (
        tuple(jax.ShapeDtypeStruct((h, width), jnp.bfloat16) for h in heights),
        tuple(pl.BlockSpec((h, block), lambda j: (0, j)) for h in heights),
    )


def back_parts(grads, weights):
    tokens = grads[0].shape[0]
    inner = sum(g.shape[1] for g in grads)
    shares, groups, rows, columns = weights.shape
    block = shares * rows
    shapes, specs = parts_out(tokens // PLANE, groups * block, block)
    return pl.pallas_call(
        functools.partial(back_kernel, len(grads)),
        grid=(groups,),
        out_shape=shapes,
        in_specs=[pl.BlockSpec(g.shape, lambda j: (0, 0), pipeline_mode=CONSTANT) for g in grads]
        + [pl.BlockSpec((shares, 1, rows, columns), lambda j: (0, j, 0, 0))],
        out_specs=specs,
        compiler_params=pltpu.CompilerParams(vmem_limit_bytes=VMEM_BYTES),
        cost_estimate=pl.CostEstimate(
            flops=2 * tokens * inner * groups * block,
            bytes_accessed=2 * (tokens * inner + groups * block * (columns + tokens)),
            transcendentals=0,
        ),
        name="back_parts",
    )(*grads, weights)


def out_kernel(values_ref, w_ref, *refs):
    weight = w_ref[...].reshape(-1, w_ref.shape[-1])
    store_all(refs, jnp.dot(values_ref[...], weight, preferred_element_type=jnp.float32))


def out_parts(values, weight):
    weight, rows = weight
    tokens, inner = values.shape
    shares, _, width = weight.shape
    block = column_block(width, 512)
    shapes, specs = parts_out(tokens // PLANE, width, block)
    return pl.pallas_call(
        out_kernel,
        grid=(width // block,),
        out_shape=shapes,
        in_specs=[
            pl.BlockSpec((tokens, inner), lambda j: (0, 0), pipeline_mode=CONSTANT),
            pl.BlockSpec((shares, rows, block), lambda j: (0, 0, j)),
        ],
        out_specs=specs,
        compiler_params=pltpu.CompilerParams(vmem_limit_bytes=VMEM_BYTES),
        cost_estimate=pl.CostEstimate(
            flops=2 * tokens * inner * width, bytes_accessed=2 * (tokens * inner + inner * width + tokens * width), transcendentals=0
        ),
        name="out_parts",
    )(values, weight)


def weight_grad_kernel(rows, me_ref, left_ref, right_ref, mine_ref, *refs):
    theirs, left_s = refs[:-1], refs[-1]

    @pl.when(pl.program_id(1) == 0)
    def _():
        left_s[...] = left_ref[...].T

    narrow, groups, _, block = mine_ref.shape
    height = narrow * rows
    total = jnp.dot(left_s[...], right_ref[0], preferred_element_type=jnp.float32).astype(jnp.bfloat16)

    def store(mine, other):
        for g in range(groups):
            start = (g * 2 + mine) * height
            mine_ref[:, g] = total[start : start + height].reshape(narrow, rows, block)
            start = (g * 2 + other) * height
            for k, ref in enumerate(theirs):
                ref[0, g] = total[start + k * rows : start + (k + 1) * rows]

    @pl.when(me_ref[0] == 0)
    def _():
        store(0, 1)

    @pl.when(me_ref[0] != 0)
    def _():
        store(1, 0)


def weight_grad(me, left, right, narrow, groups, rows):
    tokens = left.shape[0]
    pieces, _, piece = right.shape
    block = column_block(piece, 768)
    steps = piece // block
    together = 2 if groups % 2 == 0 else 1
    height = together * 2 * narrow * rows
    columns = pieces * piece
    return pl.pallas_call(
        functools.partial(weight_grad_kernel, rows),
        grid_spec=pltpu.PrefetchScalarGridSpec(
            num_scalar_prefetch=1,
            grid=(groups // together, pieces * steps),
            in_specs=[
                pl.BlockSpec((tokens, height), lambda g, j, me_ref: (0, g)),
                pl.BlockSpec((1, tokens, block), lambda g, j, me_ref: (j // steps, 0, j % steps)),
            ],
            out_specs=(pl.BlockSpec((narrow, together, rows, block), lambda g, j, me_ref: (0, g, 0, j)),)
            + (pl.BlockSpec((1, together, rows, block), lambda g, j, me_ref: (0, g, 0, j)),) * narrow,
            scratch_shapes=[pltpu.VMEM((height, tokens), jnp.bfloat16)],
        ),
        out_shape=(jax.ShapeDtypeStruct((narrow, groups, rows, columns), jnp.bfloat16),)
        + (jax.ShapeDtypeStruct((1, groups, rows, columns), jnp.bfloat16),) * narrow,
        compiler_params=pltpu.CompilerParams(vmem_limit_bytes=VMEM_BYTES),
        cost_estimate=pl.CostEstimate(
            flops=2 * tokens * left.shape[1] * columns,
            bytes_accessed=2 * (left.size + groups // together * right.size + left.shape[1] * columns),
            transcendentals=0,
        ),
        name="weight_grad",
    )(me, left, right)


def add_pieces_kernel(mine_ref, *refs):
    for k, ref in enumerate(refs[:-1]):
        refs[-1][k] = (mine_ref[k].astype(jnp.float32) + ref[0].astype(jnp.float32)).astype(jnp.bfloat16)


def add_pieces(mine, others):
    narrow, groups, rows, columns = mine.shape
    block = column_block(columns, 1024)
    place = pl.BlockSpec((narrow, 1, rows, block), lambda g, j: (0, g, 0, j))
    return pl.pallas_call(
        add_pieces_kernel,
        grid=(groups, columns // block),
        out_shape=jax.ShapeDtypeStruct(mine.shape, jnp.bfloat16),
        in_specs=[place] + [pl.BlockSpec((1, 1, rows, block), lambda g, j: (0, g, 0, j))] * narrow,
        out_specs=place,
        compiler_params=pltpu.CompilerParams(vmem_limit_bytes=VMEM_BYTES),
        cost_estimate=pl.CostEstimate(flops=mine.size, bytes_accessed=6 * mine.size, transcendentals=0),
        name="add_pieces",
    )(mine, *others)


def block_diagonal(table):
    size, channels = table.shape
    tall = jnp.concatenate([table] * (channels // size), axis=0)
    row_head = lax.broadcasted_iota(jnp.int32, tall.shape, 0) // size
    column_head = lax.broadcasted_iota(jnp.int32, tall.shape, 1) // size
    return jnp.where(row_head == column_head, tall, jnp.zeros_like(tall))


def diagonal_blocks(square, size):
    channels = square.shape[0]
    cube = square.reshape(channels // size, size, channels)
    row_head = lax.broadcasted_iota(jnp.int32, cube.shape, 0)
    column_head = lax.broadcasted_iota(jnp.int32, cube.shape, 2) // size
    return jnp.sum(jnp.where(row_head == column_head, cube, jnp.zeros_like(cube)), axis=0)


def shift_rows(values, seqs, by):
    rows, channels = values.shape
    length = rows // seqs
    cube = values.reshape(seqs, length, channels)
    if by > 0:
        cube = jnp.pad(cube, ((0, 0), (by, 0), (0, 0)))[:, :length]
    elif by < 0:
        cube = jnp.pad(cube, ((0, 0), (0, -by), (0, 0)))[:, -by:]
    return cube.reshape(rows, channels)


def make_block(rest_size, narrow_size):
    bf16, f32 = jnp.bfloat16, jnp.float32
    spread = ("rest", "narrow")

    def swap(values, mask):
        return lax.ppermute(values, "wide", [(i, i ^ mask) for i in range(PLANE)])

    def gather_parts(shard):
        half = shard.shape[0] // 2
        one, two = swap(shard, 1), swap(shard, 2)
        return [swap(one[:half], 2), swap(two[half:], 1), one, two, shard]

    def gather_rows(shard):
        return jnp.concatenate(gather_parts(shard), axis=0)

    def scatter_start(parts):
        far_low, far_high, one, two, own = parts
        half = own.shape[0] // 2
        via_one, via_two = swap(far_low, 1), swap(far_high, 2)
        one = jnp.concatenate([one[:half], (one[half:].astype(f32) + via_two.astype(f32)).astype(bf16)], axis=0)
        two = jnp.concatenate([(two[:half].astype(f32) + via_one.astype(f32)).astype(bf16), two[half:]], axis=0)
        return one, two, own

    def scatter_finish(one, two, own):
        return own.astype(f32) + swap(one, 1).astype(f32) + swap(two, 2).astype(f32)

    def scatter_rows(parts):
        return scatter_finish(*scatter_start(parts))

    def cut_columns(blocks):
        return lax.all_to_all(blocks, "wide", 0, 0, tiled=False)

    def gather_spread(part):
        whole = lax.all_gather(part.reshape(-1, part.shape[-1]), spread, axis=0, tiled=True)
        return whole.reshape((rest_size * narrow_size,) + part.shape)

    def grad_shares(left, right, rows, groups):
        if rest_size != 2:
            grad = matmul_tn(left, right.swapaxes(0, 1).reshape(right.shape[1], -1)).astype(bf16)
            cut = grad.reshape(groups, rest_size, narrow_size, rows, -1).transpose(1, 2, 0, 3, 4)
            return grad, lambda *waits: lax.psum_scatter(after(cut, *waits), "rest", scatter_dimension=0, tiled=False)
        me = lax.axis_index("rest").astype(jnp.int32)[None]
        mine, *theirs = weight_grad(me, left, right, narrow_size, groups, rows)
        others = [lax.ppermute(piece, "rest", [(0, 1), (1, 0)]) for piece in theirs]
        return mine, lambda *waits: add_pieces(after(mine, *waits), others)

    def sum_rest(values):
        if rest_size != 2:
            return lax.psum_scatter(values, "rest", scatter_dimension=0, tiled=False)
        me = lax.axis_index("rest")
        theirs = lax.dynamic_index_in_dim(values, 1 - me, 0, keepdims=False)
        mine = lax.dynamic_index_in_dim(values, me, 0, keepdims=False)
        other = lax.ppermute(theirs, "rest", [(0, 1), (1, 0)])
        return (mine.astype(f32) + other.astype(f32)).astype(values.dtype)

    def sum_narrow(values):
        return lax.psum_scatter(values.reshape(-1, values.shape[-1]), "narrow", scatter_dimension=0, tiled=True)

    def columns_home(mine, rows):
        return lax.all_to_all(mine.reshape(PLANE, rows, -1), "wide", 0, 1, tiled=False)

    def sum_narrow_direct(values):
        me = lax.axis_index("narrow")
        total = lax.dynamic_index_in_dim(values, me, 0, keepdims=False).astype(f32)
        for step in range(1, narrow_size):
            part = lax.dynamic_index_in_dim(values, lax.rem(me + step, narrow_size), 0, keepdims=False)
            pairs = [(i, (i + step) % narrow_size) for i in range(narrow_size)]
            total = total + lax.ppermute(part, "narrow", pairs).astype(f32)
        return total

    def to_all(values, axes, count):
        return lax.all_to_all(jnp.broadcast_to(values[None], (count,) + values.shape), axes, 0, 0, tiled=False)

    def rows_cut(grad):
        return grad.reshape(rest_size, narrow_size, -1, grad.shape[-1])

    def fence(*values):
        return lax.optimization_barrier(values)

    def after(values, *others):
        return lax.optimization_barrier((values,) + others)[0]

    def on_device(
        tokens,
        lengths,
        cotangent,
        norm_gain1,
        gate_in,
        x_in,
        conv_kernel,
        conv_bias,
        rate_weight,
        rate_bias,
        input_weight,
        input_bias,
        decay_param,
        out_proj,
        norm_gain2,
        mlp_gate,
        mlp_up,
        mlp_down,
    ):
        row_count, width = tokens.shape
        head = rate_weight.shape[0]
        rows = gate_in.shape[0]
        taps = conv_kernel.shape[0]
        seqs = PLANE
        channels = gate_in.shape[1] // PLANE
        hidden = mlp_gate.shape[1] // PLANE
        live = (jnp.arange(row_count, dtype=jnp.int32) < lengths[0]).astype(f32)[:, None]

        def by_plane(*weights):
            cut = [w.reshape(rows, PLANE, -1).swapaxes(0, 1) for w in weights]
            return jnp.concatenate(cut, axis=2)

        table = jnp.concatenate(
            [
                conv_kernel,
                conv_bias[None],
                rate_weight,
                rate_bias[None],
                input_weight,
                input_bias[None],
                decay_param[None],
            ],
            axis=0,
        )
        cuts = [taps, 1, head, 1, head, 1, 1]
        places = [sum(cuts[:i]) for i in range(len(cuts) + 1)]
        columns = 2 * channels
        shares = rest_size * narrow_size
        part_rec = cut_columns(by_plane(gate_in, x_in)).reshape(PLANE, rows, columns)
        w_rec = gather_spread(part_rec)
        tokens_all = gather_rows(after(tokens, part_rec))
        table = jnp.pad(table, ((0, -places[-1] % LANES), (0, 0))).T
        table = to_all(after(table, part_rec), spread, shares)
        gains = to_all(after(jnp.stack([norm_gain1, norm_gain2]), table), ("wide",) + spread, PLANE * shares)
        cut_mlp = by_plane(mlp_gate, mlp_up)
        w_rec, tokens_all, table, gains, cut_mlp = fence(w_rec, tokens_all, table, gains, cut_mlp)

        out_and_down = lax.all_gather(
            after(jnp.concatenate([out_proj, mlp_down], axis=0), w_rec), spread, axis=0, tiled=True
        ).reshape(rest_size * narrow_size, -1, width)
        low_res = (cotangent.astype(f32) * live).astype(bf16)
        low_res_parts = gather_parts(after(low_res, w_rec))
        low_res_all = jnp.concatenate(low_res_parts, axis=0)
        gains = gains.swapaxes(0, 1).reshape(2, width).astype(f32)
        gain_one, gain_two = gains[0:1], gains[1:2]
        table = table.reshape(channels, -1).T
        w_flat = w_rec.swapaxes(0, 1).reshape(width, columns)
        tokens_f = tokens_all.astype(f32)
        inverse_all = rms_inverse(tokens_f)
        normed1 = (tokens_f * inverse_all * gain_one).astype(bf16)
        gate_pre = matmul_low(normed1, w_flat[:, :channels])
        branch_pre = matmul_low(normed1, w_flat[:, channels:])
        kernel, shift, rate_table, b_rate, input_table, b_input, decay = (
            table[places[i] : places[i + 1]] for i in range(len(cuts))
        )
        kernel_f, shift_f, b_rate, b_input, decay_f = (v.astype(f32) for v in (kernel, shift, b_rate, b_input, decay))
        w_rate = block_diagonal(rate_table)
        w_input = block_diagonal(input_table)
        soft = softplus_minus(decay_f)
        soft_rows = jnp.broadcast_to(soft, (8, soft.shape[1]))
        part_mlp = cut_columns(after(cut_mlp, *low_res_parts))

        conv = shift_f
        for tap in range(taps):
            conv = conv + kernel_f[tap] * shift_rows(branch_pre, seqs, taps - 1 - tap)
        conv = conv.astype(bf16)
        rate_pre = matmul_low(conv, w_rate) + b_rate
        input_pre = matmul_low(conv, w_input) + b_input
        states, mixed = lru_forward(seqs, conv, rate_pre, input_pre, gate_pre, soft_rows)
        mixed, part_mlp, out_and_down = fence(mixed, part_mlp, out_and_down)
        out_rows = out_proj.shape[0]
        if out_rows % 16 == 0:
            w_out = (out_and_down, out_rows)
        else:
            w_out = (out_and_down[:, :out_rows].reshape(1, -1, width), shares * out_rows)
        w_down = out_and_down[:, out_rows:].reshape(-1, width)

        w_mlp = gather_spread(part_mlp)
        merged = tokens.astype(f32) + scatter_rows(out_parts(mixed, w_out))
        inverse2 = rms_inverse(merged)
        normed2 = (merged * inverse2 * gain_two).astype(bf16)
        *normed2_parts, w_mlp = fence(*gather_parts(normed2), w_mlp)

        product, d_gate_two, d_up_two, normed2_all = mlp_both(normed2_parts, low_res_all, w_mlp, w_down)
        first, finish_down = grad_shares(product, low_res_all[None], mlp_down.shape[0], 1)
        parts2 = back_parts((after(d_gate_two, first), d_up_two), w_mlp)
        grad_down = finish_down(parts2[0])
        down_out = sum_narrow(grad_down)
        d_normed2 = scatter_rows(parts2)
        _, finish = grad_shares(normed2_all, after(d_gate_two, parts2)[None], rows, PLANE)
        grad_mgate = finish()
        d_normed2, grad_mgate, down_out = fence(d_normed2, grad_mgate, down_out)

        mgate_sum = sum_narrow(grad_mgate)
        grad_gain2 = jnp.sum(d_normed2 * merged * inverse2, axis=0)
        d_merged = low_res.astype(f32) + rms_back(merged, inverse2, gain_two, d_normed2)
        low_merged = d_merged.astype(bf16)
        low_merged_parts = gather_parts(low_merged)
        _, finish = grad_shares(normed2_all, after(d_up_two, low_merged)[None], rows, PLANE)
        grad_mup = finish(*low_merged_parts[2:4])
        parts_result = out_parts(after(product, *low_merged_parts[2:4]), (w_down[None], w_down.shape[0]))
        *low_merged_parts, parts_result, mgate_sum, grad_mup = fence(*low_merged_parts, parts_result, mgate_sum, grad_mup)
        d_mixed, low_merged_all = mixed_grad(low_merged_parts, w_out)
        mup_sum = sum_narrow(grad_mup)
        sums_result = scatter_start(parts_result)
        d_mixed, *sums_result = fence(d_mixed, *sums_result)
        d_conv_lru, d_rate, d_input, d_gate, sums = lru_backward(
            seqs, conv, rate_pre, input_pre, gate_pre, soft_rows, states, d_mixed
        )
        mgate_out = columns_home(after(mgate_sum, d_conv_lru), rows)
        sums = sums.reshape(3, 8, -1).sum(axis=1)
        grad_decay = sums[2] * (-1.0 / (1.0 + jnp.exp(decay_f[0])))
        d_conv = d_conv_lru + matmul_nt(d_rate, w_rate) + matmul_nt(d_input, w_input)
        result = merged + scatter_finish(*sums_result)
        d_branch = jnp.zeros_like(d_conv)
        grad_taps = []
        for tap in range(taps):
            moved = shift_rows(d_conv, seqs, tap - (taps - 1))
            d_branch = d_branch + kernel_f[tap] * moved
            grad_taps.append(jnp.sum(branch_pre * moved, axis=0))
        low_branch = d_branch.astype(bf16)
        d_rec = jnp.stack([d_gate, low_branch])

        d_rec, mgate_out, result = fence(d_rec, mgate_out, result)
        _, finish = grad_shares(normed1, d_rec, rows, PLANE)
        grad_rec = finish(mup_sum)
        rec_sum = sum_narrow(grad_rec)
        mup_out = columns_home(after(mup_sum, d_rec), rows)
        parts1 = back_parts((after(d_gate, grad_rec, mup_out), low_branch), w_rec)
        one, two, own = scatter_start(parts1)
        d_normed1 = scatter_finish(one, two, own)
        grad_out = matmul_tn(mixed, after(low_merged_all, parts1)).astype(bf16)
        normed_f = after(tokens_all, grad_rec).astype(f32) * inverse_all
        grad_gain1 = jnp.zeros((width,), f32)
        start = 0
        for part in parts1:
            grad_gain1 = grad_gain1 + jnp.sum(part.astype(f32) * normed_f[start : start + part.shape[0]], axis=0)
            start += part.shape[0]
        gain_grads = jnp.stack([grad_gain1, grad_gain2]).reshape(2, -1, rows).swapaxes(0, 1)
        grad_rate_weight = diagonal_blocks(matmul_tn(conv, after(d_rate, grad_rec)), head)
        grad_input_weight = diagonal_blocks(matmul_tn(conv, after(d_input, grad_rec)), head)
        table_grad = jnp.concatenate(
            [
                jnp.stack(grad_taps),
                jnp.sum(d_conv, axis=0)[None],
                grad_rate_weight,
                sums[0:1],
                grad_input_weight,
                sums[1:2],
                grad_decay[None],
            ],
            axis=0,
        )
        table_grad = jnp.pad(table_grad, ((0, -places[-1] % LANES), (0, 0))).T.astype(bf16)
        last = sum_rest(rows_cut(jnp.concatenate([grad_out, table_grad], axis=1)))
        rec_sum, d_normed1 = fence(rec_sum, d_normed1)
        last = sum_narrow(after(last, rec_sum)).astype(f32)
        out_out, table_out = last[:, :width], last[:, width:].T

        rec_out = columns_home(rec_sum, rows)
        gain_out = lax.all_to_all(after(gain_grads, rec_out), ("wide",) + spread, 0, 0, tiled=False).sum(axis=0)
        block_out = (result * live).astype(bf16)
        own = tokens.astype(f32)
        input_grad = d_merged + rms_back(own, rms_inverse(own), gain_one, d_normed1)

        kernel_out, shift_out, rate_out, rate_bias_out, input_out, input_bias_out, decay_out = (
            table_out[places[i] : places[i + 1]] for i in range(len(cuts))
        )
        def whole_rows(cut):
            return cut.reshape(rows, -1).astype(f32)

        return (
            block_out,
            input_grad,
            gain_out[0],
            whole_rows(rec_out[:, :, :channels]),
            whole_rows(rec_out[:, :, channels:]),
            kernel_out,
            shift_out[0],
            rate_out,
            rate_bias_out[0],
            input_out,
            input_bias_out[0],
            decay_out[0],
            out_out,
            gain_out[1],
            whole_rows(mgate_out),
            whole_rows(mup_out),
            down_out.astype(f32),
        )

    return on_device


def solution(mesh):
    wide, narrow = mesh.shape["wide"], mesh.shape["narrow"]
    mesh = Mesh(mesh.devices.reshape(PLANE, wide // PLANE, narrow), ("wide", "rest", "narrow"))
    every = mesh.axis_names
    rows, columns, vector = P(every, None), P(None, every), P(every)
    return jax.shard_map(
        make_block(wide // PLANE, narrow),
        mesh=mesh,
        in_specs=(
            rows,
            vector,
            rows,
            vector,
            rows,
            rows,
            columns,
            vector,
            columns,
            vector,
            columns,
            vector,
            vector,
            rows,
            vector,
            rows,
            rows,
            rows,
        ),
        out_specs=(
            rows,
            rows,
            vector,
            rows,
            rows,
            columns,
            vector,
            columns,
            vector,
            columns,
            vector,
            vector,
            rows,
            vector,
            rows,
            rows,
            rows,
        ),
        check_vma=False,
    )
```

```python
import functools

import jax
import jax.numpy as jnp
from jax import lax
from jax.experimental import pallas as pl
from jax.experimental.pallas import tpu as pltpu
from jax.sharding import Mesh
from jax.sharding import PartitionSpec as P

EPSILON = 1e-06
RATE_SCALE = 8.0
GELU_ROOT = 0.7978845608028654
GELU_CUBE = 0.044715
LANES = 128
PLANE = 4


def matmul_low(left, right):
    return jnp.dot(left, right, preferred_element_type=jnp.float32)


def matmul_nt(left, right):
    return lax.dot_general(left, right, (((1,), (1,)), ((), ())), preferred_element_type=jnp.float32)


def matmul_tn(left, right):
    return lax.dot_general(left, right, (((0,), (0,)), ((), ())), preferred_element_type=jnp.float32)


def rms_inverse(values):
    return lax.rsqrt(jnp.mean(values * values, axis=-1, keepdims=True) + EPSILON)


def rms_back(values, inverse, gain, grads):
    scaled = grads * gain
    dots = jnp.mean(scaled * values, axis=-1, keepdims=True)
    return inverse * scaled - values * (inverse * inverse * inverse * dots)


def gelu_pair(values):
    square = values * values
    slope = jnp.tanh(GELU_ROOT * values * (1.0 + GELU_CUBE * square))
    half = 0.5 * (1.0 + slope)
    grad = half + 0.5 * values * (1.0 - slope * slope) * (GELU_ROOT * (1.0 + 3.0 * GELU_CUBE * square))
    return values * half, grad


def softplus_minus(values):
    return jnp.maximum(-values, 0.0) + jnp.log(1.0 + jnp.exp(-jnp.abs(values)))


def sigmoid(values):
    return 1.0 / (1.0 + jnp.exp(jnp.minimum(-values, 80.0)))


def lru_terms(rate_pre, input_pre, soft):
    rate_gate = sigmoid(rate_pre)
    input_gate = sigmoid(input_pre)
    log_decay = -RATE_SCALE * rate_gate * soft
    decay_now = jnp.exp(log_decay)
    twice = 2.0 * log_decay
    series = -twice * (1.0 + twice * 0.5 * (1.0 + twice * (1.0 / 3.0) * (1.0 + twice * 0.25)))
    square = jnp.maximum(jnp.where(twice > -0.0625, series, 1.0 - decay_now * decay_now), 1e-30)
    return rate_gate, input_gate, decay_now, square, lax.rsqrt(square)


CHUNK = 160
UNROLL = 16


def lru_forward_kernel(seqs, conv_ref, rate_ref, input_ref, gate_ref, soft_ref, states_ref, mixed_ref, decay_s, drive_s):
    rows = conv_ref.shape[0]
    length = rows // seqs
    soft = soft_ref[0:1, :]

    def prepare(i, carry):
        at = pl.ds(pl.multiple_of(i * CHUNK, CHUNK), CHUNK)
        conv = conv_ref[at, :].astype(jnp.float32)
        _, input_gate, decay_now, square, inverse = lru_terms(rate_ref[at, :], input_ref[at, :], soft)
        decay_s[at, :] = decay_now
        drive_s[at, :] = square * inverse * input_gate * conv
        return carry

    lax.fori_loop(0, rows // CHUNK, prepare, 0)

    def advance(i, state):
        places = [pl.ds(i * UNROLL + j, seqs, stride=length) for j in range(UNROLL)]
        decays = [decay_s[at, :] for at in places]
        drives = [drive_s[at, :] for at in places]
        for at, decay, drive in zip(places, decays, drives):
            state = decay * state + drive
            states_ref[at, :] = state
        return state

    lax.fori_loop(0, length // UNROLL, advance, jnp.zeros((seqs, LANES), jnp.float32))

    def finish(i, carry):
        at = pl.ds(pl.multiple_of(i * CHUNK, CHUNK), CHUNK)
        value, _ = gelu_pair(gate_ref[at, :])
        mixed_ref[at, :] = (states_ref[at, :] * value).astype(jnp.bfloat16)
        return carry

    lax.fori_loop(0, rows // CHUNK, finish, 0)


def lru_backward_kernel(
    seqs,
    conv_ref,
    rate_ref,
    input_ref,
    gate_ref,
    soft_ref,
    states_ref,
    grad_ref,
    d_conv_ref,
    d_rate_ref,
    d_input_ref,
    d_gate_ref,
    sums_ref,
    decay_s,
    flow_s,
    total_s,
    gate_s,
    drive_s,
    input_s,
    scale_s,
):
    rows = conv_ref.shape[0]
    length = rows // seqs
    soft = soft_ref[0:1, :]

    def prepare(i, carry):
        at = pl.ds(pl.multiple_of(i * CHUNK, CHUNK), CHUNK)
        value, slope = gelu_pair(gate_ref[at, :])
        grad = grad_ref[at, :]
        d_gate_ref[at, :] = (grad * states_ref[at, :] * slope).astype(jnp.bfloat16)
        flow_s[at, :] = grad * value
        conv = conv_ref[at, :].astype(jnp.float32)
        rate_gate, input_gate, decay_now, square, inverse = lru_terms(rate_ref[at, :], input_ref[at, :], soft)
        drive = square * inverse * input_gate
        decay_s[at, :] = decay_now
        gate_s[at, :] = rate_gate
        drive_s[at, :] = drive
        input_s[at, :] = drive * conv * (1.0 - input_gate)
        scale_s[at, :] = input_gate * conv * decay_now * inverse
        return carry

    lax.fori_loop(0, rows // CHUNK, prepare, 0)

    def retreat(i, carry):
        flow, decay = carry
        places = [pl.ds(length - 1 - (i * UNROLL + j), seqs, stride=length) for j in range(UNROLL)]
        flows = [flow_s[at, :] for at in places]
        decays = [decay_s[at, :] for at in places]
        for at, here, later in zip(places, flows, [decay] + decays[:-1]):
            flow = here + later * flow
            total_s[at, :] = flow
        return flow, decays[-1]

    nothing = jnp.zeros((seqs, LANES), jnp.float32)
    lax.fori_loop(0, length // UNROLL, retreat, (nothing, nothing))

    first_row = lax.broadcasted_iota(jnp.int32, (CHUNK, LANES), 0) == 0

    def finish(i, carry):
        rate_sum, input_sum, soft_sum, last = carry
        at = pl.ds(pl.multiple_of(i * CHUNK, CHUNK), CHUNK)
        states = states_ref[at, :]
        last = jnp.where(lax.rem(i, length // CHUNK) == 0, jnp.zeros_like(last), last)
        before = jnp.where(first_row, last, pltpu.roll(states, 1, 0))
        flow = total_s[at, :]
        rate_gate = gate_s[at, :]
        d_log = flow * decay_s[at, :] * (before - scale_s[at, :])
        d_soft = d_log * rate_gate * (-RATE_SCALE)
        d_rate = d_soft * soft * (1.0 - rate_gate)
        d_input = flow * input_s[at, :]
        d_conv_ref[at, :] = flow * drive_s[at, :]
        d_rate_ref[at, :] = d_rate.astype(jnp.bfloat16)
        d_input_ref[at, :] = d_input.astype(jnp.bfloat16)

        def fold(total, part):
            for k in range(CHUNK // 8):
                total = total + part[k * 8 : (k + 1) * 8, :]
            return total

        return fold(rate_sum, d_rate), fold(input_sum, d_input), fold(soft_sum, d_soft), states[CHUNK - 1 :, :]

    blank = jnp.zeros((8, LANES), jnp.float32)
    sums = lax.fori_loop(0, rows // CHUNK, finish, (blank, blank, blank, jnp.zeros((1, LANES), jnp.float32)))
    for k in range(3):
        sums_ref[k * 8 : (k + 1) * 8, :] = sums[k]


def lru_forward(seqs, conv, rate_pre, input_pre, gate_pre, soft):
    rows, channels = conv.shape
    block = pl.BlockSpec((rows, LANES), lambda i: (0, i))
    return pl.pallas_call(
        functools.partial(lru_forward_kernel, seqs),
        grid=(pl.cdiv(channels, LANES),),
        out_shape=(
            jax.ShapeDtypeStruct((rows, channels), jnp.float32),
            jax.ShapeDtypeStruct((rows, channels), jnp.bfloat16),
        ),
        in_specs=[block, block, block, block, pl.BlockSpec((8, LANES), lambda i: (0, i))],
        out_specs=(block, block),
        scratch_shapes=[pltpu.VMEM((rows, LANES), jnp.float32)] * 2,
        compiler_params=pltpu.CompilerParams(vmem_limit_bytes=48 * 2**20),
        cost_estimate=pl.CostEstimate(flops=200000 * rows * channels // 10, bytes_accessed=20 * rows * channels, transcendentals=8 * rows * channels),
        name="lru_forward",
    )(conv, rate_pre, input_pre, gate_pre, soft)


def lru_backward(seqs, conv, rate_pre, input_pre, gate_pre, soft, states, grads):
    rows, channels = conv.shape
    block = pl.BlockSpec((rows, LANES), lambda i: (0, i))
    return pl.pallas_call(
        functools.partial(lru_backward_kernel, seqs),
        grid=(pl.cdiv(channels, LANES),),
        out_shape=(
            jax.ShapeDtypeStruct((rows, channels), jnp.float32),
            jax.ShapeDtypeStruct((rows, channels), jnp.bfloat16),
            jax.ShapeDtypeStruct((rows, channels), jnp.bfloat16),
            jax.ShapeDtypeStruct((rows, channels), jnp.bfloat16),
            jax.ShapeDtypeStruct((24, channels), jnp.float32),
        ),
        in_specs=[block, block, block, block, pl.BlockSpec((8, LANES), lambda i: (0, i)), block, block],
        out_specs=(block, block, block, block, pl.BlockSpec((24, LANES), lambda i: (0, i))),
        scratch_shapes=[pltpu.VMEM((rows, LANES), jnp.float32)] * 7,
        compiler_params=pltpu.CompilerParams(vmem_limit_bytes=48 * 2**20),
        cost_estimate=pl.CostEstimate(flops=200000 * rows * channels // 10, bytes_accessed=20 * rows * channels, transcendentals=16 * rows * channels),
        name="lru_backward",
    )(conv, rate_pre, input_pre, gate_pre, soft, states, grads)


CONSTANT = pl.Buffered(1)
VMEM_BYTES = 56 * 2**20


def column_block(columns, most):
    return max(w for w in range(LANES, most + 1, LANES) if columns % w == 0)


def mlp_kernel(slots, *refs):
    parts, refs = refs[: slots + 1], refs[slots + 1 :]
    low_ref, gate_ref, up_ref, down_ref, product_ref, d_gate_ref, d_up_ref, normed_ref, w_s = refs
    groups, rows = gate_ref.shape[1], gate_ref.shape[2]
    stride = gate_ref.shape[0] * rows

    @pl.when(pl.program_id(0) == 0)
    def _():
        start = 0
        for part in parts:
            normed_ref[start : start + part.shape[0], :] = part[...]
            start += part.shape[0]

    for c in range(groups):
        for k in range(gate_ref.shape[0]):
            at = pl.ds(c * stride + k * rows, rows)
            w_s[0, at, :] = gate_ref[k, c]
            w_s[1, at, :] = up_ref[k, c]
    length = low_ref.shape[0] // slots

    for i in range(slots):
        at = pl.ds(i * length, length)
        here = normed_ref[at, :]
        gate = jnp.dot(here, w_s[0], preferred_element_type=jnp.float32)
        up = jnp.dot(here, w_s[1], preferred_element_type=jnp.float32)
        grad = matmul_nt(low_ref[at, :], down_ref[...])
        value, slope = gelu_pair(gate)
        product_ref[at, :] = (value * up).astype(jnp.bfloat16)
        d_gate_ref[at, :] = (grad * up * slope).astype(jnp.bfloat16)
        d_up_ref[at, :] = (grad * value).astype(jnp.bfloat16)


def mlp_both(parts, low_res, weights, w_down):
    tokens, width = low_res.shape
    hidden = w_down.shape[0]
    block = column_block(hidden, 256)
    steps = hidden // block
    lead = weights.shape[:3]
    return pl.pallas_call(
        functools.partial(mlp_kernel, PLANE),
        grid=(steps,),
        out_shape=(jax.ShapeDtypeStruct((tokens, hidden), jnp.bfloat16),) * 3
        + (jax.ShapeDtypeStruct((tokens, width), jnp.bfloat16),),
        in_specs=[pl.BlockSpec(p.shape, lambda j: (0, 0), pipeline_mode=CONSTANT) for p in parts]
        + [
            pl.BlockSpec((tokens, width), lambda j: (0, 0), pipeline_mode=CONSTANT),
            pl.BlockSpec(lead + (block,), lambda j: (0, 0, 0, j)),
            pl.BlockSpec(lead + (block,), lambda j: (0, 0, 0, j + steps)),
            pl.BlockSpec((block, width), lambda j: (j, 0)),
        ],
        out_specs=(pl.BlockSpec((tokens, block), lambda j: (0, j)),) * 3
        + (pl.BlockSpec((tokens, width), lambda j: (0, 0)),),
        scratch_shapes=[pltpu.VMEM((2, width, block), jnp.bfloat16)],
        compiler_params=pltpu.CompilerParams(vmem_limit_bytes=VMEM_BYTES),
        cost_estimate=pl.CostEstimate(
            flops=6 * tokens * width * hidden, bytes_accessed=2 * (3 * tokens * width + 3 * width * hidden), transcendentals=tokens * hidden
        ),
        name="mlp_both",
    )(*parts, low_res, weights, weights, w_down)


def mixed_grad_kernel(*refs):
    parts, w_ref, grad_ref, whole_ref = refs[:-3], refs[-3], refs[-2], refs[-1]
    start = 0
    weight = w_ref[...].reshape(-1, w_ref.shape[-1])
    for part in parts:
        at = pl.ds(start, part.shape[0])
        here = part[...]
        whole_ref[at, :] = here
        grad_ref[at, :] = matmul_nt(here, weight)
        start += part.shape[0]


def mixed_grad(parts, weight):
    weight, rows = weight
    width = parts[0].shape[1]
    tokens = sum(p.shape[0] for p in parts)
    inner = weight.shape[0] * rows
    return pl.pallas_call(
        mixed_grad_kernel,
        grid=(1,),
        out_shape=(jax.ShapeDtypeStruct((tokens, inner), jnp.float32), jax.ShapeDtypeStruct((tokens, width), jnp.bfloat16)),
        in_specs=[pl.BlockSpec(p.shape, lambda j: (0, 0)) for p in parts]
        + [pl.BlockSpec((weight.shape[0], rows, width), lambda j: (0, 0, 0))],
        out_specs=(pl.BlockSpec((tokens, inner), lambda j: (0, 0)), pl.BlockSpec((tokens, width), lambda j: (0, 0))),
        compiler_params=pltpu.CompilerParams(vmem_limit_bytes=VMEM_BYTES),
        cost_estimate=pl.CostEstimate(
            flops=2 * tokens * inner * width, bytes_accessed=4 * tokens * (width + inner) + 2 * inner * width, transcendentals=0
        ),
        name="mixed_grad",
    )(*parts, weight)


def store_parts(refs, length, part, value):
    value = value.astype(jnp.bfloat16)
    if part == 0:
        refs[0][...] = value[: length // 2]
        refs[1][...] = value[length // 2 :]
    else:
        refs[part + 1][...] = value


def store_all(refs, total):
    length = refs[-1].shape[0]
    for part in range(PLANE):
        store_parts(refs, length, part, total[part * length : (part + 1) * length])


def back_kernel(pieces, summed, *refs):
    grads, w_ref, refs = refs[:pieces], refs[pieces], refs[pieces + 1 :]
    if summed:
        values_ref, inverse_ref, *outs, sums_ref = refs
    else:
        outs = refs
    shares, _, rows, _ = w_ref.shape
    total = None
    start = 0
    for grads_ref in grads:
        cut = grads_ref.shape[1]
        weight = w_ref[:, 0, :, start : start + cut].reshape(shares * rows, cut)
        term = matmul_nt(grads_ref[...], weight)
        total = term if total is None else total + term
        start += cut
    store_all(outs, total)
    if summed:
        scaled = total * values_ref[...].astype(jnp.float32) * inverse_ref[...]
        sums_ref[...] = jnp.sum(scaled, axis=0, keepdims=True)


def parts_out(length, width, block):
    heights = (length // 2, length // 2, length, length, length)
    return (
        tuple(jax.ShapeDtypeStruct((h, width), jnp.bfloat16) for h in heights),
        tuple(pl.BlockSpec((h, block), lambda j: (0, j)) for h in heights),
    )


def back_parts(grads, weights, summed=None):
    tokens = grads[0].shape[0]
    inner = sum(g.shape[1] for g in grads)
    shares, groups, rows, columns = weights.shape
    block = shares * rows
    shapes, specs = parts_out(tokens // PLANE, groups * block, block)
    in_specs = [pl.BlockSpec(g.shape, lambda j: (0, 0), pipeline_mode=CONSTANT) for g in grads]
    in_specs.append(pl.BlockSpec((shares, 1, rows, columns), lambda j: (0, j, 0, 0)))
    if summed is not None:
        in_specs.append(pl.BlockSpec((tokens, block), lambda j: (0, j)))
        in_specs.append(pl.BlockSpec((tokens, 1), lambda j: (0, 0)))
        shapes += (jax.ShapeDtypeStruct((1, groups * block), jnp.float32),)
        specs += (pl.BlockSpec((1, block), lambda j: (0, j)),)
    return pl.pallas_call(
        functools.partial(back_kernel, len(grads), summed is not None),
        grid=(groups,),
        out_shape=shapes,
        in_specs=in_specs,
        out_specs=specs,
        compiler_params=pltpu.CompilerParams(vmem_limit_bytes=VMEM_BYTES),
        cost_estimate=pl.CostEstimate(
            flops=2 * tokens * inner * groups * block,
            bytes_accessed=2 * (tokens * inner + groups * block * (columns + tokens)),
            transcendentals=0,
        ),
        name="back_parts",
    )(*grads, weights, *(summed or ()))


def conv_back_kernel(seqs, taps, d_conv_ref, d_rate_ref, d_input_ref, rate_ref, input_ref, branch_ref, kernel_ref, out_ref, sums_ref, d_s):
    rows, channels = branch_ref.shape
    length = rows // seqs
    total = d_conv_ref[...] + matmul_nt(d_rate_ref[...], rate_ref[...]) + matmul_nt(d_input_ref[...], input_ref[...])
    nothing = jnp.zeros((8, channels), jnp.float32)
    for q in range(seqs):
        d_s[q, :length, :] = total[q * length : (q + 1) * length]
        d_s[q, length:, :] = nothing
    half = length // 2
    sums = [jnp.zeros((1, channels), jnp.float32) for _ in range(taps + 1)]
    for q in range(seqs):
        for start in (0, half):
            at = pl.ds(q * length + start, half)
            branch = branch_ref[at, :]
            d_branch = None
            for tap in range(taps):
                moved = d_s[q, pl.ds(start + taps - 1 - tap, half), :]
                term = kernel_ref[tap : tap + 1, :] * moved
                d_branch = term if d_branch is None else d_branch + term
                sums[tap] = sums[tap] + jnp.sum(branch * moved, axis=0, keepdims=True)
                if tap == taps - 1:
                    sums[taps] = sums[taps] + jnp.sum(moved, axis=0, keepdims=True)
            out_ref[at, :] = d_branch.astype(jnp.bfloat16)
    for k in range(taps + 1):
        sums_ref[k : k + 1, :] = sums[k]


def conv_back(seqs, d_conv, d_rate, d_input, w_rate, w_input, branch, kernel):
    rows, channels = branch.shape
    taps = kernel.shape[0]
    whole = lambda v: pl.BlockSpec(v.shape, lambda i: (0, 0))
    args = (d_conv, d_rate, d_input, w_rate, w_input, branch, kernel)
    return pl.pallas_call(
        functools.partial(conv_back_kernel, seqs, taps),
        grid=(1,),
        out_shape=(jax.ShapeDtypeStruct((rows, channels), jnp.bfloat16), jax.ShapeDtypeStruct((taps + 1, channels), jnp.float32)),
        in_specs=[whole(v) for v in args],
        out_specs=(pl.BlockSpec((rows, channels), lambda i: (0, 0)), pl.BlockSpec((taps + 1, channels), lambda i: (0, 0))),
        scratch_shapes=[pltpu.VMEM((seqs, rows // seqs + 8, channels), jnp.float32)],
        compiler_params=pltpu.CompilerParams(vmem_limit_bytes=VMEM_BYTES),
        cost_estimate=pl.CostEstimate(flops=8 * rows * channels * channels, bytes_accessed=16 * rows * channels, transcendentals=0),
        name="conv_back",
    )(*args)


def out_kernel(values_ref, w_ref, *refs):
    weight = w_ref[...].reshape(-1, w_ref.shape[-1])
    store_all(refs, jnp.dot(values_ref[...], weight, preferred_element_type=jnp.float32))


def out_parts(values, weight):
    weight, rows = weight
    tokens, inner = values.shape
    shares, _, width = weight.shape
    block = column_block(width, 512)
    shapes, specs = parts_out(tokens // PLANE, width, block)
    return pl.pallas_call(
        out_kernel,
        grid=(width // block,),
        out_shape=shapes,
        in_specs=[
            pl.BlockSpec((tokens, inner), lambda j: (0, 0), pipeline_mode=CONSTANT),
            pl.BlockSpec((shares, rows, block), lambda j: (0, 0, j)),
        ],
        out_specs=specs,
        compiler_params=pltpu.CompilerParams(vmem_limit_bytes=VMEM_BYTES),
        cost_estimate=pl.CostEstimate(
            flops=2 * tokens * inner * width, bytes_accessed=2 * (tokens * inner + inner * width + tokens * width), transcendentals=0
        ),
        name="out_parts",
    )(values, weight)


def weight_grad_kernel(rows, rights, steps, me_ref, left_ref, *refs):
    right_refs, mine_ref, theirs, left_s = refs[:rights], refs[rights], refs[rights + 1 : -1], refs[-1]
    narrow, groups, _, block = mine_ref.shape
    height = narrow * rows

    @pl.when(pl.program_id(1) == 0)
    def _():
        left_s[...] = left_ref[...].T

    def store(total, mine, other):
        for g in range(groups):
            start = (g * 2 + mine) * height
            mine_ref[:, g] = total[start : start + height].reshape(narrow, rows, block)
            start = (g * 2 + other) * height
            for k, ref in enumerate(theirs):
                ref[0, g] = total[start + k * rows : start + (k + 1) * rows]

    for k, right_ref in enumerate(right_refs):

        @pl.when(pl.program_id(1) // steps == k)
        def _(right_ref=right_ref):
            total = jnp.dot(left_s[...], right_ref[...], preferred_element_type=jnp.float32).astype(jnp.bfloat16)

            @pl.when(me_ref[0] == 0)
            def _():
                store(total, 0, 1)

            @pl.when(me_ref[0] != 0)
            def _():
                store(total, 1, 0)


def weight_grad(me, left, rights, narrow, groups, rows):
    tokens, piece = rights[0].shape
    block = column_block(piece, 768)
    steps = piece // block
    together = 2 if groups % 2 == 0 else 1
    height = together * 2 * narrow * rows
    columns = len(rights) * piece

    def right_spec(k):
        return pl.BlockSpec((tokens, block), lambda g, j, me_ref: (0, jnp.clip(j - k * steps, 0, steps - 1)))

    return pl.pallas_call(
        functools.partial(weight_grad_kernel, rows, len(rights), steps),
        grid_spec=pltpu.PrefetchScalarGridSpec(
            num_scalar_prefetch=1,
            grid=(groups // together, len(rights) * steps),
            in_specs=[pl.BlockSpec((tokens, height), lambda g, j, me_ref: (0, g))]
            + [right_spec(k) for k in range(len(rights))],
            out_specs=(pl.BlockSpec((narrow, together, rows, block), lambda g, j, me_ref: (0, g, 0, j)),)
            + (pl.BlockSpec((1, together, rows, block), lambda g, j, me_ref: (0, g, 0, j)),) * narrow,
            scratch_shapes=[pltpu.VMEM((height, tokens), jnp.bfloat16)],
        ),
        out_shape=(jax.ShapeDtypeStruct((narrow, groups, rows, columns), jnp.bfloat16),)
        + (jax.ShapeDtypeStruct((1, groups, rows, columns), jnp.bfloat16),) * narrow,
        compiler_params=pltpu.CompilerParams(vmem_limit_bytes=VMEM_BYTES),
        cost_estimate=pl.CostEstimate(
            flops=2 * tokens * left.shape[1] * columns,
            bytes_accessed=2 * (left.size + groups // together * tokens * columns + left.shape[1] * columns),
            transcendentals=0,
        ),
        name="weight_grad",
    )(me, left, *rights)


def add_pieces_kernel(mine_ref, *refs):
    for k, ref in enumerate(refs[:-1]):
        refs[-1][k] = (mine_ref[k].astype(jnp.float32) + ref[0].astype(jnp.float32)).astype(jnp.bfloat16)


def add_pieces(mine, others):
    narrow, groups, rows, columns = mine.shape
    block = column_block(columns, 1024)
    place = pl.BlockSpec((narrow, 1, rows, block), lambda g, j: (0, g, 0, j))
    return pl.pallas_call(
        add_pieces_kernel,
        grid=(groups, columns // block),
        out_shape=jax.ShapeDtypeStruct(mine.shape, jnp.bfloat16),
        in_specs=[place] + [pl.BlockSpec((1, 1, rows, block), lambda g, j: (0, g, 0, j))] * narrow,
        out_specs=place,
        compiler_params=pltpu.CompilerParams(vmem_limit_bytes=VMEM_BYTES),
        cost_estimate=pl.CostEstimate(flops=mine.size, bytes_accessed=6 * mine.size, transcendentals=0),
        name="add_pieces",
    )(mine, *others)


def block_diagonal(table):
    size, channels = table.shape
    tall = jnp.concatenate([table] * (channels // size), axis=0)
    row_head = lax.broadcasted_iota(jnp.int32, tall.shape, 0) // size
    column_head = lax.broadcasted_iota(jnp.int32, tall.shape, 1) // size
    return jnp.where(row_head == column_head, tall, jnp.zeros_like(tall))


def diagonal_blocks(square, size):
    channels = square.shape[0]
    cube = square.reshape(channels // size, size, channels)
    row_head = lax.broadcasted_iota(jnp.int32, cube.shape, 0)
    column_head = lax.broadcasted_iota(jnp.int32, cube.shape, 2) // size
    return jnp.sum(jnp.where(row_head == column_head, cube, jnp.zeros_like(cube)), axis=0)


def shift_rows(values, seqs, by):
    rows, channels = values.shape
    length = rows // seqs
    cube = values.reshape(seqs, length, channels)
    if by > 0:
        cube = jnp.pad(cube, ((0, 0), (by, 0), (0, 0)))[:, :length]
    elif by < 0:
        cube = jnp.pad(cube, ((0, 0), (0, -by), (0, 0)))[:, -by:]
    return cube.reshape(rows, channels)


def make_block(rest_size, narrow_size):
    bf16, f32 = jnp.bfloat16, jnp.float32
    spread = ("rest", "narrow")

    def swap(values, mask):
        return lax.ppermute(values, "wide", [(i, i ^ mask) for i in range(PLANE)])

    def gather_parts(shard):
        half = shard.shape[0] // 2
        one, two = swap(shard, 1), swap(shard, 2)
        return [swap(one[:half], 2), swap(two[half:], 1), one, two, shard]

    def gather_rows(shard):
        return jnp.concatenate(gather_parts(shard), axis=0)

    def scatter_start(parts, *beside):
        far_low, far_high, one, two, own = parts
        half = own.shape[0] // 2
        via_one, via_two, *beside = fence(swap(far_low, 1), swap(far_high, 2), *beside)
        one = jnp.concatenate([one[:half], (one[half:].astype(f32) + via_two.astype(f32)).astype(bf16)], axis=0)
        two = jnp.concatenate([(two[:half].astype(f32) + via_one.astype(f32)).astype(bf16), two[half:]], axis=0)
        return (one, two, own, *beside)

    def scatter_sum(own, one, two):
        return own.astype(f32) + one.astype(f32) + two.astype(f32)

    def scatter_finish(one, two, own):
        return scatter_sum(own, swap(one, 1), swap(two, 2))

    def scatter_rows(parts):
        return scatter_finish(*scatter_start(parts))

    def cut_columns(blocks):
        return lax.all_to_all(blocks, "wide", 0, 0, tiled=False)

    def gather_spread(part):
        whole = lax.all_gather(part.reshape(-1, part.shape[-1]), spread, axis=0, tiled=True)
        return whole.reshape((rest_size * narrow_size,) + part.shape)

    def grad_shares(left, rights, rows, groups):
        if rest_size != 2:
            grad = matmul_tn(left, jnp.concatenate(rights, axis=1)).astype(bf16)
            cut = grad.reshape(groups, rest_size, narrow_size, rows, -1).transpose(1, 2, 0, 3, 4)
            return cut, lambda term: lax.psum_scatter(term, "rest", scatter_dimension=0, tiled=False)
        me = lax.axis_index("rest").astype(jnp.int32)[None]
        mine, *theirs = weight_grad(me, left, rights, narrow_size, groups, rows)
        others = [lax.ppermute(piece, "rest", [(0, 1), (1, 0)]) for piece in theirs]
        return mine, lambda term: add_pieces(term, others)

    def sum_rest(values):
        if rest_size != 2:
            return lax.psum_scatter(values, "rest", scatter_dimension=0, tiled=False)
        me = lax.axis_index("rest")
        theirs = lax.dynamic_index_in_dim(values, 1 - me, 0, keepdims=False)
        mine = lax.dynamic_index_in_dim(values, me, 0, keepdims=False)
        other = lax.ppermute(theirs, "rest", [(0, 1), (1, 0)])
        return (mine.astype(f32) + other.astype(f32)).astype(values.dtype)

    def sum_narrow(values):
        return lax.psum_scatter(values.reshape(-1, values.shape[-1]), "narrow", scatter_dimension=0, tiled=True)

    def columns_home(mine, rows):
        return lax.all_to_all(mine.reshape(PLANE, rows, -1), "wide", 0, 1, tiled=False)

    def sum_narrow_direct(values):
        me = lax.axis_index("narrow")
        total = lax.dynamic_index_in_dim(values, me, 0, keepdims=False).astype(f32)
        for step in range(1, narrow_size):
            part = lax.dynamic_index_in_dim(values, lax.rem(me + step, narrow_size), 0, keepdims=False)
            pairs = [(i, (i + step) % narrow_size) for i in range(narrow_size)]
            total = total + lax.ppermute(part, "narrow", pairs).astype(f32)
        return total

    def to_all(values, axes, count):
        return lax.all_to_all(jnp.broadcast_to(values[None], (count,) + values.shape), axes, 0, 0, tiled=False)

    def rows_cut(grad):
        return grad.reshape(rest_size, narrow_size, -1, grad.shape[-1])

    def fence(*values):
        return lax.optimization_barrier(values)

    def after(values, *others):
        return lax.optimization_barrier((values,) + others)[0]

    def on_device(
        tokens,
        lengths,
        cotangent,
        norm_gain1,
        gate_in,
        x_in,
        conv_kernel,
        conv_bias,
        rate_weight,
        rate_bias,
        input_weight,
        input_bias,
        decay_param,
        out_proj,
        norm_gain2,
        mlp_gate,
        mlp_up,
        mlp_down,
    ):
        row_count, width = tokens.shape
        head = rate_weight.shape[0]
        rows = gate_in.shape[0]
        taps = conv_kernel.shape[0]
        seqs = PLANE
        channels = gate_in.shape[1] // PLANE
        hidden = mlp_gate.shape[1] // PLANE
        live = (jnp.arange(row_count, dtype=jnp.int32) < lengths[0]).astype(f32)[:, None]

        def by_plane(*weights):
            cut = [w.reshape(rows, PLANE, -1).swapaxes(0, 1) for w in weights]
            return jnp.concatenate(cut, axis=2)

        table = jnp.concatenate(
            [
                conv_kernel,
                conv_bias[None],
                rate_weight,
                rate_bias[None],
                input_weight,
                input_bias[None],
                decay_param[None],
            ],
            axis=0,
        )
        cuts = [taps, 1, head, 1, head, 1, 1]
        places = [sum(cuts[:i]) for i in range(len(cuts) + 1)]
        columns = 2 * channels
        shares = rest_size * narrow_size
        part_rec = cut_columns(by_plane(gate_in, x_in)).reshape(PLANE, rows, columns)
        w_rec = gather_spread(part_rec)
        tokens_all = gather_rows(after(tokens, part_rec))
        table = jnp.pad(table, ((0, -places[-1] % LANES), (0, 0))).T
        table = to_all(after(table, part_rec), spread, shares)
        gains = to_all(after(jnp.stack([norm_gain1, norm_gain2]), table), ("wide",) + spread, PLANE * shares)
        cut_mlp = by_plane(mlp_gate, mlp_up)
        w_rec, tokens_all, table, gains, cut_mlp = fence(w_rec, tokens_all, table, gains, cut_mlp)

        out_and_down = lax.all_gather(
            after(jnp.concatenate([out_proj, mlp_down], axis=0), w_rec), spread, axis=0, tiled=True
        ).reshape(rest_size * narrow_size, -1, width)
        low_res = (cotangent.astype(f32) * live).astype(bf16)
        low_res_parts = gather_parts(after(low_res, w_rec))
        low_res_all = jnp.concatenate(low_res_parts, axis=0)
        gains = gains.swapaxes(0, 1).reshape(2, width).astype(f32)
        gain_one, gain_two = gains[0:1], gains[1:2]
        table = table.reshape(channels, -1).T
        w_flat = w_rec.swapaxes(0, 1).reshape(width, columns)
        tokens_f = tokens_all.astype(f32)
        inverse_all = rms_inverse(tokens_f)
        normed1 = (tokens_f * inverse_all * gain_one).astype(bf16)
        gate_pre = matmul_low(normed1, w_flat[:, :channels])
        branch_pre = matmul_low(normed1, w_flat[:, channels:])
        kernel, shift, rate_table, b_rate, input_table, b_input, decay = (
            table[places[i] : places[i + 1]] for i in range(len(cuts))
        )
        kernel_f, shift_f, b_rate, b_input, decay_f = (v.astype(f32) for v in (kernel, shift, b_rate, b_input, decay))
        w_rate = block_diagonal(rate_table)
        w_input = block_diagonal(input_table)
        soft = softplus_minus(decay_f)
        soft_rows = jnp.broadcast_to(soft, (8, soft.shape[1]))
        part_mlp = cut_columns(after(cut_mlp, *low_res_parts))

        conv = shift_f
        for tap in range(taps):
            conv = conv + kernel_f[tap] * shift_rows(branch_pre, seqs, taps - 1 - tap)
        conv = conv.astype(bf16)
        rate_pre = matmul_low(conv, w_rate) + b_rate
        input_pre = matmul_low(conv, w_input) + b_input
        states, mixed = lru_forward(seqs, conv, rate_pre, input_pre, gate_pre, soft_rows)
        mixed, part_mlp, out_and_down = fence(mixed, part_mlp, out_and_down)
        out_rows = out_proj.shape[0]
        if out_rows % 16 == 0:
            w_out = (out_and_down, out_rows)
        else:
            w_out = (out_and_down[:, :out_rows].reshape(1, -1, width), shares * out_rows)
        w_down = out_and_down[:, out_rows:].reshape(-1, width)

        w_mlp = gather_spread(part_mlp)
        merged = tokens.astype(f32) + scatter_rows(out_parts(mixed, w_out))
        inverse2 = rms_inverse(merged)
        normed2 = (merged * inverse2 * gain_two).astype(bf16)
        *normed2_parts, w_mlp = fence(*gather_parts(normed2), w_mlp)

        product, d_gate_two, d_up_two, normed2_all = mlp_both(normed2_parts, low_res_all, w_mlp, w_down)
        mine, finish = grad_shares(product, (low_res_all,), mlp_down.shape[0], 1)
        mine, late_gate_two = fence(mine, d_gate_two)
        parts2 = back_parts((late_gate_two, d_up_two), w_mlp)
        down_out = sum_narrow(finish(mine))
        one, two, own = scatter_start(parts2)
        mine, finish = grad_shares(normed2_all, (late_gate_two,), rows, PLANE)
        grad_mgate = finish(mine)
        d_normed2 = scatter_finish(one, two, own)
        d_normed2, grad_mgate, down_out, late_up_two, late_product = fence(
            d_normed2, grad_mgate, down_out, d_up_two, product
        )

        mgate_sum = sum_narrow(grad_mgate)
        grad_gain2 = jnp.sum(d_normed2 * merged * inverse2, axis=0)
        d_merged = low_res.astype(f32) + rms_back(merged, inverse2, gain_two, d_normed2)
        low_merged_parts = gather_parts(d_merged.astype(bf16))
        mine, finish = grad_shares(normed2_all, (late_up_two,), rows, PLANE)
        grad_mup = finish(mine)
        parts_result = out_parts(late_product, (w_down[None], w_down.shape[0]))
        *low_merged_parts, parts_result, mgate_sum, grad_mup = fence(*low_merged_parts, parts_result, mgate_sum, grad_mup)
        d_mixed, low_merged_all = mixed_grad(low_merged_parts, w_out)
        mup_sum = sum_narrow(grad_mup)
        sums_result = scatter_start(parts_result)
        d_mixed, *sums_result = fence(d_mixed, *sums_result)
        d_conv_lru, d_rate, d_input, d_gate, sums = lru_backward(
            seqs, conv, rate_pre, input_pre, gate_pre, soft_rows, states, d_mixed
        )
        mgate_out = columns_home(mgate_sum, rows)
        sums = sums.reshape(3, 8, -1).sum(axis=1)
        grad_decay = sums[2] * (-1.0 / (1.0 + jnp.exp(decay_f[0])))
        low_branch, conv_sums = conv_back(seqs, d_conv_lru, d_rate, d_input, w_rate, w_input, branch_pre, kernel_f)
        one, two, own = sums_result
        result_one, result_two = swap(one, 1), swap(two, 2)

        low_branch, mgate_out, result_one, result_two = fence(low_branch, mgate_out, result_one, result_two)
        result = merged + scatter_sum(own, result_one, result_two)
        mine, finish = grad_shares(normed1, (d_gate, low_branch), rows, PLANE)
        rec_sum = sum_narrow(finish(mine))
        *parts1, grad_gain1 = back_parts((d_gate, low_branch), w_rec, (tokens_all, inverse_all))
        one, two, own = scatter_start(parts1)
        one, two, late_mixed, late_rate, late_input = fence(one, two, mixed, d_rate, d_input)
        d_normed1 = scatter_finish(one, two, own)
        grad_out = matmul_tn(late_mixed, low_merged_all).astype(bf16)
        gain_grads = jnp.stack([grad_gain1[0], grad_gain2]).reshape(2, -1, rows).swapaxes(0, 1)
        grad_rate_weight = diagonal_blocks(matmul_tn(conv, late_rate), head)
        grad_input_weight = diagonal_blocks(matmul_tn(conv, late_input), head)
        table_grad = jnp.concatenate(
            [
                conv_sums,
                grad_rate_weight,
                sums[0:1],
                grad_input_weight,
                sums[1:2],
                grad_decay[None],
            ],
            axis=0,
        )
        table_grad = jnp.pad(table_grad, ((0, -places[-1] % LANES), (0, 0))).T.astype(bf16)
        last = sum_rest(rows_cut(jnp.concatenate([grad_out, table_grad], axis=1)))
        rec_sum, d_normed1, last, gain_grads, mup_sum = fence(rec_sum, d_normed1, last, gain_grads, mup_sum)
        last = sum_narrow(last).astype(f32)
        out_out, table_out = last[:, :width], last[:, width:].T

        rec_out = columns_home(rec_sum, rows)
        mup_out = columns_home(mup_sum, rows)
        gain_out = lax.all_to_all(gain_grads, ("wide",) + spread, 0, 0, tiled=False).sum(axis=0)
        block_out = (result * live).astype(bf16)
        own = tokens.astype(f32)
        input_grad = d_merged + rms_back(own, rms_inverse(own), gain_one, d_normed1)

        kernel_out, shift_out, rate_out, rate_bias_out, input_out, input_bias_out, decay_out = (
            table_out[places[i] : places[i + 1]] for i in range(len(cuts))
        )
        def whole_rows(cut):
            return cut.reshape(rows, -1).astype(f32)

        return (
            block_out,
            input_grad,
            gain_out[0],
            whole_rows(rec_out[:, :, :channels]),
            whole_rows(rec_out[:, :, channels:]),
            kernel_out,
            shift_out[0],
            rate_out,
            rate_bias_out[0],
            input_out,
            input_bias_out[0],
            decay_out[0],
            out_out,
            gain_out[1],
            whole_rows(mgate_out),
            whole_rows(mup_out),
            down_out.astype(f32),
        )

    return on_device


def solution(mesh):
    wide, narrow = mesh.shape["wide"], mesh.shape["narrow"]
    mesh = Mesh(mesh.devices.reshape(PLANE, wide // PLANE, narrow), ("wide", "rest", "narrow"))
    every = mesh.axis_names
    rows, columns, vector = P(every, None), P(None, every), P(every)
    return jax.shard_map(
        make_block(wide // PLANE, narrow),
        mesh=mesh,
        in_specs=(
            rows,
            vector,
            rows,
            vector,
            rows,
            rows,
            columns,
            vector,
            columns,
            vector,
            columns,
            vector,
            vector,
            rows,
            vector,
            rows,
            rows,
            rows,
        ),
        out_specs=(
            rows,
            rows,
            vector,
            rows,
            rows,
            columns,
            vector,
            columns,
            vector,
            columns,
            vector,
            vector,
            rows,
            vector,
            rows,
            rows,
            rows,
        ),
        check_vma=False,
    )
```

```python
import functools

import jax
import jax.numpy as jnp
from jax import lax
from jax.experimental import pallas as pl
from jax.experimental.pallas import tpu as pltpu
from jax.sharding import Mesh
from jax.sharding import PartitionSpec as P

EPSILON = 1e-06
RATE_SCALE = 8.0
GELU_ROOT = 0.7978845608028654
GELU_CUBE = 0.044715
LANES = 128
PLANE = 4


def matmul_low(left, right):
    return jnp.dot(left, right, preferred_element_type=jnp.float32)


def matmul_nt(left, right):
    return lax.dot_general(left, right, (((1,), (1,)), ((), ())), preferred_element_type=jnp.float32)


def matmul_tn(left, right):
    return lax.dot_general(left, right, (((0,), (0,)), ((), ())), preferred_element_type=jnp.float32)


def rms_inverse(values):
    return lax.rsqrt(jnp.mean(values * values, axis=-1, keepdims=True) + EPSILON)


def rms_back(values, inverse, gain, grads):
    scaled = grads * gain
    dots = jnp.mean(scaled * values, axis=-1, keepdims=True)
    return inverse * scaled - values * (inverse * inverse * inverse * dots)


def gelu_pair(values):
    square = values * values
    slope = jnp.tanh(GELU_ROOT * values * (1.0 + GELU_CUBE * square))
    half = 0.5 * (1.0 + slope)
    grad = half + 0.5 * values * (1.0 - slope * slope) * (GELU_ROOT * (1.0 + 3.0 * GELU_CUBE * square))
    return values * half, grad


def softplus_minus(values):
    return jnp.maximum(-values, 0.0) + jnp.log(1.0 + jnp.exp(-jnp.abs(values)))


def sigmoid(values):
    return 1.0 / (1.0 + jnp.exp(jnp.minimum(-values, 80.0)))


def lru_terms(rate_pre, input_pre, soft):
    rate_gate = sigmoid(rate_pre)
    input_gate = sigmoid(input_pre)
    log_decay = -RATE_SCALE * rate_gate * soft
    decay_now = jnp.exp(log_decay)
    twice = 2.0 * log_decay
    series = -twice * (1.0 + twice * 0.5 * (1.0 + twice * (1.0 / 3.0) * (1.0 + twice * 0.25)))
    square = jnp.maximum(jnp.where(twice > -0.0625, series, 1.0 - decay_now * decay_now), 1e-30)
    return rate_gate, input_gate, decay_now, square, lax.rsqrt(square)


CHUNK = 160
UNROLL = 16


def lru_forward_kernel(seqs, conv_ref, rate_ref, input_ref, gate_ref, soft_ref, states_ref, mixed_ref, decay_s, drive_s):
    rows = conv_ref.shape[0]
    length = rows // seqs
    soft = soft_ref[0:1, :]

    def prepare(i, carry):
        at = pl.ds(pl.multiple_of(i * CHUNK, CHUNK), CHUNK)
        conv = conv_ref[at, :].astype(jnp.float32)
        _, input_gate, decay_now, square, inverse = lru_terms(rate_ref[at, :], input_ref[at, :], soft)
        decay_s[at, :] = decay_now
        drive_s[at, :] = square * inverse * input_gate * conv
        return carry

    lax.fori_loop(0, rows // CHUNK, prepare, 0)

    def advance(i, state):
        places = [pl.ds(i * UNROLL + j, seqs, stride=length) for j in range(UNROLL)]
        decays = [decay_s[at, :] for at in places]
        drives = [drive_s[at, :] for at in places]
        for at, decay, drive in zip(places, decays, drives):
            state = decay * state + drive
            states_ref[at, :] = state
        return state

    lax.fori_loop(0, length // UNROLL, advance, jnp.zeros((seqs, LANES), jnp.float32))

    def finish(i, carry):
        at = pl.ds(pl.multiple_of(i * CHUNK, CHUNK), CHUNK)
        value, _ = gelu_pair(gate_ref[at, :])
        mixed_ref[at, :] = (states_ref[at, :] * value).astype(jnp.bfloat16)
        return carry

    lax.fori_loop(0, rows // CHUNK, finish, 0)


def lru_backward_kernel(
    seqs,
    conv_ref,
    rate_ref,
    input_ref,
    gate_ref,
    soft_ref,
    states_ref,
    grad_ref,
    d_conv_ref,
    d_rate_ref,
    d_input_ref,
    d_gate_ref,
    sums_ref,
    decay_s,
    flow_s,
    total_s,
    gate_s,
    drive_s,
    input_s,
    scale_s,
):
    rows = conv_ref.shape[0]
    length = rows // seqs
    soft = soft_ref[0:1, :]

    def prepare(i, carry):
        at = pl.ds(pl.multiple_of(i * CHUNK, CHUNK), CHUNK)
        value, slope = gelu_pair(gate_ref[at, :])
        grad = grad_ref[at, :]
        d_gate_ref[at, :] = (grad * states_ref[at, :] * slope).astype(jnp.bfloat16)
        flow_s[at, :] = grad * value
        conv = conv_ref[at, :].astype(jnp.float32)
        rate_gate, input_gate, decay_now, square, inverse = lru_terms(rate_ref[at, :], input_ref[at, :], soft)
        drive = square * inverse * input_gate
        decay_s[at, :] = decay_now
        gate_s[at, :] = rate_gate
        drive_s[at, :] = drive
        input_s[at, :] = drive * conv * (1.0 - input_gate)
        scale_s[at, :] = input_gate * conv * decay_now * inverse
        return carry

    lax.fori_loop(0, rows // CHUNK, prepare, 0)

    def retreat(i, carry):
        flow, decay = carry
        places = [pl.ds(length - 1 - (i * UNROLL + j), seqs, stride=length) for j in range(UNROLL)]
        flows = [flow_s[at, :] for at in places]
        decays = [decay_s[at, :] for at in places]
        for at, here, later in zip(places, flows, [decay] + decays[:-1]):
            flow = here + later * flow
            total_s[at, :] = flow
        return flow, decays[-1]

    nothing = jnp.zeros((seqs, LANES), jnp.float32)
    lax.fori_loop(0, length // UNROLL, retreat, (nothing, nothing))

    first_row = lax.broadcasted_iota(jnp.int32, (CHUNK, LANES), 0) == 0

    def finish(i, carry):
        rate_sum, input_sum, soft_sum, last = carry
        at = pl.ds(pl.multiple_of(i * CHUNK, CHUNK), CHUNK)
        states = states_ref[at, :]
        last = jnp.where(lax.rem(i, length // CHUNK) == 0, jnp.zeros_like(last), last)
        before = jnp.where(first_row, last, pltpu.roll(states, 1, 0))
        flow = total_s[at, :]
        rate_gate = gate_s[at, :]
        d_log = flow * decay_s[at, :] * (before - scale_s[at, :])
        d_soft = d_log * rate_gate * (-RATE_SCALE)
        d_rate = d_soft * soft * (1.0 - rate_gate)
        d_input = flow * input_s[at, :]
        d_conv_ref[at, :] = flow * drive_s[at, :]
        d_rate_ref[at, :] = d_rate.astype(jnp.bfloat16)
        d_input_ref[at, :] = d_input.astype(jnp.bfloat16)

        def fold(total, part):
            for k in range(CHUNK // 8):
                total = total + part[k * 8 : (k + 1) * 8, :]
            return total

        return fold(rate_sum, d_rate), fold(input_sum, d_input), fold(soft_sum, d_soft), states[CHUNK - 1 :, :]

    blank = jnp.zeros((8, LANES), jnp.float32)
    sums = lax.fori_loop(0, rows // CHUNK, finish, (blank, blank, blank, jnp.zeros((1, LANES), jnp.float32)))
    for k in range(3):
        sums_ref[k * 8 : (k + 1) * 8, :] = sums[k]


def lru_forward(seqs, conv, rate_pre, input_pre, gate_pre, soft):
    rows, channels = conv.shape
    block = pl.BlockSpec((rows, LANES), lambda i: (0, i))
    return pl.pallas_call(
        functools.partial(lru_forward_kernel, seqs),
        grid=(pl.cdiv(channels, LANES),),
        out_shape=(
            jax.ShapeDtypeStruct((rows, channels), jnp.float32),
            jax.ShapeDtypeStruct((rows, channels), jnp.bfloat16),
        ),
        in_specs=[block, block, block, block, pl.BlockSpec((8, LANES), lambda i: (0, i))],
        out_specs=(block, block),
        scratch_shapes=[pltpu.VMEM((rows, LANES), jnp.float32)] * 2,
        compiler_params=pltpu.CompilerParams(vmem_limit_bytes=48 * 2**20),
        cost_estimate=pl.CostEstimate(flops=200000 * rows * channels // 10, bytes_accessed=20 * rows * channels, transcendentals=8 * rows * channels),
        name="lru_forward",
    )(conv, rate_pre, input_pre, gate_pre, soft)


def lru_backward(seqs, conv, rate_pre, input_pre, gate_pre, soft, states, grads):
    rows, channels = conv.shape
    block = pl.BlockSpec((rows, LANES), lambda i: (0, i))
    return pl.pallas_call(
        functools.partial(lru_backward_kernel, seqs),
        grid=(pl.cdiv(channels, LANES),),
        out_shape=(
            jax.ShapeDtypeStruct((rows, channels), jnp.float32),
            jax.ShapeDtypeStruct((rows, channels), jnp.bfloat16),
            jax.ShapeDtypeStruct((rows, channels), jnp.bfloat16),
            jax.ShapeDtypeStruct((rows, channels), jnp.bfloat16),
            jax.ShapeDtypeStruct((24, channels), jnp.float32),
        ),
        in_specs=[block, block, block, block, pl.BlockSpec((8, LANES), lambda i: (0, i)), block, block],
        out_specs=(block, block, block, block, pl.BlockSpec((24, LANES), lambda i: (0, i))),
        scratch_shapes=[pltpu.VMEM((rows, LANES), jnp.float32)] * 7,
        compiler_params=pltpu.CompilerParams(vmem_limit_bytes=48 * 2**20),
        cost_estimate=pl.CostEstimate(flops=200000 * rows * channels // 10, bytes_accessed=20 * rows * channels, transcendentals=16 * rows * channels),
        name="lru_backward",
    )(conv, rate_pre, input_pre, gate_pre, soft, states, grads)


CONSTANT = pl.Buffered(1)
VMEM_BYTES = 56 * 2**20


def column_block(columns, most):
    return max(w for w in range(LANES, most + 1, LANES) if columns % w == 0)


def mlp_kernel(slots, *refs):
    parts, refs = refs[: slots + 1], refs[slots + 1 :]
    low_ref, gate_ref, up_ref, down_ref, product_ref, d_gate_ref, d_up_ref, normed_ref, w_s = refs
    groups, rows = gate_ref.shape[1], gate_ref.shape[2]
    stride = gate_ref.shape[0] * rows

    @pl.when(pl.program_id(0) == 0)
    def _():
        start = 0
        for part in parts:
            normed_ref[start : start + part.shape[0], :] = part[...]
            start += part.shape[0]

    for c in range(groups):
        for k in range(gate_ref.shape[0]):
            at = pl.ds(c * stride + k * rows, rows)
            w_s[0, at, :] = gate_ref[k, c]
            w_s[1, at, :] = up_ref[k, c]
    length = low_ref.shape[0] // slots

    for i in range(slots):
        at = pl.ds(i * length, length)
        here = normed_ref[at, :]
        gate = jnp.dot(here, w_s[0], preferred_element_type=jnp.float32)
        up = jnp.dot(here, w_s[1], preferred_element_type=jnp.float32)
        grad = matmul_nt(low_ref[at, :], down_ref[...])
        value, slope = gelu_pair(gate)
        product_ref[at, :] = (value * up).astype(jnp.bfloat16)
        d_gate_ref[at, :] = (grad * up * slope).astype(jnp.bfloat16)
        d_up_ref[at, :] = (grad * value).astype(jnp.bfloat16)


def mlp_both(parts, low_res, weights, w_down):
    tokens, width = low_res.shape
    hidden = w_down.shape[0]
    block = column_block(hidden, 256)
    steps = hidden // block
    lead = weights.shape[:3]
    return pl.pallas_call(
        functools.partial(mlp_kernel, PLANE),
        grid=(steps,),
        out_shape=(jax.ShapeDtypeStruct((tokens, hidden), jnp.bfloat16),) * 3
        + (jax.ShapeDtypeStruct((tokens, width), jnp.bfloat16),),
        in_specs=[pl.BlockSpec(p.shape, lambda j: (0, 0), pipeline_mode=CONSTANT) for p in parts]
        + [
            pl.BlockSpec((tokens, width), lambda j: (0, 0), pipeline_mode=CONSTANT),
            pl.BlockSpec(lead + (block,), lambda j: (0, 0, 0, j)),
            pl.BlockSpec(lead + (block,), lambda j: (0, 0, 0, j + steps)),
            pl.BlockSpec((block, width), lambda j: (j, 0)),
        ],
        out_specs=(pl.BlockSpec((tokens, block), lambda j: (0, j)),) * 3
        + (pl.BlockSpec((tokens, width), lambda j: (0, 0)),),
        scratch_shapes=[pltpu.VMEM((2, width, block), jnp.bfloat16)],
        compiler_params=pltpu.CompilerParams(vmem_limit_bytes=VMEM_BYTES),
        cost_estimate=pl.CostEstimate(
            flops=6 * tokens * width * hidden, bytes_accessed=2 * (3 * tokens * width + 3 * width * hidden), transcendentals=tokens * hidden
        ),
        name="mlp_both",
    )(*parts, low_res, weights, weights, w_down)


def mixed_grad_kernel(*refs):
    parts, w_ref, grad_ref, whole_ref = refs[:-3], refs[-3], refs[-2], refs[-1]
    start = 0
    weight = w_ref[...].reshape(-1, w_ref.shape[-1])
    for part in parts:
        at = pl.ds(start, part.shape[0])
        here = part[...]
        whole_ref[at, :] = here
        grad_ref[at, :] = matmul_nt(here, weight)
        start += part.shape[0]


def mixed_grad(parts, weight):
    weight, rows = weight
    width = parts[0].shape[1]
    tokens = sum(p.shape[0] for p in parts)
    inner = weight.shape[0] * rows
    return pl.pallas_call(
        mixed_grad_kernel,
        grid=(1,),
        out_shape=(jax.ShapeDtypeStruct((tokens, inner), jnp.float32), jax.ShapeDtypeStruct((tokens, width), jnp.bfloat16)),
        in_specs=[pl.BlockSpec(p.shape, lambda j: (0, 0)) for p in parts]
        + [pl.BlockSpec((weight.shape[0], rows, width), lambda j: (0, 0, 0))],
        out_specs=(pl.BlockSpec((tokens, inner), lambda j: (0, 0)), pl.BlockSpec((tokens, width), lambda j: (0, 0))),
        compiler_params=pltpu.CompilerParams(vmem_limit_bytes=VMEM_BYTES),
        cost_estimate=pl.CostEstimate(
            flops=2 * tokens * inner * width, bytes_accessed=4 * tokens * (width + inner) + 2 * inner * width, transcendentals=0
        ),
        name="mixed_grad",
    )(*parts, weight)


def store_parts(refs, length, part, value):
    value = value.astype(jnp.bfloat16)
    if part == 0:
        refs[0][...] = value[: length // 2]
        refs[1][...] = value[length // 2 :]
    else:
        refs[part + 1][...] = value


def store_all(refs, total):
    length = refs[-1].shape[0]
    for part in range(PLANE):
        store_parts(refs, length, part, total[part * length : (part + 1) * length])


def back_kernel(pieces, summed, *refs):
    grads, w_ref, refs = refs[:pieces], refs[pieces], refs[pieces + 1 :]
    if summed:
        values_ref, inverse_ref, *outs, sums_ref = refs
    else:
        outs = refs
    shares, _, rows, _ = w_ref.shape
    total = None
    start = 0
    for grads_ref in grads:
        cut = grads_ref.shape[1]
        weight = w_ref[:, 0, :, start : start + cut].reshape(shares * rows, cut)
        term = matmul_nt(grads_ref[...], weight)
        total = term if total is None else total + term
        start += cut
    store_all(outs, total)
    if summed:
        scaled = total * values_ref[...].astype(jnp.float32) * inverse_ref[...]
        sums_ref[...] = jnp.sum(scaled, axis=0, keepdims=True)


def parts_out(length, width, block):
    heights = (length // 2, length // 2, length, length, length)
    return (
        tuple(jax.ShapeDtypeStruct((h, width), jnp.bfloat16) for h in heights),
        tuple(pl.BlockSpec((h, block), lambda j: (0, j)) for h in heights),
    )


def back_parts(grads, weights, summed=None):
    tokens = grads[0].shape[0]
    inner = sum(g.shape[1] for g in grads)
    shares, groups, rows, columns = weights.shape
    block = shares * rows
    shapes, specs = parts_out(tokens // PLANE, groups * block, block)
    in_specs = [pl.BlockSpec(g.shape, lambda j: (0, 0), pipeline_mode=CONSTANT) for g in grads]
    in_specs.append(pl.BlockSpec((shares, 1, rows, columns), lambda j: (0, j, 0, 0)))
    if summed is not None:
        in_specs.append(pl.BlockSpec((tokens, block), lambda j: (0, j)))
        in_specs.append(pl.BlockSpec((tokens, 1), lambda j: (0, 0)))
        shapes += (jax.ShapeDtypeStruct((1, groups * block), jnp.float32),)
        specs += (pl.BlockSpec((1, block), lambda j: (0, j)),)
    return pl.pallas_call(
        functools.partial(back_kernel, len(grads), summed is not None),
        grid=(groups,),
        out_shape=shapes,
        in_specs=in_specs,
        out_specs=specs,
        compiler_params=pltpu.CompilerParams(vmem_limit_bytes=VMEM_BYTES),
        cost_estimate=pl.CostEstimate(
            flops=2 * tokens * inner * groups * block,
            bytes_accessed=2 * (tokens * inner + groups * block * (columns + tokens)),
            transcendentals=0,
        ),
        name="back_parts",
    )(*grads, weights, *(summed or ()))


def conv_back_kernel(seqs, taps, d_conv_ref, d_rate_ref, d_input_ref, rate_ref, input_ref, branch_ref, kernel_ref, out_ref, sums_ref, d_s):
    rows, channels = branch_ref.shape
    length = rows // seqs
    total = d_conv_ref[...] + matmul_nt(d_rate_ref[...], rate_ref[...]) + matmul_nt(d_input_ref[...], input_ref[...])
    nothing = jnp.zeros((8, channels), jnp.float32)
    for q in range(seqs):
        d_s[q, :length, :] = total[q * length : (q + 1) * length]
        d_s[q, length:, :] = nothing
    half = length // 2
    sums = [jnp.zeros((1, channels), jnp.float32) for _ in range(taps + 1)]
    for q in range(seqs):
        for start in (0, half):
            at = pl.ds(q * length + start, half)
            branch = branch_ref[at, :]
            d_branch = None
            for tap in range(taps):
                moved = d_s[q, pl.ds(start + taps - 1 - tap, half), :]
                term = kernel_ref[tap : tap + 1, :] * moved
                d_branch = term if d_branch is None else d_branch + term
                sums[tap] = sums[tap] + jnp.sum(branch * moved, axis=0, keepdims=True)
                if tap == taps - 1:
                    sums[taps] = sums[taps] + jnp.sum(moved, axis=0, keepdims=True)
            out_ref[at, :] = d_branch.astype(jnp.bfloat16)
    for k in range(taps + 1):
        sums_ref[k : k + 1, :] = sums[k]


def conv_back(seqs, d_conv, d_rate, d_input, w_rate, w_input, branch, kernel):
    rows, channels = branch.shape
    taps = kernel.shape[0]
    whole = lambda v: pl.BlockSpec(v.shape, lambda i: (0, 0))
    args = (d_conv, d_rate, d_input, w_rate, w_input, branch, kernel)
    return pl.pallas_call(
        functools.partial(conv_back_kernel, seqs, taps),
        grid=(1,),
        out_shape=(jax.ShapeDtypeStruct((rows, channels), jnp.bfloat16), jax.ShapeDtypeStruct((taps + 1, channels), jnp.float32)),
        in_specs=[whole(v) for v in args],
        out_specs=(pl.BlockSpec((rows, channels), lambda i: (0, 0)), pl.BlockSpec((taps + 1, channels), lambda i: (0, 0))),
        scratch_shapes=[pltpu.VMEM((seqs, rows // seqs + 8, channels), jnp.float32)],
        compiler_params=pltpu.CompilerParams(vmem_limit_bytes=VMEM_BYTES),
        cost_estimate=pl.CostEstimate(flops=8 * rows * channels * channels, bytes_accessed=16 * rows * channels, transcendentals=0),
        name="conv_back",
    )(*args)


def out_kernel(values_ref, w_ref, *refs):
    weight = w_ref[...].reshape(-1, w_ref.shape[-1])
    store_all(refs, jnp.dot(values_ref[...], weight, preferred_element_type=jnp.float32))


def out_parts(values, weight):
    weight, rows = weight
    tokens, inner = values.shape
    shares, _, width = weight.shape
    block = column_block(width, 512)
    shapes, specs = parts_out(tokens // PLANE, width, block)
    return pl.pallas_call(
        out_kernel,
        grid=(width // block,),
        out_shape=shapes,
        in_specs=[
            pl.BlockSpec((tokens, inner), lambda j: (0, 0), pipeline_mode=CONSTANT),
            pl.BlockSpec((shares, rows, block), lambda j: (0, 0, j)),
        ],
        out_specs=specs,
        compiler_params=pltpu.CompilerParams(vmem_limit_bytes=VMEM_BYTES),
        cost_estimate=pl.CostEstimate(
            flops=2 * tokens * inner * width, bytes_accessed=2 * (tokens * inner + inner * width + tokens * width), transcendentals=0
        ),
        name="out_parts",
    )(values, weight)


def weight_grad_kernel(rows, rights, steps, me_ref, left_ref, *refs):
    right_refs, mine_ref, theirs, left_s = refs[:rights], refs[rights], refs[rights + 1 : -1], refs[-1]
    narrow, groups, _, block = mine_ref.shape
    height = narrow * rows

    @pl.when(pl.program_id(1) == 0)
    def _():
        left_s[...] = left_ref[...].T

    def store(total, mine, other):
        for g in range(groups):
            start = (g * 2 + mine) * height
            mine_ref[:, g] = total[start : start + height].reshape(narrow, rows, block)
            start = (g * 2 + other) * height
            for k, ref in enumerate(theirs):
                ref[0, g] = total[start + k * rows : start + (k + 1) * rows]

    for k, right_ref in enumerate(right_refs):

        @pl.when(pl.program_id(1) // steps == k)
        def _(right_ref=right_ref):
            total = jnp.dot(left_s[...], right_ref[...], preferred_element_type=jnp.float32).astype(jnp.bfloat16)

            @pl.when(me_ref[0] == 0)
            def _():
                store(total, 0, 1)

            @pl.when(me_ref[0] != 0)
            def _():
                store(total, 1, 0)


def weight_grad(me, left, rights, narrow, groups, rows):
    tokens, piece = rights[0].shape
    block = column_block(piece, 768)
    steps = piece // block
    together = 2 if groups % 2 == 0 else 1
    height = together * 2 * narrow * rows
    columns = len(rights) * piece

    def right_spec(k):
        return pl.BlockSpec((tokens, block), lambda g, j, me_ref: (0, jnp.clip(j - k * steps, 0, steps - 1)))

    return pl.pallas_call(
        functools.partial(weight_grad_kernel, rows, len(rights), steps),
        grid_spec=pltpu.PrefetchScalarGridSpec(
            num_scalar_prefetch=1,
            grid=(groups // together, len(rights) * steps),
            in_specs=[pl.BlockSpec((tokens, height), lambda g, j, me_ref: (0, g))]
            + [right_spec(k) for k in range(len(rights))],
            out_specs=(pl.BlockSpec((narrow, together, rows, block), lambda g, j, me_ref: (0, g, 0, j)),)
            + (pl.BlockSpec((1, together, rows, block), lambda g, j, me_ref: (0, g, 0, j)),) * narrow,
            scratch_shapes=[pltpu.VMEM((height, tokens), jnp.bfloat16)],
        ),
        out_shape=(jax.ShapeDtypeStruct((narrow, groups, rows, columns), jnp.bfloat16),)
        + (jax.ShapeDtypeStruct((1, groups, rows, columns), jnp.bfloat16),) * narrow,
        compiler_params=pltpu.CompilerParams(vmem_limit_bytes=VMEM_BYTES),
        cost_estimate=pl.CostEstimate(
            flops=2 * tokens * left.shape[1] * columns,
            bytes_accessed=2 * (left.size + groups // together * tokens * columns + left.shape[1] * columns),
            transcendentals=0,
        ),
        name="weight_grad",
    )(me, left, *rights)


def add_pieces_kernel(mine_ref, *refs):
    for k, ref in enumerate(refs[:-1]):
        refs[-1][k] = (mine_ref[k].astype(jnp.float32) + ref[0].astype(jnp.float32)).astype(jnp.bfloat16)


def add_pieces(mine, others):
    narrow, groups, rows, columns = mine.shape
    block = column_block(columns, 2048 if groups > 1 else 512)
    place = pl.BlockSpec((narrow, 1, rows, block), lambda g, j: (0, g, 0, j))
    return pl.pallas_call(
        add_pieces_kernel,
        grid=(groups, columns // block),
        out_shape=jax.ShapeDtypeStruct(mine.shape, jnp.bfloat16),
        in_specs=[place] + [pl.BlockSpec((1, 1, rows, block), lambda g, j: (0, g, 0, j))] * narrow,
        out_specs=place,
        compiler_params=pltpu.CompilerParams(vmem_limit_bytes=VMEM_BYTES),
        cost_estimate=pl.CostEstimate(flops=mine.size, bytes_accessed=6 * mine.size, transcendentals=0),
        name="add_pieces",
    )(mine, *others)


def block_diagonal(table):
    size, channels = table.shape
    tall = jnp.concatenate([table] * (channels // size), axis=0)
    row_head = lax.broadcasted_iota(jnp.int32, tall.shape, 0) // size
    column_head = lax.broadcasted_iota(jnp.int32, tall.shape, 1) // size
    return jnp.where(row_head == column_head, tall, jnp.zeros_like(tall))


def diagonal_blocks(square, size):
    channels = square.shape[0]
    cube = square.reshape(channels // size, size, channels)
    row_head = lax.broadcasted_iota(jnp.int32, cube.shape, 0)
    column_head = lax.broadcasted_iota(jnp.int32, cube.shape, 2) // size
    return jnp.sum(jnp.where(row_head == column_head, cube, jnp.zeros_like(cube)), axis=0)


def shift_rows(values, seqs, by):
    rows, channels = values.shape
    length = rows // seqs
    cube = values.reshape(seqs, length, channels)
    if by > 0:
        cube = jnp.pad(cube, ((0, 0), (by, 0), (0, 0)))[:, :length]
    elif by < 0:
        cube = jnp.pad(cube, ((0, 0), (0, -by), (0, 0)))[:, -by:]
    return cube.reshape(rows, channels)


def make_block(rest_size, narrow_size):
    bf16, f32 = jnp.bfloat16, jnp.float32
    spread = ("rest", "narrow")

    def swap(values, mask):
        return lax.ppermute(values, "wide", [(i, i ^ mask) for i in range(PLANE)])

    def gather_parts(shard):
        half = shard.shape[0] // 2
        one, two = swap(shard, 1), swap(shard, 2)
        return [swap(one[:half], 2), swap(two[half:], 1), one, two, shard]

    def gather_rows(shard):
        return jnp.concatenate(gather_parts(shard), axis=0)

    def scatter_start(parts, *beside):
        far_low, far_high, one, two, own = parts
        half = own.shape[0] // 2
        via_one, via_two, *beside = fence(swap(far_low, 1), swap(far_high, 2), *beside)
        one = jnp.concatenate([one[:half], (one[half:].astype(f32) + via_two.astype(f32)).astype(bf16)], axis=0)
        two = jnp.concatenate([(two[:half].astype(f32) + via_one.astype(f32)).astype(bf16), two[half:]], axis=0)
        return (one, two, own, *beside)

    def scatter_sum(own, one, two):
        return own.astype(f32) + one.astype(f32) + two.astype(f32)

    def scatter_finish(one, two, own):
        return scatter_sum(own, swap(one, 1), swap(two, 2))

    def scatter_rows(parts):
        return scatter_finish(*scatter_start(parts))

    def cut_columns(blocks):
        return lax.all_to_all(blocks, "wide", 0, 0, tiled=False)

    def gather_spread(part):
        whole = lax.all_gather(part.reshape(-1, part.shape[-1]), spread, axis=0, tiled=True)
        return whole.reshape((rest_size * narrow_size,) + part.shape)

    def grad_shares(left, rights, rows, groups):
        if rest_size != 2:
            grad = matmul_tn(left, jnp.concatenate(rights, axis=1)).astype(bf16)
            cut = grad.reshape(groups, rest_size, narrow_size, rows, -1).transpose(1, 2, 0, 3, 4)
            return cut, lambda term: lax.psum_scatter(term, "rest", scatter_dimension=0, tiled=False)
        me = lax.axis_index("rest").astype(jnp.int32)[None]
        mine, *theirs = weight_grad(me, left, rights, narrow_size, groups, rows)
        others = [lax.ppermute(piece, "rest", [(0, 1), (1, 0)]) for piece in theirs]
        return mine, lambda term: add_pieces(term, others)

    def sum_rest(values):
        if rest_size != 2:
            return lax.psum_scatter(values, "rest", scatter_dimension=0, tiled=False)
        me = lax.axis_index("rest")
        theirs = lax.dynamic_index_in_dim(values, 1 - me, 0, keepdims=False)
        mine = lax.dynamic_index_in_dim(values, me, 0, keepdims=False)
        other = lax.ppermute(theirs, "rest", [(0, 1), (1, 0)])
        return (mine.astype(f32) + other.astype(f32)).astype(values.dtype)

    def sum_narrow(values):
        return lax.psum_scatter(values.reshape(-1, values.shape[-1]), "narrow", scatter_dimension=0, tiled=True)

    def columns_home(mine, rows):
        return lax.all_to_all(mine.reshape(PLANE, rows, -1), "wide", 0, 1, tiled=False)

    def sum_narrow_direct(values):
        me = lax.axis_index("narrow")
        total = lax.dynamic_index_in_dim(values, me, 0, keepdims=False).astype(f32)
        for step in range(1, narrow_size):
            part = lax.dynamic_index_in_dim(values, lax.rem(me + step, narrow_size), 0, keepdims=False)
            pairs = [(i, (i + step) % narrow_size) for i in range(narrow_size)]
            total = total + lax.ppermute(part, "narrow", pairs).astype(f32)
        return total

    def to_all(values, axes, count):
        return lax.all_to_all(jnp.broadcast_to(values[None], (count,) + values.shape), axes, 0, 0, tiled=False)

    def rows_cut(grad):
        return grad.reshape(rest_size, narrow_size, -1, grad.shape[-1])

    def fence(*values):
        return lax.optimization_barrier(values)

    def after(values, *others):
        return lax.optimization_barrier((values,) + others)[0]

    def on_device(
        tokens,
        lengths,
        cotangent,
        norm_gain1,
        gate_in,
        x_in,
        conv_kernel,
        conv_bias,
        rate_weight,
        rate_bias,
        input_weight,
        input_bias,
        decay_param,
        out_proj,
        norm_gain2,
        mlp_gate,
        mlp_up,
        mlp_down,
    ):
        row_count, width = tokens.shape
        head = rate_weight.shape[0]
        rows = gate_in.shape[0]
        taps = conv_kernel.shape[0]
        seqs = PLANE
        channels = gate_in.shape[1] // PLANE
        hidden = mlp_gate.shape[1] // PLANE
        live = (jnp.arange(row_count, dtype=jnp.int32) < lengths[0]).astype(f32)[:, None]

        def by_plane(*weights):
            cut = [w.reshape(rows, PLANE, -1).swapaxes(0, 1) for w in weights]
            return jnp.concatenate(cut, axis=2)

        table = jnp.concatenate(
            [
                conv_kernel,
                conv_bias[None],
                rate_weight,
                rate_bias[None],
                input_weight,
                input_bias[None],
                decay_param[None],
            ],
            axis=0,
        )
        cuts = [taps, 1, head, 1, head, 1, 1]
        places = [sum(cuts[:i]) for i in range(len(cuts) + 1)]
        columns = 2 * channels
        shares = rest_size * narrow_size
        part_rec = cut_columns(by_plane(gate_in, x_in)).reshape(PLANE, rows, columns)
        w_rec = gather_spread(part_rec)
        tokens_all = gather_rows(after(tokens, part_rec))
        table = jnp.pad(table, ((0, -places[-1] % LANES), (0, 0))).T
        table = to_all(after(table, part_rec), spread, shares)
        gains = to_all(after(jnp.stack([norm_gain1, norm_gain2]), table), ("wide",) + spread, PLANE * shares)
        cut_mlp = by_plane(mlp_gate, mlp_up)
        w_rec, tokens_all, table, gains, cut_mlp = fence(w_rec, tokens_all, table, gains, cut_mlp)

        out_and_down = lax.all_gather(
            after(jnp.concatenate([out_proj, mlp_down], axis=0), w_rec), spread, axis=0, tiled=True
        ).reshape(rest_size * narrow_size, -1, width)
        low_res = (cotangent.astype(f32) * live).astype(bf16)
        low_res_parts = gather_parts(after(low_res, w_rec))
        low_res_all = jnp.concatenate(low_res_parts, axis=0)
        gains = gains.swapaxes(0, 1).reshape(2, width).astype(f32)
        gain_one, gain_two = gains[0:1], gains[1:2]
        table = table.reshape(channels, -1).T
        w_flat = w_rec.swapaxes(0, 1).reshape(width, columns)
        tokens_f = tokens_all.astype(f32)
        inverse_all = rms_inverse(tokens_f)
        normed1 = (tokens_f * inverse_all * gain_one).astype(bf16)
        gate_pre = matmul_low(normed1, w_flat[:, :channels])
        branch_pre = matmul_low(normed1, w_flat[:, channels:])
        kernel, shift, rate_table, b_rate, input_table, b_input, decay = (
            table[places[i] : places[i + 1]] for i in range(len(cuts))
        )
        kernel_f, shift_f, b_rate, b_input, decay_f = (v.astype(f32) for v in (kernel, shift, b_rate, b_input, decay))
        w_rate = block_diagonal(rate_table)
        w_input = block_diagonal(input_table)
        soft = softplus_minus(decay_f)
        soft_rows = jnp.broadcast_to(soft, (8, soft.shape[1]))
        part_mlp = cut_columns(after(cut_mlp, *low_res_parts))

        conv = shift_f
        for tap in range(taps):
            conv = conv + kernel_f[tap] * shift_rows(branch_pre, seqs, taps - 1 - tap)
        conv = conv.astype(bf16)
        rate_pre = matmul_low(conv, w_rate) + b_rate
        input_pre = matmul_low(conv, w_input) + b_input
        states, mixed = lru_forward(seqs, conv, rate_pre, input_pre, gate_pre, soft_rows)
        mixed, part_mlp, out_and_down = fence(mixed, part_mlp, out_and_down)
        out_rows = out_proj.shape[0]
        if out_rows % 16 == 0:
            w_out = (out_and_down, out_rows)
        else:
            w_out = (out_and_down[:, :out_rows].reshape(1, -1, width), shares * out_rows)
        w_down = out_and_down[:, out_rows:].reshape(-1, width)

        w_mlp = gather_spread(part_mlp)
        merged = tokens.astype(f32) + scatter_rows(out_parts(mixed, w_out))
        inverse2 = rms_inverse(merged)
        normed2 = (merged * inverse2 * gain_two).astype(bf16)
        *normed2_parts, w_mlp = fence(*gather_parts(normed2), w_mlp)

        product, d_gate_two, d_up_two, normed2_all = mlp_both(normed2_parts, low_res_all, w_mlp, w_down)
        mine, finish = grad_shares(product, (low_res_all,), mlp_down.shape[0], 1)
        mine, late_gate_two = fence(mine, d_gate_two)
        parts2 = back_parts((late_gate_two, d_up_two), w_mlp)
        down_out = sum_narrow(finish(mine))
        one, two, own = scatter_start(parts2)
        mine, finish = grad_shares(normed2_all, (late_gate_two,), rows, PLANE)
        grad_mgate = finish(mine)
        d_normed2 = scatter_finish(one, two, own)
        d_normed2, grad_mgate, down_out, late_up_two, late_product = fence(
            d_normed2, grad_mgate, down_out, d_up_two, product
        )

        mgate_sum = sum_narrow(grad_mgate)
        grad_gain2 = jnp.sum(d_normed2 * merged * inverse2, axis=0)
        d_merged = low_res.astype(f32) + rms_back(merged, inverse2, gain_two, d_normed2)
        low_merged_parts = gather_parts(d_merged.astype(bf16))
        mine, finish = grad_shares(normed2_all, (late_up_two,), rows, PLANE)
        grad_mup = finish(mine)
        parts_result = out_parts(late_product, (w_down[None], w_down.shape[0]))
        *low_merged_parts, parts_result, mgate_sum, grad_mup = fence(*low_merged_parts, parts_result, mgate_sum, grad_mup)
        d_mixed, low_merged_all = mixed_grad(low_merged_parts, w_out)
        mup_sum = sum_narrow(grad_mup)
        sums_result = scatter_start(parts_result)
        d_mixed, *sums_result = fence(d_mixed, *sums_result)
        d_conv_lru, d_rate, d_input, d_gate, sums = lru_backward(
            seqs, conv, rate_pre, input_pre, gate_pre, soft_rows, states, d_mixed
        )
        mgate_out = columns_home(mgate_sum, rows)
        sums = sums.reshape(3, 8, -1).sum(axis=1)
        grad_decay = sums[2] * (-1.0 / (1.0 + jnp.exp(decay_f[0])))
        low_branch, conv_sums = conv_back(seqs, d_conv_lru, d_rate, d_input, w_rate, w_input, branch_pre, kernel_f)
        one, two, own = sums_result
        result_one, result_two = swap(one, 1), swap(two, 2)

        low_branch, mgate_out, result_one, result_two = fence(low_branch, mgate_out, result_one, result_two)
        result = merged + scatter_sum(own, result_one, result_two)
        *parts1, grad_gain1 = back_parts((d_gate, low_branch), w_rec, (tokens_all, inverse_all))
        *parts1, late_gate = fence(*parts1, d_gate)
        mine, finish = grad_shares(normed1, (late_gate, low_branch), rows, PLANE)
        grad_rec = finish(mine)
        rec_sum = sum_narrow(grad_rec)
        one, two, own = scatter_start(parts1)
        one, two, late_mixed, late_rate, late_input = fence(one, two, mixed, d_rate, d_input)
        d_normed1 = scatter_finish(one, two, own)
        grad_out = matmul_tn(late_mixed, low_merged_all).astype(bf16)
        gain_grads = jnp.stack([grad_gain1[0], grad_gain2]).reshape(2, -1, rows).swapaxes(0, 1)
        grad_rate_weight = diagonal_blocks(matmul_tn(conv, late_rate), head)
        grad_input_weight = diagonal_blocks(matmul_tn(conv, late_input), head)
        table_grad = jnp.concatenate(
            [
                conv_sums,
                grad_rate_weight,
                sums[0:1],
                grad_input_weight,
                sums[1:2],
                grad_decay[None],
            ],
            axis=0,
        )
        table_grad = jnp.pad(table_grad, ((0, -places[-1] % LANES), (0, 0))).T.astype(bf16)
        last = sum_rest(rows_cut(jnp.concatenate([grad_out, table_grad], axis=1)))
        mup_out = columns_home(mup_sum, rows)
        rec_sum, d_normed1, last, gain_grads, mup_out = fence(rec_sum, d_normed1, last, gain_grads, mup_out)
        last = sum_narrow(last).astype(f32)
        out_out, table_out = last[:, :width], last[:, width:].T

        rec_out = columns_home(rec_sum, rows)
        gain_out = lax.all_to_all(gain_grads, ("wide",) + spread, 0, 0, tiled=False).sum(axis=0)
        block_out = (result * live).astype(bf16)
        own = tokens.astype(f32)
        input_grad = d_merged + rms_back(own, rms_inverse(own), gain_one, d_normed1)

        kernel_out, shift_out, rate_out, rate_bias_out, input_out, input_bias_out, decay_out = (
            table_out[places[i] : places[i + 1]] for i in range(len(cuts))
        )
        def whole_rows(cut):
            return cut.reshape(rows, -1).astype(f32)

        return (
            block_out,
            input_grad,
            gain_out[0],
            whole_rows(rec_out[:, :, :channels]),
            whole_rows(rec_out[:, :, channels:]),
            kernel_out,
            shift_out[0],
            rate_out,
            rate_bias_out[0],
            input_out,
            input_bias_out[0],
            decay_out[0],
            out_out,
            gain_out[1],
            whole_rows(mgate_out),
            whole_rows(mup_out),
            down_out.astype(f32),
        )

    return on_device


def solution(mesh):
    wide, narrow = mesh.shape["wide"], mesh.shape["narrow"]
    mesh = Mesh(mesh.devices.reshape(PLANE, wide // PLANE, narrow), ("wide", "rest", "narrow"))
    every = mesh.axis_names
    rows, columns, vector = P(every, None), P(None, every), P(every)
    return jax.shard_map(
        make_block(wide // PLANE, narrow),
        mesh=mesh,
        in_specs=(
            rows,
            vector,
            rows,
            vector,
            rows,
            rows,
            columns,
            vector,
            columns,
            vector,
            columns,
            vector,
            vector,
            rows,
            vector,
            rows,
            rows,
            rows,
        ),
        out_specs=(
            rows,
            rows,
            vector,
            rows,
            rows,
            columns,
            vector,
            columns,
            vector,
            columns,
            vector,
            vector,
            rows,
            vector,
            rows,
            rows,
            rows,
        ),
        check_vma=False,
    )
```

```python
import functools

import jax
import jax.numpy as jnp
from jax import lax
from jax.experimental import pallas as pl
from jax.experimental.pallas import tpu as pltpu
from jax.sharding import Mesh
from jax.sharding import PartitionSpec as P

EPSILON = 1e-06
RATE_SCALE = 8.0
GELU_ROOT = 0.7978845608028654
GELU_CUBE = 0.044715
LANES = 128
PLANE = 4


def matmul_low(left, right):
    return jnp.dot(left, right, preferred_element_type=jnp.float32)


def matmul_nt(left, right):
    return lax.dot_general(left, right, (((1,), (1,)), ((), ())), preferred_element_type=jnp.float32)


def matmul_tn(left, right):
    return lax.dot_general(left, right, (((0,), (0,)), ((), ())), preferred_element_type=jnp.float32)


def rms_inverse(values):
    return lax.rsqrt(jnp.mean(values * values, axis=-1, keepdims=True) + EPSILON)


def rms_back(values, inverse, gain, grads):
    scaled = grads * gain
    dots = jnp.mean(scaled * values, axis=-1, keepdims=True)
    return inverse * scaled - values * (inverse * inverse * inverse * dots)


def gelu_pair(values):
    square = values * values
    slope = jnp.tanh(GELU_ROOT * values * (1.0 + GELU_CUBE * square))
    half = 0.5 * (1.0 + slope)
    grad = half + 0.5 * values * (1.0 - slope * slope) * (GELU_ROOT * (1.0 + 3.0 * GELU_CUBE * square))
    return values * half, grad


def softplus_minus(values):
    return jnp.maximum(-values, 0.0) + jnp.log(1.0 + jnp.exp(-jnp.abs(values)))


def sigmoid(values):
    return 1.0 / (1.0 + jnp.exp(jnp.minimum(-values, 80.0)))


def lru_terms(rate_pre, input_pre, soft):
    rate_gate = sigmoid(rate_pre)
    input_gate = sigmoid(input_pre)
    log_decay = -RATE_SCALE * rate_gate * soft
    decay_now = jnp.exp(log_decay)
    twice = 2.0 * log_decay
    series = -twice * (1.0 + twice * 0.5 * (1.0 + twice * (1.0 / 3.0) * (1.0 + twice * 0.25)))
    square = jnp.maximum(jnp.where(twice > -0.0625, series, 1.0 - decay_now * decay_now), 1e-30)
    return rate_gate, input_gate, decay_now, square, lax.rsqrt(square)


CHUNK = 160
UNROLL = 16


def lru_forward_kernel(seqs, conv_ref, rate_ref, input_ref, gate_ref, soft_ref, states_ref, mixed_ref, decay_s, drive_s):
    rows = conv_ref.shape[0]
    length = rows // seqs
    soft = soft_ref[0:1, :]

    def prepare(i, carry):
        at = pl.ds(pl.multiple_of(i * CHUNK, CHUNK), CHUNK)
        conv = conv_ref[at, :].astype(jnp.float32)
        _, input_gate, decay_now, square, inverse = lru_terms(rate_ref[at, :], input_ref[at, :], soft)
        decay_s[at, :] = decay_now
        drive_s[at, :] = square * inverse * input_gate * conv
        return carry

    lax.fori_loop(0, rows // CHUNK, prepare, 0)

    def advance(i, state):
        places = [pl.ds(i * UNROLL + j, seqs, stride=length) for j in range(UNROLL)]
        decays = [decay_s[at, :] for at in places]
        drives = [drive_s[at, :] for at in places]
        for at, decay, drive in zip(places, decays, drives):
            state = decay * state + drive
            states_ref[at, :] = state
        return state

    lax.fori_loop(0, length // UNROLL, advance, jnp.zeros((seqs, LANES), jnp.float32))

    def finish(i, carry):
        at = pl.ds(pl.multiple_of(i * CHUNK, CHUNK), CHUNK)
        value, _ = gelu_pair(gate_ref[at, :])
        mixed_ref[at, :] = (states_ref[at, :] * value).astype(jnp.bfloat16)
        return carry

    lax.fori_loop(0, rows // CHUNK, finish, 0)


def lru_backward_kernel(
    seqs,
    conv_ref,
    rate_ref,
    input_ref,
    gate_ref,
    soft_ref,
    states_ref,
    grad_ref,
    d_conv_ref,
    d_rate_ref,
    d_input_ref,
    d_gate_ref,
    sums_ref,
    decay_s,
    flow_s,
    total_s,
    gate_s,
    drive_s,
    input_s,
    scale_s,
):
    rows = conv_ref.shape[0]
    length = rows // seqs
    soft = soft_ref[0:1, :]

    def prepare(i, carry):
        at = pl.ds(pl.multiple_of(i * CHUNK, CHUNK), CHUNK)
        value, slope = gelu_pair(gate_ref[at, :])
        grad = grad_ref[at, :]
        d_gate_ref[at, :] = (grad * states_ref[at, :] * slope).astype(jnp.bfloat16)
        flow_s[at, :] = grad * value
        conv = conv_ref[at, :].astype(jnp.float32)
        rate_gate, input_gate, decay_now, square, inverse = lru_terms(rate_ref[at, :], input_ref[at, :], soft)
        drive = square * inverse * input_gate
        decay_s[at, :] = decay_now
        gate_s[at, :] = rate_gate
        drive_s[at, :] = drive
        input_s[at, :] = drive * conv * (1.0 - input_gate)
        scale_s[at, :] = input_gate * conv * decay_now * inverse
        return carry

    lax.fori_loop(0, rows // CHUNK, prepare, 0)

    def retreat(i, carry):
        flow, decay = carry
        places = [pl.ds(length - 1 - (i * UNROLL + j), seqs, stride=length) for j in range(UNROLL)]
        flows = [flow_s[at, :] for at in places]
        decays = [decay_s[at, :] for at in places]
        for at, here, later in zip(places, flows, [decay] + decays[:-1]):
            flow = here + later * flow
            total_s[at, :] = flow
        return flow, decays[-1]

    nothing = jnp.zeros((seqs, LANES), jnp.float32)
    lax.fori_loop(0, length // UNROLL, retreat, (nothing, nothing))

    first_row = lax.broadcasted_iota(jnp.int32, (CHUNK, LANES), 0) == 0

    def finish(i, carry):
        rate_sum, input_sum, soft_sum, last = carry
        at = pl.ds(pl.multiple_of(i * CHUNK, CHUNK), CHUNK)
        states = states_ref[at, :]
        last = jnp.where(lax.rem(i, length // CHUNK) == 0, jnp.zeros_like(last), last)
        before = jnp.where(first_row, last, pltpu.roll(states, 1, 0))
        flow = total_s[at, :]
        rate_gate = gate_s[at, :]
        d_log = flow * decay_s[at, :] * (before - scale_s[at, :])
        d_soft = d_log * rate_gate * (-RATE_SCALE)
        d_rate = d_soft * soft * (1.0 - rate_gate)
        d_input = flow * input_s[at, :]
        d_conv_ref[at, :] = flow * drive_s[at, :]
        d_rate_ref[at, :] = d_rate.astype(jnp.bfloat16)
        d_input_ref[at, :] = d_input.astype(jnp.bfloat16)

        def fold(total, part):
            for k in range(CHUNK // 8):
                total = total + part[k * 8 : (k + 1) * 8, :]
            return total

        return fold(rate_sum, d_rate), fold(input_sum, d_input), fold(soft_sum, d_soft), states[CHUNK - 1 :, :]

    blank = jnp.zeros((8, LANES), jnp.float32)
    sums = lax.fori_loop(0, rows // CHUNK, finish, (blank, blank, blank, jnp.zeros((1, LANES), jnp.float32)))
    for k in range(3):
        sums_ref[k * 8 : (k + 1) * 8, :] = sums[k]


def lru_forward(seqs, conv, rate_pre, input_pre, gate_pre, soft):
    rows, channels = conv.shape
    block = pl.BlockSpec((rows, LANES), lambda i: (0, i))
    return pl.pallas_call(
        functools.partial(lru_forward_kernel, seqs),
        grid=(pl.cdiv(channels, LANES),),
        out_shape=(
            jax.ShapeDtypeStruct((rows, channels), jnp.float32),
            jax.ShapeDtypeStruct((rows, channels), jnp.bfloat16),
        ),
        in_specs=[block, block, block, block, pl.BlockSpec((8, LANES), lambda i: (0, i))],
        out_specs=(block, block),
        scratch_shapes=[pltpu.VMEM((rows, LANES), jnp.float32)] * 2,
        compiler_params=pltpu.CompilerParams(vmem_limit_bytes=48 * 2**20),
        cost_estimate=pl.CostEstimate(flops=200000 * rows * channels // 10, bytes_accessed=20 * rows * channels, transcendentals=8 * rows * channels),
        name="lru_forward",
    )(conv, rate_pre, input_pre, gate_pre, soft)


def lru_backward(seqs, conv, rate_pre, input_pre, gate_pre, soft, states, grads):
    rows, channels = conv.shape
    block = pl.BlockSpec((rows, LANES), lambda i: (0, i))
    return pl.pallas_call(
        functools.partial(lru_backward_kernel, seqs),
        grid=(pl.cdiv(channels, LANES),),
        out_shape=(
            jax.ShapeDtypeStruct((rows, channels), jnp.float32),
            jax.ShapeDtypeStruct((rows, channels), jnp.bfloat16),
            jax.ShapeDtypeStruct((rows, channels), jnp.bfloat16),
            jax.ShapeDtypeStruct((rows, channels), jnp.bfloat16),
            jax.ShapeDtypeStruct((24, channels), jnp.float32),
        ),
        in_specs=[block, block, block, block, pl.BlockSpec((8, LANES), lambda i: (0, i)), block, block],
        out_specs=(block, block, block, block, pl.BlockSpec((24, LANES), lambda i: (0, i))),
        scratch_shapes=[pltpu.VMEM((rows, LANES), jnp.float32)] * 7,
        compiler_params=pltpu.CompilerParams(vmem_limit_bytes=48 * 2**20),
        cost_estimate=pl.CostEstimate(flops=200000 * rows * channels // 10, bytes_accessed=20 * rows * channels, transcendentals=16 * rows * channels),
        name="lru_backward",
    )(conv, rate_pre, input_pre, gate_pre, soft, states, grads)


CONSTANT = pl.Buffered(1)
VMEM_BYTES = 56 * 2**20


def column_block(columns, most):
    return max(w for w in range(LANES, most + 1, LANES) if columns % w == 0)


def mlp_kernel(slots, *refs):
    parts, refs = refs[: slots + 1], refs[slots + 1 :]
    low_ref, gate_ref, up_ref, down_ref, product_ref, d_gate_ref, d_up_ref, normed_ref, w_s = refs
    groups, rows = gate_ref.shape[1], gate_ref.shape[2]
    stride = gate_ref.shape[0] * rows

    @pl.when(pl.program_id(0) == 0)
    def _():
        start = 0
        for part in parts:
            normed_ref[start : start + part.shape[0], :] = part[...]
            start += part.shape[0]

    for c in range(groups):
        for k in range(gate_ref.shape[0]):
            at = pl.ds(c * stride + k * rows, rows)
            w_s[0, at, :] = gate_ref[k, c]
            w_s[1, at, :] = up_ref[k, c]
    length = low_ref.shape[0] // slots

    for i in range(slots):
        at = pl.ds(i * length, length)
        here = normed_ref[at, :]
        gate = jnp.dot(here, w_s[0], preferred_element_type=jnp.float32)
        up = jnp.dot(here, w_s[1], preferred_element_type=jnp.float32)
        grad = matmul_nt(low_ref[at, :], down_ref[...])
        value, slope = gelu_pair(gate)
        product_ref[at, :] = (value * up).astype(jnp.bfloat16)
        d_gate_ref[at, :] = (grad * up * slope).astype(jnp.bfloat16)
        d_up_ref[at, :] = (grad * value).astype(jnp.bfloat16)


def mlp_both(parts, low_res, weights, w_down):
    tokens, width = low_res.shape
    hidden = w_down.shape[0]
    block = column_block(hidden, 256)
    steps = hidden // block
    lead = weights.shape[:3]
    return pl.pallas_call(
        functools.partial(mlp_kernel, PLANE),
        grid=(steps,),
        out_shape=(jax.ShapeDtypeStruct((tokens, hidden), jnp.bfloat16),) * 3
        + (jax.ShapeDtypeStruct((tokens, width), jnp.bfloat16),),
        in_specs=[pl.BlockSpec(p.shape, lambda j: (0, 0), pipeline_mode=CONSTANT) for p in parts]
        + [
            pl.BlockSpec((tokens, width), lambda j: (0, 0), pipeline_mode=CONSTANT),
            pl.BlockSpec(lead + (block,), lambda j: (0, 0, 0, j)),
            pl.BlockSpec(lead + (block,), lambda j: (0, 0, 0, j + steps)),
            pl.BlockSpec((block, width), lambda j: (j, 0)),
        ],
        out_specs=(pl.BlockSpec((tokens, block), lambda j: (0, j)),) * 3
        + (pl.BlockSpec((tokens, width), lambda j: (0, 0)),),
        scratch_shapes=[pltpu.VMEM((2, width, block), jnp.bfloat16)],
        compiler_params=pltpu.CompilerParams(vmem_limit_bytes=VMEM_BYTES),
        cost_estimate=pl.CostEstimate(
            flops=6 * tokens * width * hidden, bytes_accessed=2 * (3 * tokens * width + 3 * width * hidden), transcendentals=tokens * hidden
        ),
        name="mlp_both",
    )(*parts, low_res, weights, weights, w_down)


def mixed_grad_kernel(*refs):
    parts, w_ref, grad_ref, whole_ref = refs[:-3], refs[-3], refs[-2], refs[-1]
    start = 0
    weight = w_ref[...].reshape(-1, w_ref.shape[-1])
    for part in parts:
        at = pl.ds(start, part.shape[0])
        here = part[...]
        whole_ref[at, :] = here
        grad_ref[at, :] = matmul_nt(here, weight)
        start += part.shape[0]


def mixed_grad(parts, weight):
    weight, rows = weight
    width = parts[0].shape[1]
    tokens = sum(p.shape[0] for p in parts)
    inner = weight.shape[0] * rows
    return pl.pallas_call(
        mixed_grad_kernel,
        grid=(1,),
        out_shape=(jax.ShapeDtypeStruct((tokens, inner), jnp.float32), jax.ShapeDtypeStruct((tokens, width), jnp.bfloat16)),
        in_specs=[pl.BlockSpec(p.shape, lambda j: (0, 0)) for p in parts]
        + [pl.BlockSpec((weight.shape[0], rows, width), lambda j: (0, 0, 0))],
        out_specs=(pl.BlockSpec((tokens, inner), lambda j: (0, 0)), pl.BlockSpec((tokens, width), lambda j: (0, 0))),
        compiler_params=pltpu.CompilerParams(vmem_limit_bytes=VMEM_BYTES),
        cost_estimate=pl.CostEstimate(
            flops=2 * tokens * inner * width, bytes_accessed=4 * tokens * (width + inner) + 2 * inner * width, transcendentals=0
        ),
        name="mixed_grad",
    )(*parts, weight)


def store_parts(refs, length, part, value):
    value = value.astype(jnp.bfloat16)
    if part == 0:
        refs[0][...] = value[: length // 2]
        refs[1][...] = value[length // 2 :]
    else:
        refs[part + 1][...] = value


def store_all(refs, total):
    length = refs[-1].shape[0]
    for part in range(PLANE):
        store_parts(refs, length, part, total[part * length : (part + 1) * length])


def back_kernel(pieces, summed, *refs):
    grads, w_ref, refs = refs[:pieces], refs[pieces], refs[pieces + 1 :]
    if summed:
        values_ref, inverse_ref, *outs, sums_ref = refs
    else:
        outs = refs
    shares, _, rows, _ = w_ref.shape
    total = None
    start = 0
    for grads_ref in grads:
        cut = grads_ref.shape[1]
        weight = w_ref[:, 0, :, start : start + cut].reshape(shares * rows, cut)
        term = matmul_nt(grads_ref[...], weight)
        total = term if total is None else total + term
        start += cut
    store_all(outs, total)
    if summed:
        scaled = total * values_ref[...].astype(jnp.float32) * inverse_ref[...]
        sums_ref[...] = jnp.sum(scaled, axis=0, keepdims=True)


def parts_out(length, width, block):
    heights = (length // 2, length // 2, length, length, length)
    return (
        tuple(jax.ShapeDtypeStruct((h, width), jnp.bfloat16) for h in heights),
        tuple(pl.BlockSpec((h, block), lambda j: (0, j)) for h in heights),
    )


def back_parts(grads, weights, summed=None):
    tokens = grads[0].shape[0]
    inner = sum(g.shape[1] for g in grads)
    shares, groups, rows, columns = weights.shape
    block = shares * rows
    shapes, specs = parts_out(tokens // PLANE, groups * block, block)
    in_specs = [pl.BlockSpec(g.shape, lambda j: (0, 0), pipeline_mode=CONSTANT) for g in grads]
    in_specs.append(pl.BlockSpec((shares, 1, rows, columns), lambda j: (0, j, 0, 0)))
    if summed is not None:
        in_specs.append(pl.BlockSpec((tokens, block), lambda j: (0, j)))
        in_specs.append(pl.BlockSpec((tokens, 1), lambda j: (0, 0)))
        shapes += (jax.ShapeDtypeStruct((1, groups * block), jnp.float32),)
        specs += (pl.BlockSpec((1, block), lambda j: (0, j)),)
    return pl.pallas_call(
        functools.partial(back_kernel, len(grads), summed is not None),
        grid=(groups,),
        out_shape=shapes,
        in_specs=in_specs,
        out_specs=specs,
        compiler_params=pltpu.CompilerParams(vmem_limit_bytes=VMEM_BYTES),
        cost_estimate=pl.CostEstimate(
            flops=2 * tokens * inner * groups * block,
            bytes_accessed=2 * (tokens * inner + groups * block * (columns + tokens)),
            transcendentals=0,
        ),
        name="back_parts",
    )(*grads, weights, *(summed or ()))


def conv_back_kernel(seqs, taps, d_conv_ref, d_rate_ref, d_input_ref, rate_ref, input_ref, branch_ref, kernel_ref, out_ref, sums_ref, d_s):
    rows, channels = branch_ref.shape
    length = rows // seqs
    total = d_conv_ref[...] + matmul_nt(d_rate_ref[...], rate_ref[...]) + matmul_nt(d_input_ref[...], input_ref[...])
    nothing = jnp.zeros((8, channels), jnp.float32)
    for q in range(seqs):
        d_s[q, :length, :] = total[q * length : (q + 1) * length]
        d_s[q, length:, :] = nothing
    half = length // 2
    sums = [jnp.zeros((1, channels), jnp.float32) for _ in range(taps + 1)]
    for q in range(seqs):
        for start in (0, half):
            at = pl.ds(q * length + start, half)
            branch = branch_ref[at, :]
            d_branch = None
            for tap in range(taps):
                moved = d_s[q, pl.ds(start + taps - 1 - tap, half), :]
                term = kernel_ref[tap : tap + 1, :] * moved
                d_branch = term if d_branch is None else d_branch + term
                sums[tap] = sums[tap] + jnp.sum(branch * moved, axis=0, keepdims=True)
                if tap == taps - 1:
                    sums[taps] = sums[taps] + jnp.sum(moved, axis=0, keepdims=True)
            out_ref[at, :] = d_branch.astype(jnp.bfloat16)
    for k in range(taps + 1):
        sums_ref[k : k + 1, :] = sums[k]


def conv_back(seqs, d_conv, d_rate, d_input, w_rate, w_input, branch, kernel):
    rows, channels = branch.shape
    taps = kernel.shape[0]
    whole = lambda v: pl.BlockSpec(v.shape, lambda i: (0, 0))
    args = (d_conv, d_rate, d_input, w_rate, w_input, branch, kernel)
    return pl.pallas_call(
        functools.partial(conv_back_kernel, seqs, taps),
        grid=(1,),
        out_shape=(jax.ShapeDtypeStruct((rows, channels), jnp.bfloat16), jax.ShapeDtypeStruct((taps + 1, channels), jnp.float32)),
        in_specs=[whole(v) for v in args],
        out_specs=(pl.BlockSpec((rows, channels), lambda i: (0, 0)), pl.BlockSpec((taps + 1, channels), lambda i: (0, 0))),
        scratch_shapes=[pltpu.VMEM((seqs, rows // seqs + 8, channels), jnp.float32)],
        compiler_params=pltpu.CompilerParams(vmem_limit_bytes=VMEM_BYTES),
        cost_estimate=pl.CostEstimate(flops=8 * rows * channels * channels, bytes_accessed=16 * rows * channels, transcendentals=0),
        name="conv_back",
    )(*args)


def out_kernel(values_ref, w_ref, *refs):
    weight = w_ref[...].reshape(-1, w_ref.shape[-1])
    store_all(refs, jnp.dot(values_ref[...], weight, preferred_element_type=jnp.float32))


def out_parts(values, weight):
    weight, rows = weight
    tokens, inner = values.shape
    shares, _, width = weight.shape
    block = column_block(width, 512)
    shapes, specs = parts_out(tokens // PLANE, width, block)
    return pl.pallas_call(
        out_kernel,
        grid=(width // block,),
        out_shape=shapes,
        in_specs=[
            pl.BlockSpec((tokens, inner), lambda j: (0, 0), pipeline_mode=CONSTANT),
            pl.BlockSpec((shares, rows, block), lambda j: (0, 0, j)),
        ],
        out_specs=specs,
        compiler_params=pltpu.CompilerParams(vmem_limit_bytes=VMEM_BYTES),
        cost_estimate=pl.CostEstimate(
            flops=2 * tokens * inner * width, bytes_accessed=2 * (tokens * inner + inner * width + tokens * width), transcendentals=0
        ),
        name="out_parts",
    )(values, weight)


def weight_grad_kernel(rows, rights, steps, me_ref, left_ref, *refs):
    right_refs, mine_ref, theirs, left_s = refs[:rights], refs[rights], refs[rights + 1 : -1], refs[-1]
    narrow, groups, _, block = mine_ref.shape
    height = narrow * rows

    @pl.when(pl.program_id(1) == 0)
    def _():
        left_s[...] = left_ref[...].T

    def store(total, mine, other):
        for g in range(groups):
            start = (g * 2 + mine) * height
            mine_ref[:, g] = total[start : start + height].reshape(narrow, rows, block)
            start = (g * 2 + other) * height
            for k, ref in enumerate(theirs):
                ref[0, g] = total[start + k * rows : start + (k + 1) * rows]

    for k, right_ref in enumerate(right_refs):

        @pl.when(pl.program_id(1) // steps == k)
        def _(right_ref=right_ref):
            total = jnp.dot(left_s[...], right_ref[...], preferred_element_type=jnp.float32).astype(jnp.bfloat16)

            @pl.when(me_ref[0] == 0)
            def _():
                store(total, 0, 1)

            @pl.when(me_ref[0] != 0)
            def _():
                store(total, 1, 0)


def weight_grad(me, left, rights, narrow, groups, rows):
    tokens, piece = rights[0].shape
    block = column_block(piece, 768)
    steps = piece // block
    together = 2 if groups % 2 == 0 else 1
    height = together * 2 * narrow * rows
    columns = len(rights) * piece

    def right_spec(k):
        return pl.BlockSpec((tokens, block), lambda g, j, me_ref: (0, jnp.clip(j - k * steps, 0, steps - 1)))

    return pl.pallas_call(
        functools.partial(weight_grad_kernel, rows, len(rights), steps),
        grid_spec=pltpu.PrefetchScalarGridSpec(
            num_scalar_prefetch=1,
            grid=(groups // together, len(rights) * steps),
            in_specs=[pl.BlockSpec((tokens, height), lambda g, j, me_ref: (0, g))]
            + [right_spec(k) for k in range(len(rights))],
            out_specs=(pl.BlockSpec((narrow, together, rows, block), lambda g, j, me_ref: (0, g, 0, j)),)
            + (pl.BlockSpec((1, together, rows, block), lambda g, j, me_ref: (0, g, 0, j)),) * narrow,
            scratch_shapes=[pltpu.VMEM((height, tokens), jnp.bfloat16)],
        ),
        out_shape=(jax.ShapeDtypeStruct((narrow, groups, rows, columns), jnp.bfloat16),)
        + (jax.ShapeDtypeStruct((1, groups, rows, columns), jnp.bfloat16),) * narrow,
        compiler_params=pltpu.CompilerParams(vmem_limit_bytes=VMEM_BYTES),
        cost_estimate=pl.CostEstimate(
            flops=2 * tokens * left.shape[1] * columns,
            bytes_accessed=2 * (left.size + groups // together * tokens * columns + left.shape[1] * columns),
            transcendentals=0,
        ),
        name="weight_grad",
    )(me, left, *rights)


def add_pieces_kernel(mine_ref, *refs):
    for k, ref in enumerate(refs[:-1]):
        refs[-1][k] = (mine_ref[k].astype(jnp.float32) + ref[0].astype(jnp.float32)).astype(jnp.bfloat16)


def add_pieces(mine, others):
    narrow, groups, rows, columns = mine.shape
    block = column_block(columns, 2048 if groups > 1 else 512)
    place = pl.BlockSpec((narrow, 1, rows, block), lambda g, j: (0, g, 0, j))
    return pl.pallas_call(
        add_pieces_kernel,
        grid=(groups, columns // block),
        out_shape=jax.ShapeDtypeStruct(mine.shape, jnp.bfloat16),
        in_specs=[place] + [pl.BlockSpec((1, 1, rows, block), lambda g, j: (0, g, 0, j))] * narrow,
        out_specs=place,
        compiler_params=pltpu.CompilerParams(vmem_limit_bytes=VMEM_BYTES),
        cost_estimate=pl.CostEstimate(flops=mine.size, bytes_accessed=6 * mine.size, transcendentals=0),
        name="add_pieces",
    )(mine, *others)


def block_diagonal(table):
    size, channels = table.shape
    tall = jnp.concatenate([table] * (channels // size), axis=0)
    row_head = lax.broadcasted_iota(jnp.int32, tall.shape, 0) // size
    column_head = lax.broadcasted_iota(jnp.int32, tall.shape, 1) // size
    return jnp.where(row_head == column_head, tall, jnp.zeros_like(tall))


def diagonal_blocks(square, size):
    channels = square.shape[0]
    cube = square.reshape(channels // size, size, channels)
    row_head = lax.broadcasted_iota(jnp.int32, cube.shape, 0)
    column_head = lax.broadcasted_iota(jnp.int32, cube.shape, 2) // size
    return jnp.sum(jnp.where(row_head == column_head, cube, jnp.zeros_like(cube)), axis=0)


def shift_rows(values, seqs, by):
    rows, channels = values.shape
    length = rows // seqs
    cube = values.reshape(seqs, length, channels)
    if by > 0:
        cube = jnp.pad(cube, ((0, 0), (by, 0), (0, 0)))[:, :length]
    elif by < 0:
        cube = jnp.pad(cube, ((0, 0), (0, -by), (0, 0)))[:, -by:]
    return cube.reshape(rows, channels)


def make_block(rest_size, narrow_size):
    bf16, f32 = jnp.bfloat16, jnp.float32
    spread = ("rest", "narrow")

    def swap(values, mask):
        return lax.ppermute(values, "wide", [(i, i ^ mask) for i in range(PLANE)])

    def gather_parts(shard):
        half = shard.shape[0] // 2
        one, two = swap(shard, 1), swap(shard, 2)
        return [swap(one[:half], 2), swap(two[half:], 1), one, two, shard]

    def gather_rows(shard):
        return jnp.concatenate(gather_parts(shard), axis=0)

    def scatter_start(parts, *beside):
        far_low, far_high, one, two, own = parts
        half = own.shape[0] // 2
        via_one, via_two, *beside = fence(swap(far_low, 1), swap(far_high, 2), *beside)
        one = jnp.concatenate([one[:half], (one[half:].astype(f32) + via_two.astype(f32)).astype(bf16)], axis=0)
        two = jnp.concatenate([(two[:half].astype(f32) + via_one.astype(f32)).astype(bf16), two[half:]], axis=0)
        return (one, two, own, *beside)

    def scatter_sum(own, one, two):
        return own.astype(f32) + one.astype(f32) + two.astype(f32)

    def scatter_finish(one, two, own):
        return scatter_sum(own, swap(one, 1), swap(two, 2))

    def scatter_rows(parts):
        return scatter_finish(*scatter_start(parts))

    def cut_columns(blocks):
        return lax.all_to_all(blocks, "wide", 0, 0, tiled=False)

    def gather_spread(part):
        whole = lax.all_gather(part.reshape(-1, part.shape[-1]), spread, axis=0, tiled=True)
        return whole.reshape((rest_size * narrow_size,) + part.shape)

    def grad_shares(left, rights, rows, groups):
        if rest_size != 2:
            grad = matmul_tn(left, jnp.concatenate(rights, axis=1)).astype(bf16)
            cut = grad.reshape(groups, rest_size, narrow_size, rows, -1).transpose(1, 2, 0, 3, 4)
            return cut, lambda term: lax.psum_scatter(term, "rest", scatter_dimension=0, tiled=False)
        me = lax.axis_index("rest").astype(jnp.int32)[None]
        mine, *theirs = weight_grad(me, left, rights, narrow_size, groups, rows)
        others = [lax.ppermute(piece, "rest", [(0, 1), (1, 0)]) for piece in theirs]
        return mine, lambda term: add_pieces(term, others)

    def sum_rest(values):
        if rest_size != 2:
            return lax.psum_scatter(values, "rest", scatter_dimension=0, tiled=False)
        me = lax.axis_index("rest")
        theirs = lax.dynamic_index_in_dim(values, 1 - me, 0, keepdims=False)
        mine = lax.dynamic_index_in_dim(values, me, 0, keepdims=False)
        other = lax.ppermute(theirs, "rest", [(0, 1), (1, 0)])
        return (mine.astype(f32) + other.astype(f32)).astype(values.dtype)

    def sum_narrow(values):
        return lax.psum_scatter(values.reshape(-1, values.shape[-1]), "narrow", scatter_dimension=0, tiled=True)

    def columns_home(mine, rows):
        return lax.all_to_all(mine.reshape(PLANE, rows, -1), "wide", 0, 1, tiled=False)

    def sum_narrow_direct(values):
        me = lax.axis_index("narrow")
        total = lax.dynamic_index_in_dim(values, me, 0, keepdims=False).astype(f32)
        for step in range(1, narrow_size):
            part = lax.dynamic_index_in_dim(values, lax.rem(me + step, narrow_size), 0, keepdims=False)
            pairs = [(i, (i + step) % narrow_size) for i in range(narrow_size)]
            total = total + lax.ppermute(part, "narrow", pairs).astype(f32)
        return total

    def to_all(values, axes, count):
        return lax.all_to_all(jnp.broadcast_to(values[None], (count,) + values.shape), axes, 0, 0, tiled=False)

    def rows_cut(grad):
        return grad.reshape(rest_size, narrow_size, -1, grad.shape[-1])

    def fence(*values):
        return lax.optimization_barrier(values)

    def after(values, *others):
        return lax.optimization_barrier((values,) + others)[0]

    def on_device(
        tokens,
        lengths,
        cotangent,
        norm_gain1,
        gate_in,
        x_in,
        conv_kernel,
        conv_bias,
        rate_weight,
        rate_bias,
        input_weight,
        input_bias,
        decay_param,
        out_proj,
        norm_gain2,
        mlp_gate,
        mlp_up,
        mlp_down,
    ):
        row_count, width = tokens.shape
        head = rate_weight.shape[0]
        rows = gate_in.shape[0]
        taps = conv_kernel.shape[0]
        seqs = PLANE
        channels = gate_in.shape[1] // PLANE
        hidden = mlp_gate.shape[1] // PLANE
        live = (jnp.arange(row_count, dtype=jnp.int32) < lengths[0]).astype(f32)[:, None]

        def by_plane(*weights):
            cut = [w.reshape(rows, PLANE, -1).swapaxes(0, 1) for w in weights]
            return jnp.concatenate(cut, axis=2)

        table = jnp.concatenate(
            [
                conv_kernel,
                conv_bias[None],
                rate_weight,
                rate_bias[None],
                input_weight,
                input_bias[None],
                decay_param[None],
            ],
            axis=0,
        )
        cuts = [taps, 1, head, 1, head, 1, 1]
        places = [sum(cuts[:i]) for i in range(len(cuts) + 1)]
        columns = 2 * channels
        shares = rest_size * narrow_size
        part_rec = cut_columns(by_plane(gate_in, x_in)).reshape(PLANE, rows, columns)
        w_rec = gather_spread(part_rec)
        tokens_all = gather_rows(after(tokens, part_rec))
        table = jnp.pad(table, ((0, -places[-1] % LANES), (0, 0))).T
        table = to_all(after(table, part_rec), spread, shares)
        gains = to_all(after(jnp.stack([norm_gain1, norm_gain2]), table), ("wide",) + spread, PLANE * shares)
        cut_mlp = by_plane(mlp_gate, mlp_up)
        w_rec, tokens_all, table, gains, cut_mlp = fence(w_rec, tokens_all, table, gains, cut_mlp)

        out_and_down = lax.all_gather(
            after(jnp.concatenate([out_proj, mlp_down], axis=0), w_rec), spread, axis=0, tiled=True
        ).reshape(rest_size * narrow_size, -1, width)
        low_res = (cotangent.astype(f32) * live).astype(bf16)
        low_res_parts = gather_parts(after(low_res, w_rec))
        low_res_all = jnp.concatenate(low_res_parts, axis=0)
        gains = gains.swapaxes(0, 1).reshape(2, width).astype(f32)
        gain_one, gain_two = gains[0:1], gains[1:2]
        table = table.reshape(channels, -1).T
        w_flat = w_rec.swapaxes(0, 1).reshape(width, columns)
        tokens_f = tokens_all.astype(f32)
        inverse_all = rms_inverse(tokens_f)
        normed1 = (tokens_f * inverse_all * gain_one).astype(bf16)
        gate_pre = matmul_low(normed1, w_flat[:, :channels])
        branch_pre = matmul_low(normed1, w_flat[:, channels:])
        kernel, shift, rate_table, b_rate, input_table, b_input, decay = (
            table[places[i] : places[i + 1]] for i in range(len(cuts))
        )
        kernel_f, shift_f, b_rate, b_input, decay_f = (v.astype(f32) for v in (kernel, shift, b_rate, b_input, decay))
        w_rate = block_diagonal(rate_table)
        w_input = block_diagonal(input_table)
        soft = softplus_minus(decay_f)
        soft_rows = jnp.broadcast_to(soft, (8, soft.shape[1]))
        part_mlp = cut_columns(after(cut_mlp, *low_res_parts))

        conv = shift_f
        for tap in range(taps):
            conv = conv + kernel_f[tap] * shift_rows(branch_pre, seqs, taps - 1 - tap)
        conv = conv.astype(bf16)
        rate_pre = matmul_low(conv, w_rate) + b_rate
        input_pre = matmul_low(conv, w_input) + b_input
        states, mixed = lru_forward(seqs, conv, rate_pre, input_pre, gate_pre, soft_rows)
        mixed, part_mlp, out_and_down = fence(mixed, part_mlp, out_and_down)
        out_rows = out_proj.shape[0]
        if out_rows % 16 == 0:
            w_out = (out_and_down, out_rows)
        else:
            w_out = (out_and_down[:, :out_rows].reshape(1, -1, width), shares * out_rows)
        w_down = out_and_down[:, out_rows:].reshape(-1, width)

        w_mlp = gather_spread(part_mlp)
        merged = tokens.astype(f32) + scatter_rows(out_parts(mixed, w_out))
        inverse2 = rms_inverse(merged)
        normed2 = (merged * inverse2 * gain_two).astype(bf16)
        *normed2_parts, w_mlp = fence(*gather_parts(normed2), w_mlp)

        product, d_gate_two, d_up_two, normed2_all = mlp_both(normed2_parts, low_res_all, w_mlp, w_down)
        mine, finish = grad_shares(product, (low_res_all,), mlp_down.shape[0], 1)
        mine, late_gate_two = fence(mine, d_gate_two)
        parts2 = back_parts((late_gate_two, d_up_two), w_mlp)
        down_out = sum_narrow(finish(mine))
        one, two, own = scatter_start(parts2)
        mine, finish = grad_shares(normed2_all, (late_gate_two,), rows, PLANE)
        grad_mgate = finish(mine)
        d_normed2 = scatter_finish(one, two, own)
        d_normed2, grad_mgate, down_out, late_up_two, late_product = fence(
            d_normed2, grad_mgate, down_out, d_up_two, product
        )

        mgate_sum = sum_narrow(grad_mgate)
        grad_gain2 = jnp.sum(d_normed2 * merged * inverse2, axis=0)
        d_merged = low_res.astype(f32) + rms_back(merged, inverse2, gain_two, d_normed2)
        low_merged_parts = gather_parts(d_merged.astype(bf16))
        mine, finish = grad_shares(normed2_all, (late_up_two,), rows, PLANE)
        grad_mup = finish(mine)
        parts_result = out_parts(late_product, (w_down[None], w_down.shape[0]))
        *low_merged_parts, parts_result, mgate_sum, grad_mup = fence(*low_merged_parts, parts_result, mgate_sum, grad_mup)
        d_mixed, low_merged_all = mixed_grad(low_merged_parts, w_out)
        mup_sum = sum_narrow(grad_mup)
        sums_result = scatter_start(parts_result)
        d_mixed, *sums_result = fence(d_mixed, *sums_result)
        d_conv_lru, d_rate, d_input, d_gate, sums = lru_backward(
            seqs, conv, rate_pre, input_pre, gate_pre, soft_rows, states, d_mixed
        )
        mgate_out = columns_home(mgate_sum, rows)
        sums = sums.reshape(3, 8, -1).sum(axis=1)
        grad_decay = sums[2] * (-1.0 / (1.0 + jnp.exp(decay_f[0])))
        low_branch, conv_sums = conv_back(seqs, d_conv_lru, d_rate, d_input, w_rate, w_input, branch_pre, kernel_f)
        one, two, own = sums_result
        result_one, result_two = swap(one, 1), swap(two, 2)

        low_branch, mgate_out, result_one, result_two = fence(low_branch, mgate_out, result_one, result_two)
        result = merged + scatter_sum(own, result_one, result_two)
        *parts1, grad_gain1 = back_parts((d_gate, low_branch), w_rec, (tokens_all, inverse_all))
        *parts1, late_gate = fence(*parts1, d_gate)
        mine, finish = grad_shares(normed1, (late_gate, low_branch), rows, PLANE)
        grad_rec = finish(mine)
        rec_sum = sum_narrow(grad_rec)
        one, two, own = scatter_start(parts1)
        mup_out = columns_home(mup_sum, rows)
        one, two, late_mixed, late_rate, late_input, mup_out = fence(one, two, mixed, d_rate, d_input, mup_out)
        d_normed1 = scatter_finish(one, two, own)
        grad_out = matmul_tn(late_mixed, low_merged_all).astype(bf16)
        gain_grads = jnp.stack([grad_gain1[0], grad_gain2]).reshape(2, -1, rows).swapaxes(0, 1)
        grad_rate_weight = diagonal_blocks(matmul_tn(conv, late_rate), head)
        grad_input_weight = diagonal_blocks(matmul_tn(conv, late_input), head)
        table_grad = jnp.concatenate(
            [
                conv_sums,
                grad_rate_weight,
                sums[0:1],
                grad_input_weight,
                sums[1:2],
                grad_decay[None],
            ],
            axis=0,
        )
        table_grad = jnp.pad(table_grad, ((0, -places[-1] % LANES), (0, 0))).T.astype(bf16)
        last = sum_rest(rows_cut(jnp.concatenate([grad_out, table_grad], axis=1)))
        rec_sum, d_normed1, last, gain_grads = fence(rec_sum, d_normed1, last, gain_grads)
        last = sum_narrow(last).astype(f32)
        out_out, table_out = last[:, :width], last[:, width:].T

        rec_out = columns_home(rec_sum, rows)
        gain_out = lax.all_to_all(gain_grads, ("wide",) + spread, 0, 0, tiled=False).sum(axis=0)
        block_out = (result * live).astype(bf16)
        own = tokens.astype(f32)
        input_grad = d_merged + rms_back(own, rms_inverse(own), gain_one, d_normed1)

        kernel_out, shift_out, rate_out, rate_bias_out, input_out, input_bias_out, decay_out = (
            table_out[places[i] : places[i + 1]] for i in range(len(cuts))
        )
        def whole_rows(cut):
            return cut.reshape(rows, -1).astype(f32)

        return (
            block_out,
            input_grad,
            gain_out[0],
            whole_rows(rec_out[:, :, :channels]),
            whole_rows(rec_out[:, :, channels:]),
            kernel_out,
            shift_out[0],
            rate_out,
            rate_bias_out[0],
            input_out,
            input_bias_out[0],
            decay_out[0],
            out_out,
            gain_out[1],
            whole_rows(mgate_out),
            whole_rows(mup_out),
            down_out.astype(f32),
        )

    return on_device


def solution(mesh):
    wide, narrow = mesh.shape["wide"], mesh.shape["narrow"]
    mesh = Mesh(mesh.devices.reshape(PLANE, wide // PLANE, narrow), ("wide", "rest", "narrow"))
    every = mesh.axis_names
    rows, columns, vector = P(every, None), P(None, every), P(every)
    return jax.shard_map(
        make_block(wide // PLANE, narrow),
        mesh=mesh,
        in_specs=(
            rows,
            vector,
            rows,
            vector,
            rows,
            rows,
            columns,
            vector,
            columns,
            vector,
            columns,
            vector,
            vector,
            rows,
            vector,
            rows,
            rows,
            rows,
        ),
        out_specs=(
            rows,
            rows,
            vector,
            rows,
            rows,
            columns,
            vector,
            columns,
            vector,
            columns,
            vector,
            vector,
            rows,
            vector,
            rows,
            rows,
            rows,
        ),
        check_vma=False,
    )
```
